32 devices in a mesh: dp: 8 (over z, y), seq: 4 (over x, core).
Axes of the slice: x: 2, y: 2, z: 4, core: 2. Of those that a mesh axis runs over, the one named last changes fastest.
Arguments:
- hidden_states: bfloat16 [64, 512, 768], P('dp', 'seq'), may hold values from -6 to 6
- prev_logits: bfloat16 [64, 12, 512, 512], P('dp', None, 'seq'), may hold values from -6 to 6
- lengths: int32 [64], P('dp'), may hold values from 128 to 512, as said below
- w_qkv: bfloat16 [768, 2304], P('dp', 'seq'), may hold values from -0.21875 to 0.21875
- w_out: bfloat16 [768, 768], P('dp', 'seq'), may hold values from -0.875 to 0.875
- w_in: bfloat16 [768, 3072], P('dp', 'seq'), may hold values from -0.21875 to 0.21875
- w_down: bfloat16 [3072, 768], P('dp', 'seq'), may hold values from -0.109375 to 0.109375
- b_in: bfloat16 [3072], P(('dp', 'seq')), may hold values from -3 to 3
- vectors: bfloat16 [8, 768], P('seq', 'dp')
- cotangent: bfloat16 [64, 512, 768], P('dp', 'seq'), may hold values from -6 to 6
Outputs:
- hidden_out: bfloat16 [64, 512, 768], P('dp', 'seq')
- grad_hidden: bfloat16 [64, 512, 768], P('dp', 'seq')
- grad_logits: bfloat16 [64, 12, 512, 512], P('dp', None, 'seq')
- grad_w_qkv: float32 [768, 2304], P('dp', 'seq')
- grad_w_out: float32 [768, 768], P('dp', 'seq')
- grad_w_in: float32 [768, 3072], P('dp', 'seq')
- grad_w_down: float32 [3072, 768], P('dp', 'seq')
- grad_b_in: float32 [3072], P(('dp', 'seq'))
- grad_vectors: float32 [8, 768], P('seq', 'dp')
The draws below stay inside these ranges and needn't reach their ends.
Inputs may be any that keep to these rules, and one draw needn't show every extreme that they name: `lengths`: keys at positions from a sequence's length on are padding. Among the 8 sequences of each index of dp, at least one is full.
All inputs are finite; a program needn't handle non-finite values.
Results may differ from the reference program's by a relative error of at most 0.017.
Values may be sent and summed in bfloat16 or wider, within the bound.
No kernel may reach another device: no remote copies, remote signals or barrier semaphores. Data moves between devices by JAX's collectives and lax.ppermute only.
A program may use at most 256 MiB of HBM per device.

```python
import math
import jax
import jax.numpy as jnp
from jax import lax

D = 768
HEADS = 12
HEAD_DIM = 64
FF = 3072
LENGTH = 512
NVEC = 8
SEQ_DEV = 8
SEQS = 64


def draw_lengths(key, part):
    key = jax.random.fold_in(key, 11)
    first, second, third = jax.random.split(key, 3)
    kinds = jax.random.randint(first, (SEQS,), 0, 8)
    padding = jax.random.randint(second, (SEQS,), 0, LENGTH * 3 // 4 + 1)
    valid_len = LENGTH - jnp.where(kinds < 5, 0, padding)
    chosen = jax.random.randint(third, (SEQS // SEQ_DEV,), 0, SEQ_DEV)
    places = jnp.arange(SEQS, dtype=jnp.int32)
    forced = places % SEQ_DEV == jnp.repeat(chosen, SEQ_DEV)
    return jnp.where(forced, LENGTH, valid_len).astype(jnp.int32)


def draw_vectors(key, part):
    key = jax.random.fold_in(key, 7)
    first, second = jax.random.split(key)
    shifts = 0.3 * jax.random.normal(first, (NVEC, D), jnp.float32)
    gains = jax.random.uniform(second, (NVEC, D), jnp.float32, 0.6, 1.4)
    row_ids = jnp.arange(NVEC)[:, None]
    gain_rows = (row_ids == 3) | (row_ids == 6)
    return jnp.where(gain_rows, gains, shifts).astype(jnp.bfloat16)


def strengthened(values, own_key, source, target, blocks, factor):
    owner, partner = [(jnp.arange(values.shape[dim]) // (values.shape[dim] // blocks)).reshape([-1 if axis == dim else 1 for axis in range(values.ndim)]) for dim in (source, target)]
    chosen = jax.random.permutation(own_key, blocks)[partner]
    strong = (owner == chosen) | (owner == (partner + blocks // 2) % blocks)
    return jnp.where(strong, factor * values, values)


def steps_of(key, extent, cuts, smallest, top_value):
    factor_of, own = 1.0, jax.random.fold_in(key, 6)
    for position, parts in cuts:
        draws = jnp.exp(jax.random.uniform(jax.random.fold_in(own, position), (parts,), jnp.float32, smallest / len(cuts), top_value / len(cuts)))
        factor_of = factor_of * jnp.repeat(draws, extent[position] // parts).reshape([-1 if axis == position else 1 for axis in range(len(extent))])
    return factor_of


def noise(rng, extent, width, limit, cuts=(), held_as=jnp.bfloat16):
    values = jax.random.normal(rng, extent, jnp.float32) * width
    if len(cuts) > 0:
        values = steps_of(rng, extent, cuts, -0.22, 0.18) * values
    return jnp.clip(values, min=-limit, max=limit).astype(held_as)


def bell_draw_with(rng, dims, width, bound, cuts, heavy, kind=jnp.bfloat16):
    drawn = width * jax.random.normal(rng, dims, jnp.float32)
    if cuts:
        drawn = drawn * steps_of(rng, dims, cuts, -0.22, 0.18)
    return jnp.clip(strengthened(drawn, jax.random.fold_in(rng, 3), *heavy), -bound, bound).astype(kind)


def setup_inputs(seed: int = 0) -> dict:
    key_of = jax.random.split(jax.random.key(seed), 11)
    hidden_states = bell_draw_with(key_of[0], (SEQS, LENGTH, D), 1.0, 6.0, ((0, 8), (1, 4)), (0, 2, 8, 2.0))
    prev_logits = noise(key_of[1], (SEQS, HEADS, LENGTH, LENGTH), 1.0, 6.0, ((0, 8), (2, 4)))
    lengths = draw_lengths(jax.random.fold_in(key_of[10], 71), 0)
    w_qkv = noise(key_of[3], (D, 3 * D), D ** -0.5, 0.21875, ((0, 8), (1, 4)))
    w_out = noise(key_of[4], (D, D), (D // 16) ** -0.5, 0.875, ((0, 8), (1, 4)))
    w_in = noise(key_of[5], (D, FF), D ** -0.5, 0.21875, ((0, 8), (1, 4)))
    w_down = noise(key_of[6], (FF, D), FF ** -0.5, 0.109375, ((0, 8), (1, 4)))
    b_in = noise(key_of[7], (FF,), 0.5, 3.0, ((0, 32),))
    vectors = draw_vectors(jax.random.fold_in(key_of[10], 71), 0)
    cotangent = noise(key_of[9], (SEQS, LENGTH, D), 1.0, 6.0, ((0, 8), (1, 4)))
    return dict(hidden_states=hidden_states, prev_logits=prev_logits, lengths=lengths, w_qkv=w_qkv, w_out=w_out, w_in=w_in, w_down=w_down, b_in=b_in, vectors=vectors, cotangent=cotangent)


@jax.custom_vjp
def low(v):
    return lax.optimization_barrier(v.astype(jnp.bfloat16)).astype(jnp.float32)

@jax.custom_vjp
def low_back(v):
    return v

def low_keep(v):
    return (low(v), None)

def low_pass(kept, grad):
    return (grad,)

def back_keep(v):
    return (v, None)

def back_low(kept, grad):
    return (low(grad),)
low.defvjp(low_keep, low_pass)
low_back.defvjp(back_keep, back_low)

def layer_norm(values, gain, shift):
    average = lax.optimization_barrier(jnp.mean(values, -1, keepdims=True))
    centred = values - average
    spread = lax.optimization_barrier(jnp.mean(centred * centred, -1, keepdims=True))
    return centred * lax.rsqrt(spread + 1e-06) * gain + shift

def block_forward(states, logits, valid_len, w_qkv, w_out, w_in, w_down, b_in, vectors):
    highest = lax.Precision.HIGHEST
    count = states.shape[0]
    rows = states.reshape(-1, D)
    qkv = jnp.dot(rows, w_qkv, precision=highest)
    queries = low_back(low(qkv[:, :D] + vectors[0]))
    key_rows = low_back(low(qkv[:, D:2 * D]))
    value_rows = low_back(low(qkv[:, 2 * D:] + vectors[1]))
    query_heads = queries.reshape(count, LENGTH, HEADS, HEAD_DIM)
    key_heads = key_rows.reshape(count, LENGTH, HEADS, HEAD_DIM)
    value_heads = value_rows.reshape(count, LENGTH, HEADS, HEAD_DIM)
    scores = jnp.einsum('bqhd,bkhd->bhqk', query_heads, key_heads, precision=highest) * HEAD_DIM ** (-0.5) + logits
    valid = jnp.arange(LENGTH, dtype=jnp.int32)[None, :] < valid_len[:, None]
    scores = jnp.where(valid[:, None, None, :], scores, -1000000000.0)
    scores = low_back(scores)
    probs = jax.nn.softmax(scores, axis=-1)
    mixed = jnp.einsum('bhqk,bkhd->bqhd', low(probs), value_heads, precision=highest).reshape(-1, D)
    context = low_back(low(mixed))
    attn_out = low_back(jnp.dot(context, w_out, precision=highest) + vectors[2])
    first = layer_norm(rows + attn_out, vectors[3], vectors[4])
    inner = low_back(jnp.dot(low(first), w_in, precision=highest) + b_in)
    gelu_out = low(jax.nn.gelu(inner, approximate=False))
    branch = low_back(jnp.dot(gelu_out, w_down, precision=highest) + vectors[5])
    second = layer_norm(first + branch, vectors[6], vectors[7])
    return second.reshape(count, LENGTH, D)

def reference(hidden_states, prev_logits, lengths, w_qkv, w_out, w_in, w_down, b_in, vectors, cotangent):
    group_size = math.gcd(SEQS, max(1, 4096 // LENGTH))
    groups = SEQS // group_size
    params = tuple((item.astype(jnp.float32) for item in (w_qkv, w_out, w_in, w_down, b_in, vectors)))

    def group_step(totals, block_item):
        states, logits, valid_len, cot_rows = block_item

        def local_layer(state_in, logit_in, *weights):
            return block_forward(state_in, logit_in, valid_len, *weights)
        result, pull = jax.vjp(local_layer, states.astype(jnp.float32), logits.astype(jnp.float32), *params)
        grads = pull(cot_rows.astype(jnp.float32))
        new_totals = tuple((total + grad for total, grad in zip(totals, grads[2:])))
        return (new_totals, (result.astype(jnp.bfloat16), grads[0].astype(jnp.bfloat16), grads[1].astype(jnp.bfloat16)))
    zeros = tuple((jnp.zeros(item.shape, jnp.float32) for item in params))
    items = (hidden_states.reshape(groups, group_size, LENGTH, D), prev_logits.reshape(groups, group_size, HEADS, LENGTH, LENGTH), lengths.reshape(groups, group_size), cotangent.reshape(groups, group_size, LENGTH, D))
    totals, stacked = lax.scan(group_step, zeros, items)
    hidden_out = stacked[0].reshape(SEQS, LENGTH, D)
    grad_hidden = stacked[1].reshape(SEQS, LENGTH, D)
    grad_logits = stacked[2].reshape(SEQS, HEADS, LENGTH, LENGTH)
    return (hidden_out, grad_hidden, grad_logits, totals[0], totals[1], totals[2], totals[3], totals[4], totals[5])
```

```python
import functools

import jax
import jax.numpy as jnp
from jax import lax
from jax.experimental import pallas as pl
from jax.experimental.pallas import tpu as pltpu
from jax.sharding import PartitionSpec as P

D = 768
HEADS = 12
HEAD_DIM = 64
PAIRS = HEADS // 2
PAIR = 2 * HEAD_DIM
SCALE = HEAD_DIM ** (-0.5)
BF = jnp.bfloat16
F32 = jnp.float32
BOTH = ("dp", "seq")
MIB = 1 << 20


def mm(a, b):
    return lax.dot_general(a, b, (((1,), (0,)), ((), ())), preferred_element_type=F32)


def mm_nt(a, b):
    return lax.dot_general(a, b, (((1,), (1,)), ((), ())), preferred_element_type=F32)


def mm_tn(a, b):
    return lax.dot_general(a, b, (((0,), (0,)), ((), ())), preferred_element_type=F32)


def stack_heads(pair):
    lane = lax.broadcasted_iota(jnp.int32, pair.shape, 1)
    zero = jnp.zeros_like(pair)
    return jnp.concatenate(
        [jnp.where(lane < HEAD_DIM, pair, zero), jnp.where(lane < HEAD_DIM, zero, pair)], 0
    )


def pick_heads(stacked):
    rows = stacked.shape[0] // 2
    lane = lax.broadcasted_iota(jnp.int32, (rows, PAIR), 1)
    return jnp.where(lane < HEAD_DIM, stacked[:rows], stacked[rows:])


def attend_kernel(blocks, order_ref, len_ref, q_ref, *refs):
    kv_refs = refs[:blocks]
    prev_ref, ctx_ref, probs_ref, kv_all = refs[blocks:]
    rows = q_ref.shape[1]
    total = kv_all.shape[0]
    for j in range(blocks):
        start = pl.multiple_of(order_ref[j] * rows, rows)
        kv_all[pl.ds(start, rows), :] = kv_refs[j][0]
    valid = len_ref[pl.program_id(0)]
    key_pos = lax.broadcasted_iota(jnp.int32, (1, total), 1)
    padding = jnp.where(key_pos < valid, 0.0, -1e9)
    for i in range(PAIRS):
        cols = slice(i * PAIR, (i + 1) * PAIR)
        vcols = slice(D + i * PAIR, D + (i + 1) * PAIR)
        query = stack_heads(q_ref[0, :, cols])
        raw = mm_nt(query, kv_all[:, cols])
        prev = prev_ref[0, 2 * i : 2 * i + 2].reshape(2 * rows, total).astype(F32)
        raw = raw + prev + padding
        largest = jnp.max(raw, -1, keepdims=True)
        expo = jnp.exp(raw - largest)
        summed = jnp.sum(expo, -1, keepdims=True)
        probs = (expo * (1.0 / summed)).astype(BF)
        probs_ref[0, 2 * i : 2 * i + 2] = probs.reshape(2, rows, total)
        ctx_ref[0, :, cols] = pick_heads(mm(probs, kv_all[:, vcols])).astype(BF)


def attend(order, lengths, queries, kv_blocks, prev_logits):
    seqs, rows, _ = queries.shape
    blocks = len(kv_blocks)
    total = prev_logits.shape[-1]
    row_spec = lambda width: pl.BlockSpec((1, rows, width), lambda b, *_: (b, 0, 0))
    head_spec = pl.BlockSpec((1, HEADS, rows, total), lambda b, *_: (b, 0, 0, 0))
    return pl.pallas_call(
        functools.partial(attend_kernel, blocks),
        grid_spec=pltpu.PrefetchScalarGridSpec(
            num_scalar_prefetch=2,
            grid=(seqs,),
            in_specs=[row_spec(D)] + [row_spec(2 * D)] * blocks + [head_spec],
            out_specs=[row_spec(D), head_spec],
            scratch_shapes=[pltpu.VMEM((total, 2 * D), BF)],
        ),
        out_shape=[
            jax.ShapeDtypeStruct(queries.shape, BF),
            jax.ShapeDtypeStruct(prev_logits.shape, BF),
        ],
        compiler_params=pltpu.CompilerParams(vmem_limit_bytes=48 * MIB),
        cost_estimate=pl.CostEstimate(
            flops=4 * seqs * HEADS * rows * total * PAIR,
            bytes_accessed=4 * seqs * HEADS * rows * total,
            transcendentals=seqs * HEADS * rows * total,
        ),
    )(order, lengths, queries, *kv_blocks, prev_logits)


def attend_back_kernel(blocks, order_ref, q_ref, *refs):
    kv_refs = refs[:blocks]
    probs_ref, dctx_ref, dlogits_ref, dq_ref = refs[blocks : blocks + 4]
    dkv_refs = refs[blocks + 4 : 2 * blocks + 4]
    kv_all, dkv_all = refs[2 * blocks + 4 :]
    rows = q_ref.shape[1]
    total = kv_all.shape[0]
    starts = [pl.multiple_of(order_ref[j] * rows, rows) for j in range(blocks)]
    for j in range(blocks):
        kv_all[pl.ds(starts[j], rows), :] = kv_refs[j][0]
    for i in range(PAIRS):
        cols = slice(i * PAIR, (i + 1) * PAIR)
        vcols = slice(D + i * PAIR, D + (i + 1) * PAIR)
        query = stack_heads(q_ref[0, :, cols])
        dctx = stack_heads(dctx_ref[0, :, cols])
        probs = probs_ref[0, 2 * i : 2 * i + 2].reshape(2 * rows, total)
        dprobs = mm_nt(dctx, kv_all[:, vcols])
        wide = probs.astype(F32)
        prod = wide * dprobs
        weighted = jnp.sum(prod, -1, keepdims=True)
        dlogits = (prod - wide * weighted).astype(BF)
        dlogits_ref[0, 2 * i : 2 * i + 2] = dlogits.reshape(2, rows, total)
        dq_ref[0, :, cols] = (pick_heads(mm(dlogits, kv_all[:, cols])) * SCALE).astype(BF)
        dkv_all[:, cols] = mm_tn(dlogits, query).astype(BF)
        dkv_all[:, vcols] = mm_tn(probs, dctx).astype(BF)
    for j in range(blocks):
        dkv_refs[j][0] = dkv_all[pl.ds(starts[j], rows), :]


def attend_back(order, queries, kv_blocks, probs, dctx):
    seqs, rows, _ = queries.shape
    blocks = len(kv_blocks)
    total = probs.shape[-1]
    row_spec = lambda width: pl.BlockSpec((1, rows, width), lambda b, *_: (b, 0, 0))
    head_spec = pl.BlockSpec((1, HEADS, rows, total), lambda b, *_: (b, 0, 0, 0))
    outs = pl.pallas_call(
        functools.partial(attend_back_kernel, blocks),
        grid_spec=pltpu.PrefetchScalarGridSpec(
            num_scalar_prefetch=1,
            grid=(seqs,),
            in_specs=[row_spec(D)] + [row_spec(2 * D)] * blocks + [head_spec, row_spec(D)],
            out_specs=[head_spec, row_spec(D)] + [row_spec(2 * D)] * blocks,
            scratch_shapes=[pltpu.VMEM((total, 2 * D), BF), pltpu.VMEM((total, 2 * D), BF)],
        ),
        out_shape=[
            jax.ShapeDtypeStruct(probs.shape, BF),
            jax.ShapeDtypeStruct(queries.shape, BF),
        ]
        + [jax.ShapeDtypeStruct((seqs, rows, 2 * D), BF)] * blocks,
        compiler_params=pltpu.CompilerParams(vmem_limit_bytes=48 * MIB),
        cost_estimate=pl.CostEstimate(
            flops=8 * seqs * HEADS * rows * total * PAIR,
            bytes_accessed=4 * seqs * HEADS * rows * total,
            transcendentals=0,
        ),
    )(order, queries, *kv_blocks, probs, dctx)
    return outs[0], outs[1], outs[2:]


def gelu_and_slope(values):
    size = jnp.abs(values)
    bell = jnp.exp(values * values * -0.5)
    t = 1.0 / (1.0 + (0.3275911 * 0.7071067811865476) * size)
    tail = (0.5 * 1.061405429) * t + (0.5 * -1.453152027)
    tail = tail * t + (0.5 * 1.421413741)
    tail = tail * t + (0.5 * -0.284496736)
    tail = tail * t + (0.5 * 0.254829592)
    tail = tail * t * bell
    cdf = jnp.where(values >= 0.0, 1.0 - tail, tail)
    return values * cdf, cdf + values * bell * 0.3989422804014327


def norm(values):
    average = jnp.mean(values, -1, keepdims=True)
    centred = values - average
    inverse = lax.rsqrt(jnp.mean(centred * centred, -1, keepdims=True) + 1e-06)
    return centred * inverse, inverse


def norm_back(grad, normed, inverse):
    first = jnp.mean(grad, -1, keepdims=True)
    second = jnp.mean(grad * normed, -1, keepdims=True)
    return inverse * (grad - first - normed * second)


def middle_kernel(
    x_ref, ctx_ref, cot_ref, w_out_ref, w_in_ref, w_down_ref, vec_ref, b_in_ref,
    out_ref, dh1_ref, dctx_ref, act_ref, dinner_ref, dbranch_ref, y1_ref, dattn_ref,
    dvec_ref, db_in_ref,
):
    @pl.when(pl.program_id(0) == 0)
    def _():
        dvec_ref[...] = jnp.zeros_like(dvec_ref)
        db_in_ref[...] = jnp.zeros_like(db_in_ref)

    vec = lambda i: vec_ref[i : i + 1, :].astype(F32)
    total = lambda v: jnp.sum(v, 0, keepdims=True)
    h1 = x_ref[...].astype(F32) + (mm(ctx_ref[...], w_out_ref[...]) + vec(2))
    normed1, inverse1 = norm(h1)
    y1 = normed1 * vec(3) + vec(4)
    y1_low = y1.astype(BF)
    y1_ref[...] = y1_low
    inner = mm(y1_low, w_in_ref[...]) + b_in_ref[...].astype(F32)
    act, slope = gelu_and_slope(inner)
    act = act.astype(BF)
    act_ref[...] = act
    h2 = y1 + (mm_nt(act, w_down_ref[...]) + vec(5))
    normed2, inverse2 = norm(h2)
    out_ref[...] = (normed2 * vec(6) + vec(7)).astype(BF)
    cot = cot_ref[...].astype(F32)
    dh2 = norm_back(cot * vec(6), normed2, inverse2)
    dbranch = dh2.astype(BF)
    dbranch_ref[...] = dbranch
    dinner = (mm(dbranch, w_down_ref[...]) * slope).astype(BF)
    dinner_ref[...] = dinner
    dy1 = dh2 + mm_nt(dinner, w_in_ref[...])
    dh1 = norm_back(dy1 * vec(3), normed1, inverse1)
    dh1_ref[...] = dh1
    dattn = dh1.astype(BF)
    dattn_ref[...] = dattn
    dctx_ref[...] = mm_nt(dattn, w_out_ref[...]).astype(BF)
    db_in_ref[...] += total(dinner.astype(F32))
    dvec_ref[2:3, :] += total(dattn.astype(F32))
    dvec_ref[3:4, :] += total(dy1 * normed1)
    dvec_ref[4:5, :] += total(dy1)
    dvec_ref[5:6, :] += total(dbranch.astype(F32))
    dvec_ref[6:7, :] += total(cot * normed2)
    dvec_ref[7:8, :] += total(cot)


def middle(x, ctx, cot, w_out, w_in, w_down_t, vectors, b_in):
    tokens = x.shape[0]
    ff = w_in.shape[1]
    step = 256
    rows = lambda width: pl.BlockSpec((step, width), lambda i: (i, 0))
    whole = lambda a: pl.BlockSpec(a.shape, lambda i: (0, 0), pipeline_mode=pl.Buffered(1))
    sds = jax.ShapeDtypeStruct
    return pl.pallas_call(
        middle_kernel,
        grid=(tokens // step,),
        in_specs=[rows(D)] * 3 + [whole(a) for a in (w_out, w_in, w_down_t, vectors, b_in)],
        out_specs=[rows(D)] * 3
        + [rows(ff)] * 2
        + [rows(D)] * 3
        + [pl.BlockSpec((8, D), lambda i: (0, 0)), pl.BlockSpec((1, ff), lambda i: (0, 0))],
        out_shape=[
            sds((tokens, D), BF),
            sds((tokens, D), F32),
            sds((tokens, D), BF),
            sds((tokens, ff), BF),
            sds((tokens, ff), BF),
            sds((tokens, D), BF),
            sds((tokens, D), BF),
            sds((tokens, D), BF),
            sds((8, D), F32),
            sds((1, ff), F32),
        ],
        compiler_params=pltpu.CompilerParams(vmem_limit_bytes=56 * MIB),
        cost_estimate=pl.CostEstimate(
            flops=tokens * (8 * D * ff + 4 * D * D),
            bytes_accessed=40 * MIB,
            transcendentals=2 * tokens * ff,
        ),
    )(x, ctx, cot, w_out, w_in, w_down_t, vectors, b_in)


def gather_weights(w_qkv, w_out, w_in, w_down, b_in, vectors):
    rows = w_qkv.shape[0]
    small = jnp.concatenate([vectors.reshape(-1), b_in])
    small = jnp.pad(small, (0, D - small.shape[0])).reshape(1, D)
    packed = jnp.concatenate(
        [
            jnp.concatenate([w_qkv, w_out], 1),
            w_in,
            w_down.T.reshape(rows, D),
            small,
        ],
        0,
    )
    dp, seq = lax.axis_size("dp"), lax.axis_size("seq")
    whole = lax.all_gather(packed, BOTH, axis=0, tiled=False).reshape(dp, seq, -1, D)
    both = whole[:, :, :rows]
    wide = w_qkv.shape[1]
    full = lambda a: a.transpose(0, 2, 1, 3).reshape(dp * rows, -1)
    f_qkv = full(both[..., :wide])
    f_out = full(both[..., wide:])
    f_in = full(whole[:, :, rows : 2 * rows])
    down = whole[:, :, 2 * rows : 3 * rows].reshape(dp, seq, w_down.shape[1], w_down.shape[0])
    f_down_t = down.transpose(1, 2, 0, 3).reshape(seq * w_down.shape[1], dp * w_down.shape[0])
    last = whole[:, :, 3 * rows]
    nv = vectors.size
    f_vec = last[..., :nv].reshape((dp, seq) + vectors.shape)
    f_vec = f_vec.transpose(1, 2, 0, 3).reshape(seq * vectors.shape[0], dp * vectors.shape[1])
    f_b = last[..., nv : nv + b_in.shape[0]].reshape(1, -1)
    return f_qkv, f_out, f_in, f_down_t, f_b, f_vec


def reduce_grads(g_qkv, g_out, g_in, g_down_t, g_b, g_vec):
    dp, seq = lax.axis_size("dp"), lax.axis_size("seq")
    rows = D // dp
    split = lambda a: a.reshape(dp, a.shape[0] // dp, seq, -1).transpose(0, 2, 1, 3)
    both = jnp.concatenate([split(g_qkv), split(g_out)], 3)
    ff = g_in.shape[1]
    down = g_down_t.reshape(seq, D // seq, dp, ff // dp).transpose(2, 0, 1, 3)
    vec = g_vec.reshape(seq, 8 // seq, dp, rows).transpose(2, 0, 1, 3).reshape(dp, seq, -1)
    small = jnp.concatenate([vec, g_b.reshape(dp, seq, -1)], 2)
    width = small.shape[2]
    small = jnp.pad(small, ((0, 0), (0, 0), (0, D - width))).reshape(dp, seq, 1, D)
    packed = jnp.concatenate(
        [both, split(g_in), down.reshape(dp, seq, rows, D), small.astype(BF)], 2
    )
    mine = lax.psum_scatter(
        packed.reshape(dp * seq, -1, D), BOTH, scatter_dimension=0, tiled=True
    )[0].astype(F32)
    wide = 3 * D // seq
    o_down = mine[2 * rows : 3 * rows].reshape(D // seq, ff // dp).T
    last = mine[3 * rows]
    nv = 8 * D // (dp * seq)
    return (
        mine[:rows, :wide],
        mine[:rows, wide:],
        mine[rows : 2 * rows],
        o_down,
        last[nv : nv + ff // (dp * seq)],
        last[:nv].reshape(8 // seq, rows),
    )


def shards(
    hidden_states, prev_logits, lengths, w_qkv, w_out, w_in, w_down, b_in, vectors, cotangent
):
    seqs, rows, _ = hidden_states.shape
    tokens = seqs * rows
    seq = lax.axis_size("seq")
    me = lax.axis_index("seq")
    f_qkv, f_out, f_in, f_down_t, f_b, f_vec = gather_weights(
        w_qkv, w_out, w_in, w_down, b_in, vectors
    )
    order = jnp.arange(seq, dtype=jnp.int32) ^ me
    x_blocks = [hidden_states]
    for j in range(1, seq):
        x_blocks.append(lax.ppermute(hidden_states, "seq", [(a, a ^ j) for a in range(seq)]))
    x_rows = [b.reshape(tokens, D) for b in x_blocks]
    vec = f_vec.astype(F32)
    f_kv = f_qkv[:, D:]
    queries = ((mm(x_rows[0], f_qkv[:, :D]) + vec[0]).astype(BF) * SCALE).astype(BF)
    queries = queries.reshape(seqs, rows, D)
    kv_bias = jnp.concatenate([jnp.zeros((D,), F32), vec[1]])
    kv_blocks = [(mm(b, f_kv) + kv_bias).astype(BF).reshape(seqs, rows, 2 * D) for b in x_rows]
    ctx, probs = attend(order, lengths, queries, kv_blocks, prev_logits)
    out, dh1, dctx, act, dinner, dbranch, y1, dattn, dvec, db_in = middle(
        x_rows[0],
        ctx.reshape(tokens, D),
        cotangent.reshape(tokens, D),
        f_out,
        f_in,
        f_down_t,
        f_vec,
        f_b,
    )
    g_down_t = mm_tn(dbranch, act).astype(BF)
    g_in = mm_tn(y1, dinner).astype(BF)
    g_out = mm_tn(ctx.reshape(tokens, D), dattn).astype(BF)
    dlogits, dq, dkv = attend_back(
        order, queries, kv_blocks, probs, dctx.reshape(seqs, rows, D)
    )
    dq = dq.reshape(tokens, D)
    dkv = [b.reshape(tokens, 2 * D) for b in dkv]
    g_q = mm_tn(x_rows[0], dq)
    g_kv = sum(mm_tn(a, b) for a, b in zip(x_rows, dkv))
    g_qkv = jnp.concatenate([g_q, g_kv], 1).astype(BF)
    dx = [mm_nt(b, f_kv) for b in dkv]
    dx_own = dh1 + mm_nt(dq, f_qkv[:, :D]) + dx[0]
    for j in range(1, seq):
        dx_own = dx_own + lax.ppermute(
            dx[j].astype(BF), "seq", [(a, a ^ j) for a in range(seq)]
        ).astype(F32)
    dvec = dvec.at[0].set(jnp.sum(dq, 0, dtype=F32))
    dvec = dvec.at[1].set(sum(jnp.sum(b[:, D:], 0, dtype=F32) for b in dkv))
    owned = reduce_grads(g_qkv, g_out, g_in, g_down_t, db_in, dvec)
    shape = hidden_states.shape
    return (out.reshape(shape), dx_own.astype(BF).reshape(shape), dlogits) + owned


def solution(mesh):
    return jax.shard_map(
        shards,
        mesh=mesh,
        in_specs=(
            P("dp", "seq", None),
            P("dp", None, "seq", None),
            P("dp"),
            P("dp", "seq"),
            P("dp", "seq"),
            P("dp", "seq"),
            P("dp", "seq"),
            P(("dp", "seq")),
            P("seq", "dp"),
            P("dp", "seq", None),
        ),
        out_specs=(
            P("dp", "seq", None),
            P("dp", "seq", None),
            P("dp", None, "seq", None),
            P("dp", "seq"),
            P("dp", "seq"),
            P("dp", "seq"),
            P("dp", "seq"),
            P(("dp", "seq")),
            P("seq", "dp"),
        ),
        check_vma=False,
    )
```

```python
import functools

import jax
import jax.numpy as jnp
from jax import lax
from jax.experimental import pallas as pl
from jax.experimental.pallas import tpu as pltpu
from jax.sharding import PartitionSpec as P

D = 768
HEADS = 12
HEAD_DIM = 64
PAIRS = HEADS // 2
PAIR = 2 * HEAD_DIM
SCALE = HEAD_DIM ** (-0.5)
BF = jnp.bfloat16
F32 = jnp.float32
BOTH = ("dp", "seq")
MIB = 1 << 20


def mm(a, b):
    return lax.dot_general(a, b, (((1,), (0,)), ((), ())), preferred_element_type=F32)


def mm_nt(a, b):
    return lax.dot_general(a, b, (((1,), (1,)), ((), ())), preferred_element_type=F32)


def mm_tn(a, b):
    return lax.dot_general(a, b, (((0,), (0,)), ((), ())), preferred_element_type=F32)


def stack_heads(pair):
    lane = lax.broadcasted_iota(jnp.int32, pair.shape, 1)
    zero = jnp.zeros_like(pair)
    return jnp.concatenate(
        [jnp.where(lane < HEAD_DIM, pair, zero), jnp.where(lane < HEAD_DIM, zero, pair)], 0
    )


def pick_heads(stacked):
    rows = stacked.shape[0] // 2
    lane = lax.broadcasted_iota(jnp.int32, (rows, PAIR), 1)
    return jnp.where(lane < HEAD_DIM, stacked[:rows], stacked[rows:])


def swap(a, axis, bit):
    size = lax.axis_size(axis)
    return lax.ppermute(a, axis, [(i, i ^ bit) for i in range(size)])


def swap_core(a):
    return swap(a, "seq", 1)


def swap_x(a):
    return swap(a, "seq", 2)


def swap_y(a):
    return swap(a, "dp", 1)


def shift_z(a, places):
    size = lax.axis_size("dp")
    return lax.ppermute(a, "dp", [(i, (i + 2 * places) % size) for i in range(size)])


def by_pieces():
    return lax.axis_size("dp") == 8 and lax.axis_size("seq") == 4


def place():
    dp, seq = lax.axis_index("dp"), lax.axis_index("seq")
    return dp >> 1, dp & 1, seq >> 1, seq & 1


def gather_pieces(a):
    own = jnp.stack([a] + [shift_z(a, k) for k in range(1, 4)])
    own_x = swap_x(own)
    half = [own, own_x, swap_y(own), swap_y(own_x)]
    return half + [swap_core(b) for b in half]


def piece_table():
    z, y, x, core = place()
    table = []
    for far in range(8):
        for k in range(4):
            table.append(2 * ((z - k) & 3) + (y ^ (far >> 1 & 1)))
            table.append(2 * (x ^ (far & 1)) + (core ^ (far >> 2)))
    return jnp.stack(table).astype(jnp.int32)


def pieces_of(refs, table_ref):
    for a, ref in enumerate(refs):
        depth = ref.shape[0]
        for k in range(depth):
            n = a * depth + k
            yield ref.at[k], table_ref[2 * n], table_ref[2 * n + 1]


def wait_whole(ref, sem):
    pltpu.make_async_copy(ref, ref, sem).wait()


def add(*parts):
    return sum(p.astype(F32) for p in parts)


def low(a):
    return a.astype(BF)


def reduce_pieces(send, keep, first, second):
    got = swap_core(send)
    got_first = first(low(add(keep[1], got[1])))
    got_second = second(low(add(keep[0, 1], got[0, 1], got_first[1])))
    parts = lambda k: add(keep[0, 0, k], got[0, 0, k], got_first[0, k], got_second[k])
    return parts(0) + add(*[shift_z(low(parts(k)), k) for k in range(1, 4)])


def project_kernel(count, table_ref, x0_ref, x1_ref, x2_ref, x3_ref, bias_ref, *refs):
    piece_refs = refs[:count]
    q_ref, kv_ref, w_ref, w_all, stage, sems = refs[count:]
    which, part = pl.program_id(0), pl.program_id(1)
    last = (which == pl.num_programs(0) - 1) & (part == pl.num_programs(1) - 1)
    keep = pltpu.make_async_copy(w_all, w_ref, sems.at[1])

    @pl.when((which == 0) & (part == 0))
    def _():
        if count == 1:
            pltpu.make_async_copy(piece_refs[0], w_all, sems.at[0]).start()
            wait_whole(w_all, sems.at[0])
        else:
            high, wide = stage.shape[1] // 8, stage.shape[2]
            for piece, dp, seq in pieces_of(piece_refs, table_ref):
                rows = pl.ds(pl.multiple_of(dp * high, high), high)
                pltpu.make_async_copy(piece, stage.at[seq, rows], sems.at[0]).start()
            wait_whole(stage, sems.at[0])
            for s in range(4):
                w_all[:, s * wide : (s + 1) * wide] = stage[s]
        keep.start()

    for j, x_ref in enumerate((x0_ref, x1_ref, x2_ref, x3_ref)):

        @pl.when(which == j)
        def _():
            rows = x_ref[...]
            kv_ref[0, :, :D] = mm(rows, w_all[:, D : 2 * D]).astype(BF)
            kv_ref[0, :, D:] = (mm(rows, w_all[:, 2 * D :]) + bias_ref[1:2]).astype(BF)
            if j == 0:
                query = (mm(rows, w_all[:, :D]) + bias_ref[0:1]).astype(BF)
                q_ref[...] = query * SCALE

    @pl.when(last)
    def _():
        keep.wait()


def project(table, x_blocks, bias, pieces):
    tokens = x_blocks[0].shape[0]
    step = 512
    parts = tokens // step

    def x_spec(j):
        return pl.BlockSpec(
            (step, D),
            lambda i, b, *_: (jnp.where(i == j, b, jnp.where(i < j, 0, parts - 1)), 0),
        )

    wide = 3 * D // 4
    return pl.pallas_call(
        functools.partial(project_kernel, len(pieces)),
        grid_spec=pltpu.PrefetchScalarGridSpec(
            num_scalar_prefetch=1,
            grid=(4, parts),
            in_specs=[x_spec(j) for j in range(4)]
            + [pl.BlockSpec((8, D), lambda i, b, *_: (0, 0))]
            + [pl.BlockSpec(memory_space=pl.ANY)] * len(pieces),
            out_specs=[
                pl.BlockSpec(
                    (step, D), lambda i, b, *_: (jnp.where(i == 0, b, parts - 1), 0)
                ),
                pl.BlockSpec((1, step, 2 * D), lambda i, b, *_: (i, b, 0)),
                pl.BlockSpec(memory_space=pl.ANY),
            ],
            scratch_shapes=[
                pltpu.VMEM((D, 3 * D), BF),
                pltpu.VMEM((4, D, wide), BF),
                pltpu.SemaphoreType.DMA((2,)),
            ],
        ),
        out_shape=[
            jax.ShapeDtypeStruct((tokens, D), BF),
            jax.ShapeDtypeStruct((4, tokens, 2 * D), BF),
            jax.ShapeDtypeStruct((D, 3 * D), BF),
        ],
        compiler_params=pltpu.CompilerParams(vmem_limit_bytes=40 * MIB),
        cost_estimate=pl.CostEstimate(
            flops=2 * tokens * D * 9 * D, bytes_accessed=30 * MIB, transcendentals=0
        ),
    )(table, *x_blocks, bias, *pieces)


def kv_specs(blocks, rows):
    return [
        pl.BlockSpec((1, 1, rows, 2 * D), functools.partial(lambda j, b, *_: (j, b, 0, 0), j))
        for j in range(blocks)
    ]


def attend_kernel(blocks, order_ref, len_ref, q_ref, *refs):
    kv_refs = refs[:blocks]
    prev_ref, ctx_ref, probs_ref, kv_all = refs[blocks:]
    rows = q_ref.shape[1]
    total = kv_all.shape[0]
    for j in range(blocks):
        start = pl.multiple_of(order_ref[j] * rows, rows)
        kv_all[pl.ds(start, rows), :] = kv_refs[j][0, 0]
    valid = len_ref[pl.program_id(0)]
    key_pos = lax.broadcasted_iota(jnp.int32, (1, total), 1)
    padding = jnp.where(key_pos < valid, 0.0, -1e9)
    for i in range(PAIRS):
        cols = slice(i * PAIR, (i + 1) * PAIR)
        vcols = slice(D + i * PAIR, D + (i + 1) * PAIR)
        query = stack_heads(q_ref[0, :, cols])
        raw = mm_nt(query, kv_all[:, cols])
        prev = prev_ref[0, 2 * i : 2 * i + 2].reshape(2 * rows, total).astype(F32)
        raw = raw + prev + padding
        largest = jnp.max(raw, -1, keepdims=True)
        expo = jnp.exp(raw - largest)
        summed = jnp.sum(expo, -1, keepdims=True)
        probs = (expo * (1.0 / summed)).astype(BF)
        probs_ref[0, 2 * i : 2 * i + 2] = probs.reshape(2, rows, total)
        ctx_ref[0, :, cols] = pick_heads(mm(probs, kv_all[:, vcols])).astype(BF)


def attend(order, lengths, queries, keys_values, prev_logits):
    seqs, rows, _ = queries.shape
    blocks = keys_values.shape[0]
    total = prev_logits.shape[-1]
    row_spec = lambda width: pl.BlockSpec((1, rows, width), lambda b, *_: (b, 0, 0))
    head_spec = pl.BlockSpec((1, HEADS, rows, total), lambda b, *_: (b, 0, 0, 0))
    return pl.pallas_call(
        functools.partial(attend_kernel, blocks),
        grid_spec=pltpu.PrefetchScalarGridSpec(
            num_scalar_prefetch=2,
            grid=(seqs,),
            in_specs=[row_spec(D)] + kv_specs(blocks, rows) + [head_spec],
            out_specs=[row_spec(D), head_spec],
            scratch_shapes=[pltpu.VMEM((total, 2 * D), BF)],
        ),
        out_shape=[
            jax.ShapeDtypeStruct(queries.shape, BF),
            jax.ShapeDtypeStruct(prev_logits.shape, BF),
        ],
        compiler_params=pltpu.CompilerParams(vmem_limit_bytes=48 * MIB),
        cost_estimate=pl.CostEstimate(
            flops=4 * seqs * HEADS * rows * total * PAIR,
            bytes_accessed=4 * seqs * HEADS * rows * total,
            transcendentals=seqs * HEADS * rows * total,
        ),
    )(order, lengths, queries, *[keys_values] * blocks, prev_logits)


def attend_back_kernel(blocks, order_ref, q_ref, *refs):
    kv_refs = refs[:blocks]
    probs_ref, dctx_ref, dlogits_ref, dq_ref = refs[blocks : blocks + 4]
    dkv_refs = refs[blocks + 4 : 2 * blocks + 4]
    kv_all, dkv_all = refs[2 * blocks + 4 :]
    rows = q_ref.shape[1]
    total = kv_all.shape[0]
    starts = [pl.multiple_of(order_ref[j] * rows, rows) for j in range(blocks)]
    for j in range(blocks):
        kv_all[pl.ds(starts[j], rows), :] = kv_refs[j][0, 0]
    for i in range(PAIRS):
        cols = slice(i * PAIR, (i + 1) * PAIR)
        vcols = slice(D + i * PAIR, D + (i + 1) * PAIR)
        query = stack_heads(q_ref[0, :, cols])
        dctx = stack_heads(dctx_ref[0, :, cols])
        probs = probs_ref[0, 2 * i : 2 * i + 2].reshape(2 * rows, total)
        dprobs = mm_nt(dctx, kv_all[:, vcols])
        wide = probs.astype(F32)
        prod = wide * dprobs
        weighted = jnp.sum(prod, -1, keepdims=True)
        dlogits = (prod - wide * weighted).astype(BF)
        dlogits_ref[0, 2 * i : 2 * i + 2] = dlogits.reshape(2, rows, total)
        dq_ref[0, :, cols] = (pick_heads(mm(dlogits, kv_all[:, cols])) * SCALE).astype(BF)
        dkv_all[:, cols] = mm_tn(dlogits, query).astype(BF)
        dkv_all[:, vcols] = mm_tn(probs, dctx).astype(BF)
    for j in range(blocks):
        dkv_refs[j][0] = dkv_all[pl.ds(starts[j], rows), :]


def attend_back(order, queries, keys_values, probs, dctx):
    seqs, rows, _ = queries.shape
    blocks = keys_values.shape[0]
    total = probs.shape[-1]
    row_spec = lambda width: pl.BlockSpec((1, rows, width), lambda b, *_: (b, 0, 0))
    head_spec = pl.BlockSpec((1, HEADS, rows, total), lambda b, *_: (b, 0, 0, 0))
    outs = pl.pallas_call(
        functools.partial(attend_back_kernel, blocks),
        grid_spec=pltpu.PrefetchScalarGridSpec(
            num_scalar_prefetch=1,
            grid=(seqs,),
            in_specs=[row_spec(D)] + kv_specs(blocks, rows) + [head_spec, row_spec(D)],
            out_specs=[head_spec, row_spec(D)] + [row_spec(2 * D)] * blocks,
            scratch_shapes=[pltpu.VMEM((total, 2 * D), BF), pltpu.VMEM((total, 2 * D), BF)],
        ),
        out_shape=[
            jax.ShapeDtypeStruct(probs.shape, BF),
            jax.ShapeDtypeStruct(queries.shape, BF),
        ]
        + [jax.ShapeDtypeStruct((seqs, rows, 2 * D), BF)] * blocks,
        compiler_params=pltpu.CompilerParams(vmem_limit_bytes=48 * MIB),
        cost_estimate=pl.CostEstimate(
            flops=8 * seqs * HEADS * rows * total * PAIR,
            bytes_accessed=4 * seqs * HEADS * rows * total,
            transcendentals=0,
        ),
    )(order, queries, *[keys_values] * blocks, probs, dctx)
    return outs[0], outs[1], outs[2:]


def gelu_and_slope(values):
    size = jnp.abs(values)
    bell = jnp.exp(values * values * -0.5)
    t = 1.0 / (1.0 + (0.3275911 * 0.7071067811865476) * size)
    tail = (0.5 * 1.061405429) * t + (0.5 * -1.453152027)
    tail = tail * t + (0.5 * 1.421413741)
    tail = tail * t + (0.5 * -0.284496736)
    tail = tail * t + (0.5 * 0.254829592)
    tail = tail * t * bell
    cdf = jnp.where(values >= 0.0, 1.0 - tail, tail)
    return values * cdf, cdf + values * bell * 0.3989422804014327


def norm(values):
    average = jnp.mean(values, -1, keepdims=True)
    centred = values - average
    inverse = lax.rsqrt(jnp.mean(centred * centred, -1, keepdims=True) + 1e-06)
    return centred * inverse, inverse


def norm_back(grad, normed, inverse):
    first = jnp.mean(grad, -1, keepdims=True)
    second = jnp.mean(grad * normed, -1, keepdims=True)
    return inverse * (grad - first - normed * second)


def load_middle(table_ref, in_refs, down_refs, w_out_ref, w_in_ref, w_down_ref, stage, sems):
    if len(in_refs) == 1:
        pltpu.make_async_copy(in_refs[0], w_in_ref, sems.at[1]).start()
        pltpu.make_async_copy(down_refs[0], w_down_ref, sems.at[2]).start()
        pltpu.make_async_copy(down_refs[1], w_out_ref, sems.at[0]).start()
        wait_whole(w_out_ref, sems.at[0])
    else:
        down = w_down_ref.shape[0] // 4
        wide = w_down_ref.shape[1] // 8
        high, half = D // 8, D // 16
        for piece, dp, seq in pieces_of(down_refs, table_ref):
            pltpu.make_async_copy(
                piece.at[pl.ds(down, half)], stage.at[seq, dp], sems.at[0]
            ).start()
        for piece, dp, seq in pieces_of(in_refs, table_ref):
            rows = pl.ds(pl.multiple_of(dp * high, high), high)
            cols = pl.ds(pl.multiple_of(seq * D, D), D)
            pltpu.make_async_copy(piece, w_in_ref.at[rows, cols], sems.at[1]).start()
        for piece, dp, seq in pieces_of(down_refs, table_ref):
            rows = pl.ds(pl.multiple_of(seq * down, down), down)
            cols = pl.ds(pl.multiple_of(dp * wide, wide), wide)
            pltpu.make_async_copy(
                piece.at[pl.ds(0, down)], w_down_ref.at[rows, cols], sems.at[2]
            ).start()
        wait_whole(stage, sems.at[0])
        for s in range(4):
            for d in range(8):
                cols = slice(s * down, (s + 1) * down)
                w_out_ref[d * high : d * high + half, cols] = stage[s, d][:, :down]
                w_out_ref[d * high + half : (d + 1) * high, cols] = stage[s, d][:, down:]


def middle_kernel(
    counts, table_ref, x_ref, ctx_ref, cot_ref, vec_ref, b_in_ref, *refs
):
    in_refs, refs = refs[: counts[0]], refs[counts[0] :]
    down_refs, refs = refs[: counts[1]], refs[counts[1] :]
    (
        out_ref, dh1_ref, dctx_ref, act_ref, dinner_ref, dbranch_ref, y1_ref, dattn_ref,
        dvec_ref, db_in_ref, w_out_ref, w_in_ref, w_down_ref, stage, sems,
    ) = refs

    @pl.when(pl.program_id(0) == 0)
    def _():
        load_middle(
            table_ref, in_refs, down_refs, w_out_ref, w_in_ref, w_down_ref, stage, sems
        )
        dvec_ref[...] = jnp.zeros_like(dvec_ref)
        db_in_ref[...] = jnp.zeros_like(db_in_ref)

    vec = lambda i: vec_ref[i : i + 1, :].astype(F32)
    total = lambda v: jnp.sum(v, 0, keepdims=True)
    h1 = x_ref[...].astype(F32) + (mm(ctx_ref[...], w_out_ref[...]) + vec(2))
    normed1, inverse1 = norm(h1)
    y1 = normed1 * vec(3) + vec(4)
    y1_low = y1.astype(BF)
    y1_ref[...] = y1_low

    @pl.when(pl.program_id(0) == 0)
    def _():
        wait_whole(w_in_ref, sems.at[1])

    inner = mm(y1_low, w_in_ref[...]) + b_in_ref[...].astype(F32)
    act, slope = gelu_and_slope(inner)
    act = act.astype(BF)
    act_ref[...] = act

    @pl.when(pl.program_id(0) == 0)
    def _():
        wait_whole(w_down_ref, sems.at[2])

    h2 = y1 + (mm_nt(act, w_down_ref[...]) + vec(5))
    normed2, inverse2 = norm(h2)
    out_ref[...] = (normed2 * vec(6) + vec(7)).astype(BF)
    cot = cot_ref[...].astype(F32)
    dh2 = norm_back(cot * vec(6), normed2, inverse2)
    dbranch = dh2.astype(BF)
    dbranch_ref[...] = dbranch
    dinner = (mm(dbranch, w_down_ref[...]) * slope).astype(BF)
    dinner_ref[...] = dinner
    dy1 = dh2 + mm_nt(dinner, w_in_ref[...])
    dh1 = norm_back(dy1 * vec(3), normed1, inverse1)
    dh1_ref[...] = dh1
    dattn = dh1.astype(BF)
    dattn_ref[...] = dattn
    dctx_ref[...] = mm_nt(dattn, w_out_ref[...]).astype(BF)
    db_in_ref[...] += total(dinner.astype(F32))
    dvec_ref[2:3, :] += total(dattn.astype(F32))
    dvec_ref[3:4, :] += total(dy1 * normed1)
    dvec_ref[4:5, :] += total(dy1)
    dvec_ref[5:6, :] += total(dbranch.astype(F32))
    dvec_ref[6:7, :] += total(cot * normed2)
    dvec_ref[7:8, :] += total(cot)


def middle(table, x, ctx, cot, vectors, b_in, in_pieces, down_pieces):
    tokens = x.shape[0]
    ff = b_in.shape[1]
    step = 256
    rows = lambda width: pl.BlockSpec((step, width), lambda i, *_: (i, 0))
    whole = lambda a: pl.BlockSpec(a.shape, lambda i, *_: (0, 0))
    fixed = lambda *shape: pl.BlockSpec(shape, lambda i, *_: (0, 0))
    sds = jax.ShapeDtypeStruct
    counts = (len(in_pieces), len(down_pieces))
    return pl.pallas_call(
        functools.partial(middle_kernel, counts),
        grid_spec=pltpu.PrefetchScalarGridSpec(
            num_scalar_prefetch=1,
            grid=(tokens // step,),
            in_specs=[rows(D)] * 3
            + [whole(vectors), whole(b_in)]
            + [pl.BlockSpec(memory_space=pl.ANY)] * sum(counts),
            out_specs=[rows(D)] * 3
            + [rows(ff)] * 2
            + [rows(D)] * 3
            + [fixed(8, D), fixed(1, ff)],
            scratch_shapes=[
                pltpu.VMEM((D, D), BF),
                pltpu.VMEM((D, ff), BF),
                pltpu.VMEM((D, ff), BF),
                pltpu.VMEM((4, 8, D // 16, ff // 8), BF),
                pltpu.SemaphoreType.DMA((3,)),
            ],
        ),
        out_shape=[
            sds((tokens, D), BF),
            sds((tokens, D), F32),
            sds((tokens, D), BF),
            sds((tokens, ff), BF),
            sds((tokens, ff), BF),
            sds((tokens, D), BF),
            sds((tokens, D), BF),
            sds((tokens, D), BF),
            sds((8, D), F32),
            sds((1, ff), F32),
        ],
        compiler_params=pltpu.CompilerParams(vmem_limit_bytes=56 * MIB),
        cost_estimate=pl.CostEstimate(
            flops=tokens * (8 * D * ff + 4 * D * D),
            bytes_accessed=40 * MIB,
            transcendentals=2 * tokens * ff,
        ),
    )(table, x, ctx, cot, vectors, b_in, *in_pieces, *down_pieces)


def grad_in_kernel(where_ref, y1_ref, dinner_ref, send_ref, keep_ref):
    z, y = where_ref[0], where_ref[1]
    step = pl.program_id(0)
    high = D // 8
    grad = mm_tn(y1_ref[...], dinner_ref[...]).astype(BF)
    for d in range(8):
        rows = grad[d * high : (d + 1) * high]
        far_y, far_z = y ^ (d & 1), ((d >> 1) - z) & 3

        @pl.when(step < 2)
        def _():
            send_ref[far_y, 0, far_z] = rows

        @pl.when(step >= 2)
        def _():
            keep_ref[far_y, 0, far_z] = rows


def grad_in(where, y1, dinner):
    tokens, ff = dinner.shape
    wide = ff // 4

    def columns(t, where):
        return (0, 2 * (where[2] ^ (t & 1)) + (where[3] ^ (1 - (t >> 1))))

    piece = (2, 1, 4, D // 8, wide)
    shape = jax.ShapeDtypeStruct((2, 2, 4, D // 8, wide), BF)
    return pl.pallas_call(
        grad_in_kernel,
        grid_spec=pltpu.PrefetchScalarGridSpec(
            num_scalar_prefetch=1,
            grid=(4,),
            in_specs=[
                pl.BlockSpec((tokens, D), lambda t, w: (0, 0)),
                pl.BlockSpec((tokens, wide), columns),
            ],
            out_specs=[
                pl.BlockSpec(piece, lambda t, w: (0, jnp.minimum(t, 1), 0, 0, 0)),
                pl.BlockSpec(piece, lambda t, w: (0, jnp.maximum(t - 2, 0), 0, 0, 0)),
            ],
        ),
        out_shape=[shape, shape],
        compiler_params=pltpu.CompilerParams(vmem_limit_bytes=40 * MIB),
        cost_estimate=pl.CostEstimate(
            flops=2 * tokens * D * ff, bytes_accessed=14 * MIB, transcendentals=0
        ),
    )(where, y1, dinner)


def grad_down_kernel(
    where_ref, dbranch_ref, act_ref, ctx_ref, dattn_ref, send_ref, keep_ref, grad_out
):
    y, x, core = where_ref[1], where_ref[2], where_ref[3]
    step = pl.program_id(0)
    wide, down = D // 2, D // 4
    high, half = D // 8, D // 16

    @pl.when(step == 0)
    def _():
        grad_out[...] = mm_tn(ctx_ref[...], dattn_ref[...])

    def put(far_x, far_y, rows, cols, even, odd):
        first = core == 0
        keep_ref[far_x, far_y, 0, rows, cols] = jnp.where(first, even, odd).astype(BF)
        send_ref[far_x, far_y, 0, rows, cols] = jnp.where(first, odd, even).astype(BF)

    grad = mm_tn(dbranch_ref[...], act_ref[...])
    for j in range(2):
        top = pl.multiple_of((2 * step + j) * high, high)
        upper, lower = grad_out[pl.ds(top, half), :], grad_out[pl.ds(top + half, half), :]
        for i in range(2):
            pair = [slice((2 * i + k) * down, (2 * i + k + 1) * down) for k in range(2)]
            side = slice(j * wide, (j + 1) * wide)
            far = (x ^ i, y ^ j)
            put(*far, slice(0, down), slice(None), grad[pair[0], side], grad[pair[1], side])
            tail = slice(down, down + half)
            put(*far, tail, slice(0, down), upper[:, pair[0]], upper[:, pair[1]])
            put(*far, tail, slice(down, 2 * down), lower[:, pair[0]], lower[:, pair[1]])


def grad_down(where, dbranch, act, ctx, dattn):
    tokens, ff = act.shape
    wide = ff // 4
    whole = pl.BlockSpec((tokens, D), lambda t, w: (0, 0))
    piece = (D // 4 + D // 16, ff // 8)
    spec = pl.BlockSpec((2, 2, 1) + piece, lambda t, w: (0, 0, (t - w[0]) & 3, 0, 0))
    shape = jax.ShapeDtypeStruct((2, 2, 4) + piece, BF)
    return pl.pallas_call(
        grad_down_kernel,
        grid_spec=pltpu.PrefetchScalarGridSpec(
            num_scalar_prefetch=1,
            grid=(4,),
            in_specs=[whole, pl.BlockSpec((tokens, wide), lambda t, w: (0, t)), whole, whole],
            out_specs=[spec, spec],
            scratch_shapes=[pltpu.VMEM((D, D), F32)],
        ),
        out_shape=[shape, shape],
        compiler_params=pltpu.CompilerParams(vmem_limit_bytes=40 * MIB),
        cost_estimate=pl.CostEstimate(
            flops=2 * tokens * D * (ff + D), bytes_accessed=20 * MIB, transcendentals=0
        ),
    )(where, dbranch, act, ctx, dattn)


def grad_qkv_kernel(
    where_ref, x0_ref, x2_ref, dq_ref, dkv0_ref, dkv2_ref, send_ref, keep_ref, grad
):
    z, y, x, core = (where_ref[i] for i in range(4))
    step = pl.program_id(0)
    wide, high = 3 * D // 4, D // 8

    @pl.when(step == 0)
    def _():
        grad[:, :D] = mm_tn(x0_ref[...], dq_ref[...])

    for t in (1, 2):

        @pl.when(step == t)
        def _():
            grad[:, t * D : (t + 1) * D] = mm_tn(x0_ref[...], dkv0_ref[...]) + mm_tn(
                x2_ref[...], dkv2_ref[...]
            )

    @pl.when(step == 2)
    def _():
        first = core == 0
        for i in range(2):
            even = grad[:, 2 * i * wide : (2 * i + 1) * wide]
            odd = grad[:, (2 * i + 1) * wide : (2 * i + 2) * wide]
            kept = jnp.where(first, even, odd).astype(BF)
            sent = jnp.where(first, odd, even).astype(BF)
            for d in range(8):
                rows = slice(d * high, (d + 1) * high)
                far = (y ^ (d & 1), x ^ i, ((d >> 1) - z) & 3)
                keep_ref[far] = kept[rows]
                send_ref[far] = sent[rows]


def grad_qkv(where, x0, x2, dq, dkv0, dkv2):
    tokens = x0.shape[0]
    whole = pl.BlockSpec((tokens, D), lambda t, w: (0, 0))
    part = pl.BlockSpec((tokens, D), lambda t, w: (0, jnp.maximum(t - 1, 0)))
    dims = (2, 2, 4, D // 8, 3 * D // 4)
    spec = pl.BlockSpec(dims, lambda t, w: (0, 0, 0, 0, 0))
    shape = jax.ShapeDtypeStruct(dims, BF)
    return pl.pallas_call(
        grad_qkv_kernel,
        grid_spec=pltpu.PrefetchScalarGridSpec(
            num_scalar_prefetch=1,
            grid=(3,),
            in_specs=[whole, whole, whole, part, part],
            out_specs=[spec, spec],
            scratch_shapes=[pltpu.VMEM((D, 3 * D), F32)],
        ),
        out_shape=[shape, shape],
        compiler_params=pltpu.CompilerParams(vmem_limit_bytes=48 * MIB),
        cost_estimate=pl.CostEstimate(
            flops=2 * tokens * D * 5 * D, bytes_accessed=16 * MIB, transcendentals=0
        ),
    )(where, x0, x2, dq, dkv0, dkv2)


def grad_rows_kernel(own, *refs):
    if own:
        dkv_ref, got_ref, w_ref, dq_ref, dh1_ref, dx_ref, sum_ref, bias_ref = refs
    else:
        dkv_ref, got_ref, w_ref, dx_ref, sum_ref, bias_ref = refs

    @pl.when(pl.program_id(0) == 0)
    def _():
        bias_ref[...] = jnp.zeros_like(bias_ref)

    total = (dkv_ref[...].astype(F32) + got_ref[...].astype(F32)).astype(BF)
    sum_ref[...] = total
    bias_ref[1:2, :] += jnp.sum(total[:, D:].astype(F32), 0, keepdims=True)
    dx = mm_nt(total, w_ref[:, D:])
    if own:
        dq = dq_ref[...]
        bias_ref[0:1, :] += jnp.sum(dq.astype(F32), 0, keepdims=True)
        dx = dx + mm_nt(dq, w_ref[:, :D]) + dh1_ref[...]
    dx_ref[...] = dx.astype(dx_ref.dtype)


def grad_rows(dkv, got, w_qkv, dq=None, dh1=None):
    own = dq is not None
    tokens = dkv.shape[0]
    step = 512
    rows = lambda width: pl.BlockSpec((step, width), lambda i: (i, 0))
    sds = jax.ShapeDtypeStruct
    return pl.pallas_call(
        functools.partial(grad_rows_kernel, own),
        grid=(tokens // step,),
        in_specs=[
            rows(2 * D),
            rows(2 * D),
            pl.BlockSpec((D, 3 * D), lambda i: (0, 0), pipeline_mode=pl.Buffered(1)),
        ]
        + [rows(D)] * (2 if own else 0),
        out_specs=[rows(D), rows(2 * D), pl.BlockSpec((8, D), lambda i: (0, 0))],
        out_shape=[
            sds((tokens, D), F32 if own else BF),
            sds((tokens, 2 * D), BF),
            sds((8, D), F32),
        ],
        compiler_params=pltpu.CompilerParams(vmem_limit_bytes=40 * MIB),
        cost_estimate=pl.CostEstimate(
            flops=2 * tokens * D * (3 if own else 2) * D,
            bytes_accessed=16 * MIB,
            transcendentals=0,
        ),
    )(dkv, got, w_qkv, *((dq, dh1) if own else ()))


def gather_small(b_in, vectors):
    dp, seq = lax.axis_size("dp"), lax.axis_size("seq")
    small = jnp.concatenate([vectors.reshape(-1), b_in])
    whole = lax.all_gather(small, BOTH, axis=0, tiled=False)
    nv = vectors.size
    vec = whole[:, :nv].reshape((dp, seq) + vectors.shape).transpose(1, 2, 0, 3)
    return whole[:, nv:].reshape(1, -1), vec.reshape(8, D)


def reduce_small(g_b, g_vec):
    dp, seq = lax.axis_size("dp"), lax.axis_size("seq")
    vec = g_vec.reshape(seq, 8 // seq, dp, D // dp).transpose(2, 0, 1, 3)
    small = jnp.concatenate([vec.reshape(dp * seq, -1), g_b.reshape(dp * seq, -1)], 1)
    mine = lax.psum_scatter(small, BOTH, scatter_dimension=0, tiled=True)[0]
    nv = 8 * D // (dp * seq)
    return mine[nv:], mine[:nv].reshape(8 // seq, D // dp)


def gather_plain(w_qkv, w_out, w_in, w_down_t):
    both = lambda a, first, second: lax.all_gather(
        lax.all_gather(a, first, axis=0, tiled=True), second, axis=1, tiled=True
    )
    return (
        [both(w_qkv, "dp", "seq")],
        [both(w_in, "dp", "seq")],
        [both(w_down_t, "seq", "dp"), both(w_out, "dp", "seq")],
    )


def reduce_plain(a, first, second):
    part = lax.psum_scatter(a.astype(BF), first, scatter_dimension=0, tiled=True)
    return lax.psum_scatter(part, second, scatter_dimension=1, tiled=True).astype(F32)


def shards(
    hidden_states, prev_logits, lengths, w_qkv, w_out, w_in, w_down, b_in, vectors, cotangent
):
    seqs, rows, _ = hidden_states.shape
    tokens = seqs * rows
    seq = lax.axis_size("seq")
    me = lax.axis_index("seq")
    apart = by_pieces()
    order = jnp.arange(seq, dtype=jnp.int32) ^ me
    x0 = hidden_states.reshape(tokens, D)
    x2 = swap_x(x0)
    x_blocks = [x0, swap_core(x0), x2, swap_core(x2)]
    f_b, f_vec = gather_small(b_in, vectors)
    if apart:
        table, where = piece_table(), jnp.stack(place()).astype(jnp.int32)
        half = w_out.shape[0] // 2
        low_rows = jnp.concatenate([w_out[:half], w_out[half:]], 1)
        qkv_pieces = gather_pieces(w_qkv)
        in_pieces = gather_pieces(w_in)
        down_pieces = gather_pieces(jnp.concatenate([w_down.T, low_rows], 0))
    else:
        table = jnp.zeros((2,), jnp.int32)
        qkv_pieces, in_pieces, down_pieces = gather_plain(w_qkv, w_out, w_in, w_down.T)
    queries, keys_values, f_qkv = project(table, x_blocks, f_vec.astype(F32), qkv_pieces)
    queries = queries.reshape(seqs, rows, D)
    keys_values = keys_values.reshape(seq, seqs, rows, 2 * D)
    ctx, probs = attend(order, lengths, queries, keys_values, prev_logits)
    ctx = ctx.reshape(tokens, D)
    out, dh1, dctx, act, dinner, dbranch, y1, dattn, dvec, db_in = middle(
        table, x0, ctx, cotangent.reshape(tokens, D), f_vec, f_b, in_pieces, down_pieces
    )
    if apart:
        o_in = reduce_pieces(*grad_in(where, y1, dinner), swap_y, swap_x)
        o_low = reduce_pieces(*grad_down(where, dbranch, act, ctx, dattn), swap_x, swap_y)
        down = w_down.shape[1]
        o_down = o_low[:down].T
        o_out = jnp.concatenate([o_low[down:, :down], o_low[down:, down:]], 0)
    else:
        o_in = reduce_plain(mm_tn(y1, dinner), "dp", "seq")
        o_down = reduce_plain(mm_tn(act, dbranch), "dp", "seq")
        o_out = reduce_plain(mm_tn(ctx, dattn), "dp", "seq")
    dlogits, dq, dkv = attend_back(
        order, queries, keys_values, probs, dctx.reshape(seqs, rows, D)
    )
    dq = dq.reshape(tokens, D)
    dkv = [b.reshape(tokens, 2 * D) for b in dkv]
    dx2, dkv2, bias2 = grad_rows(dkv[2], swap_core(dkv[3]), f_qkv)
    got_rows = swap_x(dx2)
    dx0, dkv0, bias0 = grad_rows(dkv[0], swap_core(dkv[1]), f_qkv, dq, dh1)
    if apart:
        o_qkv = reduce_pieces(*grad_qkv(where, x0, x2, dq, dkv0, dkv2), swap_y, swap_x)
    else:
        g_kv = mm_tn(x0, dkv0) + mm_tn(x2, dkv2)
        o_qkv = reduce_plain(jnp.concatenate([mm_tn(x0, dq), g_kv], 1), "dp", "seq")
    g_b, g_vec = reduce_small(db_in, dvec + bias0 + bias2)
    grad_hidden = low(dx0 + got_rows.astype(F32))
    shape = hidden_states.shape
    return (
        out.reshape(shape),
        grad_hidden.reshape(shape),
        dlogits,
        o_qkv,
        o_out,
        o_in,
        o_down,
        g_b,
        g_vec,
    )


def solution(mesh):
    return jax.shard_map(
        shards,
        mesh=mesh,
        in_specs=(
            P("dp", "seq", None),
            P("dp", None, "seq", None),
            P("dp"),
            P("dp", "seq"),
            P("dp", "seq"),
            P("dp", "seq"),
            P("dp", "seq"),
            P(("dp", "seq")),
            P("seq", "dp"),
            P("dp", "seq", None),
        ),
        out_specs=(
            P("dp", "seq", None),
            P("dp", "seq", None),
            P("dp", None, "seq", None),
            P("dp", "seq"),
            P("dp", "seq"),
            P("dp", "seq"),
            P("dp", "seq"),
            P(("dp", "seq")),
            P("seq", "dp"),
        ),
        check_vma=False,
    )
```

```python
import functools

import jax
import jax.numpy as jnp
from jax import lax
from jax.experimental import pallas as pl
from jax.experimental.pallas import tpu as pltpu
from jax.sharding import PartitionSpec as P

D = 768
HEADS = 12
HEAD_DIM = 64
PAIRS = HEADS // 2
PAIR = 2 * HEAD_DIM
SCALE = HEAD_DIM ** (-0.5)
BF = jnp.bfloat16
F32 = jnp.float32
BOTH = ("dp", "seq")
MIB = 1 << 20
PAD = 16
ANY = pl.BlockSpec(memory_space=pl.ANY)
GRANT = 60 * MIB


def mm(a, b):
    return lax.dot_general(a, b, (((1,), (0,)), ((), ())), preferred_element_type=F32)


def mm_nt(a, b):
    return lax.dot_general(a, b, (((1,), (1,)), ((), ())), preferred_element_type=F32)


def mm_tn(a, b):
    return lax.dot_general(a, b, (((0,), (0,)), ((), ())), preferred_element_type=F32)


def stack_heads(pair):
    lane = lax.broadcasted_iota(jnp.int32, pair.shape, 1)
    zero = jnp.zeros_like(pair)
    return jnp.concatenate(
        [jnp.where(lane < HEAD_DIM, pair, zero), jnp.where(lane < HEAD_DIM, zero, pair)], 0
    )


def pick_heads(stacked):
    rows = stacked.shape[0] // 2
    lane = lax.broadcasted_iota(jnp.int32, (rows, PAIR), 1)
    return jnp.where(lane < HEAD_DIM, stacked[:rows], stacked[rows:])


def swap(a, axis, bit):
    size = lax.axis_size(axis)
    return lax.ppermute(a, axis, [(i, i ^ bit) for i in range(size)])


def swap_core(a):
    return swap(a, "seq", 1)


def swap_x(a):
    return swap(a, "seq", 2)


def swap_y(a):
    return swap(a, "dp", 1)


def swap_z(a, places):
    return swap(a, "dp", 2 * places)


def by_pieces():
    return lax.axis_size("dp") == 8 and lax.axis_size("seq") == 4


def place():
    dp, seq = lax.axis_index("dp"), lax.axis_index("seq")
    return dp >> 1, dp & 1, seq >> 1, seq & 1


def stack_z(a):
    pair = jnp.stack([a, swap_z(a, 1)])
    return jnp.concatenate([pair, swap_z(pair, 2)], 0)


def stack_z_direct(a):
    return jnp.stack([a] + [swap_z(a, k) for k in range(1, 4)])


def spread(own, own_x, own_y, own_xy):
    half = [own, own_x, own_y, own_xy]
    return half + [swap_core(b) for b in half]


def piece_table():
    z, y, x, core = place()
    table = []
    for far in range(8):
        for k in range(4):
            table.append(2 * (z ^ k) + (y ^ (far >> 1 & 1)))
            table.append(2 * (x ^ (far & 1)) + (core ^ (far >> 2)))
    return jnp.stack(table).astype(jnp.int32)


def pieces_of(refs, table_ref):
    for a, ref in enumerate(refs):
        depth = ref.shape[0]
        for k in range(depth):
            n = a * depth + k
            yield ref.at[k], table_ref[2 * n], table_ref[2 * n + 1]


def wait_whole(ref, sem):
    pltpu.make_async_copy(ref, ref, sem).wait()


def add(*parts):
    return sum(p.astype(F32) for p in parts)


def low(a):
    return a.astype(BF)


def after(a, *done):
    return lax.optimization_barrier((a,) + done)[0]


def load_qkv(table_ref, piece_refs, w_all, vec_ref, b_ref, stage, sems):
    high, wide = D // 8 + PAD, 3 * D // 4
    for piece, dp, seq in pieces_of(piece_refs, table_ref):
        rows = pl.ds(pl.multiple_of(dp * high, PAD), high)
        pltpu.make_async_copy(piece, stage.at[seq, rows], sems.at[0]).start()
    wait_whole(stage, sems.at[0])
    body, width = D // 8, D // 8
    for s in range(4):
        for d in range(8):
            top = d * high
            w_all[d * body : (d + 1) * body, s * wide : (s + 1) * wide] = stage[
                s, top : top + body
            ]
            extra = stage[s, top + body : top + high, :width].astype(F32)
            vec_ref[2 * s : 2 * s + 2, d * width : (d + 1) * width] = extra[0:2]
            place_of = (4 * d + s) * width
            b_ref[0:1, place_of : place_of + width] = extra[2:3]


def project_kernel(count, assemble, table_ref, x0_ref, x1_ref, x2_ref, x3_ref, *refs):
    piece_refs, refs = refs[:count], refs[count:]
    if assemble:
        q_ref, kv_ref, w_ref, vec_ref, b_ref, w_all, stage, sems = refs[-8:]
    else:
        vec_ref = refs[0]
        q_ref, kv_ref, w_all, stage, sems = refs[-5:]
    which, part = pl.program_id(0), pl.program_id(1)

    @pl.when((which == 0) & (part == 0))
    def _():
        if assemble:
            load_qkv(table_ref, piece_refs, w_all, vec_ref, b_ref, stage, sems)
            pltpu.make_async_copy(w_all, w_ref, sems.at[1]).start()
        else:
            pltpu.make_async_copy(piece_refs[0], w_all, sems.at[0]).start()
            wait_whole(w_all, sems.at[0])

    for j, x_ref in enumerate((x0_ref, x1_ref, x2_ref, x3_ref)):

        @pl.when(which == j)
        def _():
            rows = x_ref[...]
            kv_ref[0, :, :D] = mm(rows, w_all[:, D : 2 * D]).astype(BF)
            kv_ref[0, :, D:] = (mm(rows, w_all[:, 2 * D :]) + vec_ref[1:2]).astype(BF)
            if j == 0:
                query = (mm(rows, w_all[:, :D]) + vec_ref[0:1]).astype(BF)
                q_ref[...] = query * SCALE

    if assemble:

        @pl.when((which == 3) & (part == pl.num_programs(1) - 1))
        def _():
            pltpu.make_async_copy(w_all, w_ref, sems.at[1]).wait()


def project(table, x_blocks, starts, tokens, pieces, vec=None, deps=()):
    assemble = vec is None
    step = min(512, tokens)
    parts = tokens // step

    def x_spec(j):
        first = starts[j] // step
        return pl.BlockSpec(
            (step, D),
            lambda i, b, *_: (
                first + jnp.where(i == j, b, jnp.where(i < j, 0, parts - 1)),
                0,
            ),
        )

    ff = 4 * D
    fixed = lambda *shape: pl.BlockSpec(shape, lambda i, b, *_: (0, 0))
    sds = jax.ShapeDtypeStruct
    out_specs = [
        pl.BlockSpec((step, D), lambda i, b, *_: (jnp.where(i == 0, b, parts - 1), 0)),
        pl.BlockSpec((1, step, 2 * D), lambda i, b, *_: (i, b, 0)),
    ]
    out_shape = [sds((tokens, D), BF), sds((4, tokens, 2 * D), BF)]
    if assemble:
        out_specs += [ANY, fixed(8, D), fixed(1, ff)]
        out_shape += [sds((D, 3 * D), BF), sds((8, D), F32), sds((1, ff), F32)]
    stage = (4, 8 * (D // 8 + PAD), 3 * D // 4) if assemble else (1, PAD, 128)
    return pl.pallas_call(
        functools.partial(project_kernel, len(pieces), assemble),
        grid_spec=pltpu.PrefetchScalarGridSpec(
            num_scalar_prefetch=1,
            grid=(4, parts),
            in_specs=[x_spec(j) for j in range(4)]
            + [ANY] * len(pieces)
            + ([] if assemble else [fixed(8, D)])
            + [ANY] * len(deps),
            out_specs=out_specs,
            scratch_shapes=[
                pltpu.VMEM((D, 3 * D), BF),
                pltpu.VMEM(stage, BF),
                pltpu.SemaphoreType.DMA((2,)),
            ],
        ),
        out_shape=out_shape,
        compiler_params=pltpu.CompilerParams(vmem_limit_bytes=GRANT),
        cost_estimate=pl.CostEstimate(
            flops=2 * tokens * D * 9 * D, bytes_accessed=15 * MIB, transcendentals=0
        ),
    )(table, *x_blocks, *pieces, *([] if assemble else [vec]), *deps)


def kv_specs(blocks, rows):
    return [
        pl.BlockSpec((1, 1, rows, 2 * D), functools.partial(lambda j, b, *_: (j, b, 0, 0), j))
        for j in range(blocks)
    ]


def attend_kernel(blocks, first, order_ref, len_ref, q_ref, *refs):
    kv_refs = refs[:blocks]
    prev_ref = refs[blocks]
    ctx_ref, probs_ref, kv_all = refs[-3:]
    rows = q_ref.shape[1]
    total = kv_all.shape[0]
    for j in range(blocks):
        start = pl.multiple_of(order_ref[j] * rows, rows)
        kv_all[pl.ds(start, rows), :] = kv_refs[j][0, 0]
    valid = len_ref[first + pl.program_id(0)]
    key_pos = lax.broadcasted_iota(jnp.int32, (1, total), 1)
    padding = jnp.where(key_pos < valid, 0.0, -1e9)
    for i in range(PAIRS):
        cols = slice(i * PAIR, (i + 1) * PAIR)
        vcols = slice(D + i * PAIR, D + (i + 1) * PAIR)
        query = stack_heads(q_ref[0, :, cols])
        raw = mm_nt(query, kv_all[:, cols])
        prev = prev_ref[0, 2 * i : 2 * i + 2].reshape(2 * rows, total).astype(F32)
        raw = raw + prev + padding
        largest = jnp.max(raw, -1, keepdims=True)
        expo = jnp.exp(raw - largest)
        summed = jnp.sum(expo, -1, keepdims=True)
        probs = (expo * (1.0 / summed)).astype(BF)
        probs_ref[0, 2 * i : 2 * i + 2] = probs.reshape(2, rows, total)
        ctx_ref[0, :, cols] = pick_heads(mm(probs, kv_all[:, vcols])).astype(BF)


def attend(order, lengths, queries, keys_values, prev_logits, first, deps=()):
    seqs, rows, _ = queries.shape
    blocks = keys_values.shape[0]
    total = prev_logits.shape[-1]
    row_spec = lambda width: pl.BlockSpec((1, rows, width), lambda b, *_: (b, 0, 0))
    prev_spec = pl.BlockSpec(
        (1, HEADS, rows, total), lambda b, *_: (first + b, 0, 0, 0)
    )
    head_spec = pl.BlockSpec((1, HEADS, rows, total), lambda b, *_: (b, 0, 0, 0))
    return pl.pallas_call(
        functools.partial(attend_kernel, blocks, first),
        grid_spec=pltpu.PrefetchScalarGridSpec(
            num_scalar_prefetch=2,
            grid=(seqs,),
            in_specs=[row_spec(D)] + kv_specs(blocks, rows) + [prev_spec] + [ANY] * len(deps),
            out_specs=[row_spec(D), head_spec],
            scratch_shapes=[pltpu.VMEM((total, 2 * D), BF)],
        ),
        out_shape=[
            jax.ShapeDtypeStruct(queries.shape, BF),
            jax.ShapeDtypeStruct((seqs, HEADS, rows, total), BF),
        ],
        compiler_params=pltpu.CompilerParams(vmem_limit_bytes=GRANT),
        cost_estimate=pl.CostEstimate(
            flops=4 * seqs * HEADS * rows * total * PAIR,
            bytes_accessed=4 * seqs * HEADS * rows * total,
            transcendentals=seqs * HEADS * rows * total,
        ),
    )(order, lengths, queries, *[keys_values] * blocks, prev_logits, *deps)


def attend_back_kernel(blocks, order_ref, q_ref, *refs):
    kv_refs = refs[:blocks]
    probs_ref, dctx_ref = refs[blocks : blocks + 2]
    dlogits_ref, dq_ref, *dkv_refs, kv_all, dkv_all = refs[-(blocks + 4) :]
    rows = q_ref.shape[1]
    total = kv_all.shape[0]
    starts = [pl.multiple_of(order_ref[j] * rows, rows) for j in range(blocks)]
    for j in range(blocks):
        kv_all[pl.ds(starts[j], rows), :] = kv_refs[j][0, 0]
    for i in range(PAIRS):
        cols = slice(i * PAIR, (i + 1) * PAIR)
        vcols = slice(D + i * PAIR, D + (i + 1) * PAIR)
        query = stack_heads(q_ref[0, :, cols])
        dctx = stack_heads(dctx_ref[0, :, cols])
        probs = probs_ref[0, 2 * i : 2 * i + 2].reshape(2 * rows, total)
        dprobs = mm_nt(dctx, kv_all[:, vcols])
        wide = probs.astype(F32)
        prod = wide * dprobs
        weighted = jnp.sum(prod, -1, keepdims=True)
        dlogits = (prod - wide * weighted).astype(BF)
        dlogits_ref[0, 2 * i : 2 * i + 2] = dlogits.reshape(2, rows, total)
        dq_ref[0, :, cols] = (pick_heads(mm(dlogits, kv_all[:, cols])) * SCALE).astype(BF)
        dkv_all[:, cols] = mm_tn(dlogits, query).astype(BF)
        dkv_all[:, vcols] = mm_tn(probs, dctx).astype(BF)
    for j in range(blocks):
        dkv_refs[j][0] = dkv_all[pl.ds(starts[j], rows), :]


def attend_back(order, queries, keys_values, probs, dctx, dlogits, first, seqs_all, deps=()):
    seqs, rows, _ = queries.shape
    blocks = keys_values.shape[0]
    total = probs.shape[-1]
    row_spec = lambda width: pl.BlockSpec((1, rows, width), lambda b, *_: (b, 0, 0))
    late_spec = lambda width: pl.BlockSpec((1, rows, width), lambda b, *_: (first + b, 0, 0))
    head_spec = pl.BlockSpec((1, HEADS, rows, total), lambda b, *_: (b, 0, 0, 0))
    late_head = pl.BlockSpec((1, HEADS, rows, total), lambda b, *_: (first + b, 0, 0, 0))
    more = ([] if dlogits is None else [dlogits]) + list(deps)
    outs = pl.pallas_call(
        functools.partial(attend_back_kernel, blocks),
        grid_spec=pltpu.PrefetchScalarGridSpec(
            num_scalar_prefetch=1,
            grid=(seqs,),
            in_specs=[row_spec(D)]
            + kv_specs(blocks, rows)
            + [head_spec, late_spec(D)]
            + [ANY] * len(more),
            out_specs=[late_head, row_spec(D)] + [row_spec(2 * D)] * blocks,
            scratch_shapes=[pltpu.VMEM((total, 2 * D), BF), pltpu.VMEM((total, 2 * D), BF)],
        ),
        out_shape=[
            jax.ShapeDtypeStruct((seqs_all, HEADS, rows, total), BF),
            jax.ShapeDtypeStruct(queries.shape, BF),
        ]
        + [jax.ShapeDtypeStruct((seqs, rows, 2 * D), BF)] * blocks,
        input_output_aliases={} if dlogits is None else {blocks + 4: 0},
        compiler_params=pltpu.CompilerParams(vmem_limit_bytes=GRANT),
        cost_estimate=pl.CostEstimate(
            flops=8 * seqs * HEADS * rows * total * PAIR,
            bytes_accessed=4 * seqs * HEADS * rows * total,
            transcendentals=0,
        ),
    )(order, queries, *[keys_values] * blocks, probs, dctx, *more)
    dkv = [b.reshape(seqs * rows, 2 * D) for b in outs[2:]]
    return outs[0], outs[1].reshape(seqs * rows, D), dkv


def gelu_and_slope(values):
    size = jnp.abs(values)
    bell = jnp.exp(values * values * -0.5)
    t = 1.0 / (1.0 + (0.3275911 * 0.7071067811865476) * size)
    tail = (0.5 * 1.061405429) * t + (0.5 * -1.453152027)
    tail = tail * t + (0.5 * 1.421413741)
    tail = tail * t + (0.5 * -0.284496736)
    tail = tail * t + (0.5 * 0.254829592)
    tail = tail * t * bell
    cdf = jnp.where(values >= 0.0, 1.0 - tail, tail)
    return values * cdf, cdf + values * bell * 0.3989422804014327


def norm(values):
    average = jnp.mean(values, -1, keepdims=True)
    centred = values - average
    inverse = lax.rsqrt(jnp.mean(centred * centred, -1, keepdims=True) + 1e-06)
    return centred * inverse, inverse


def norm_back(grad, normed, inverse):
    first = jnp.mean(grad, -1, keepdims=True)
    second = jnp.mean(grad * normed, -1, keepdims=True)
    return inverse * (grad - first - normed * second)


def load_middle(table_ref, in_refs, down_refs, w_out_ref, w_in_ref, w_down_ref, stage, sems):
    if len(in_refs) == 1:
        pltpu.make_async_copy(in_refs[0], w_in_ref, sems.at[1]).start()
        pltpu.make_async_copy(down_refs[0], w_down_ref, sems.at[2]).start()
        pltpu.make_async_copy(down_refs[1], w_out_ref, sems.at[0]).start()
        wait_whole(w_out_ref, sems.at[0])
    else:
        down = w_down_ref.shape[0] // 4
        wide = w_down_ref.shape[1] // 8
        high, half = D // 8, D // 16
        for piece, dp, seq in pieces_of(down_refs, table_ref):
            pltpu.make_async_copy(
                piece.at[pl.ds(down, half)], stage.at[seq, dp], sems.at[0]
            ).start()
        for piece, dp, seq in pieces_of(in_refs, table_ref):
            rows = pl.ds(pl.multiple_of(dp * high, high), high)
            cols = pl.ds(pl.multiple_of(seq * D, D), D)
            pltpu.make_async_copy(piece, w_in_ref.at[rows, cols], sems.at[1]).start()
        for piece, dp, seq in pieces_of(down_refs, table_ref):
            rows = pl.ds(pl.multiple_of(seq * down, down), down)
            cols = pl.ds(pl.multiple_of(dp * wide, wide), wide)
            pltpu.make_async_copy(
                piece.at[pl.ds(0, down)], w_down_ref.at[rows, cols], sems.at[2]
            ).start()
        wait_whole(stage, sems.at[0])
        for s in range(4):
            for d in range(8):
                cols = slice(s * down, (s + 1) * down)
                w_out_ref[d * high : d * high + half, cols] = stage[s, d][:, :down]
                w_out_ref[d * high + half : (d + 1) * high, cols] = stage[s, d][:, down:]


def middle_kernel(
    counts, table_ref, x_ref, ctx_a_ref, ctx_b_ref, cot_ref, vec_ref, b_in_ref, *refs
):
    in_refs, refs = refs[: counts[0]], refs[counts[0] :]
    down_refs, refs = refs[: counts[1]], refs[counts[1] :]
    (
        out_ref, dh1_ref, dctx_ref, act_ref, dinner_ref, dbranch_ref, y1_ref, dattn_ref,
        dvec_ref, db_in_ref, w_out_ref, w_in_ref, w_down_ref, stage, sems,
    ) = refs

    @pl.when(pl.program_id(0) == 0)
    def _():
        load_middle(
            table_ref, in_refs, down_refs, w_out_ref, w_in_ref, w_down_ref, stage, sems
        )
        dvec_ref[...] = jnp.zeros_like(dvec_ref)
        db_in_ref[...] = jnp.zeros_like(db_in_ref)

    vec = lambda i: vec_ref[i : i + 1, :].astype(F32)
    total = lambda v: jnp.sum(v, 0, keepdims=True)
    early = pl.program_id(0) < pl.num_programs(0) // 2
    ctx = jnp.where(early, ctx_a_ref[...], ctx_b_ref[...])
    h1 = x_ref[...].astype(F32) + (mm(ctx, w_out_ref[...]) + vec(2))
    normed1, inverse1 = norm(h1)
    y1 = normed1 * vec(3) + vec(4)
    y1_low = y1.astype(BF)
    y1_ref[...] = y1_low

    @pl.when(pl.program_id(0) == 0)
    def _():
        wait_whole(w_in_ref, sems.at[1])

    inner = mm(y1_low, w_in_ref[...]) + b_in_ref[...].astype(F32)
    act, slope = gelu_and_slope(inner)
    act = act.astype(BF)
    act_ref[...] = act

    @pl.when(pl.program_id(0) == 0)
    def _():
        wait_whole(w_down_ref, sems.at[2])

    h2 = y1 + (mm_nt(act, w_down_ref[...]) + vec(5))
    normed2, inverse2 = norm(h2)
    out_ref[...] = (normed2 * vec(6) + vec(7)).astype(BF)
    cot = cot_ref[...].astype(F32)
    dh2 = norm_back(cot * vec(6), normed2, inverse2)
    dbranch = dh2.astype(BF)
    dbranch_ref[...] = dbranch
    dinner = (mm(dbranch, w_down_ref[...]) * slope).astype(BF)
    dinner_ref[...] = dinner
    dy1 = dh2 + mm_nt(dinner, w_in_ref[...])
    dh1 = norm_back(dy1 * vec(3), normed1, inverse1)
    dh1_ref[...] = dh1
    dattn = dh1.astype(BF)
    dattn_ref[...] = dattn
    dctx_ref[...] = mm_nt(dattn, w_out_ref[...]).astype(BF)
    db_in_ref[...] += total(dinner.astype(F32))
    dvec_ref[2:3, :] += total(dattn.astype(F32))
    dvec_ref[3:4, :] += total(dy1 * normed1)
    dvec_ref[4:5, :] += total(dy1)
    dvec_ref[5:6, :] += total(dbranch.astype(F32))
    dvec_ref[6:7, :] += total(cot * normed2)
    dvec_ref[7:8, :] += total(cot)


def middle(table, x, ctx_a, ctx_b, cot, vectors, b_in, in_pieces, down_pieces):
    tokens = x.shape[0]
    ff = b_in.shape[1]
    step = 256
    half = tokens // step // 2
    rows = lambda width: pl.BlockSpec((step, width), lambda i, *_: (i, 0))
    ctx_specs = [
        pl.BlockSpec((step, D), lambda i, *_: (jnp.minimum(i, half - 1), 0)),
        pl.BlockSpec((step, D), lambda i, *_: (jnp.maximum(i - half, 0), 0)),
    ]
    whole = lambda a: pl.BlockSpec(a.shape, lambda i, *_: (0, 0))
    fixed = lambda *shape: pl.BlockSpec(shape, lambda i, *_: (0, 0))
    sds = jax.ShapeDtypeStruct
    counts = (len(in_pieces), len(down_pieces))
    return pl.pallas_call(
        functools.partial(middle_kernel, counts),
        grid_spec=pltpu.PrefetchScalarGridSpec(
            num_scalar_prefetch=1,
            grid=(tokens // step,),
            in_specs=[rows(D)]
            + ctx_specs
            + [rows(D)]
            + [whole(vectors), whole(b_in)]
            + [pl.BlockSpec(memory_space=pl.ANY)] * sum(counts),
            out_specs=[rows(D)] * 3
            + [rows(ff)] * 2
            + [rows(D)] * 3
            + [fixed(8, D), fixed(1, ff)],
            scratch_shapes=[
                pltpu.VMEM((D, D), BF),
                pltpu.VMEM((D, ff), BF),
                pltpu.VMEM((D, ff), BF),
                pltpu.VMEM((4, 8, D // 16, ff // 8), BF),
                pltpu.SemaphoreType.DMA((3,)),
            ],
        ),
        out_shape=[
            sds((tokens, D), BF),
            sds((tokens, D), F32),
            sds((tokens, D), BF),
            sds((tokens, ff), BF),
            sds((tokens, ff), BF),
            sds((tokens, D), BF),
            sds((tokens, D), BF),
            sds((tokens, D), BF),
            sds((8, D), F32),
            sds((1, ff), F32),
        ],
        compiler_params=pltpu.CompilerParams(vmem_limit_bytes=GRANT),
        cost_estimate=pl.CostEstimate(
            flops=tokens * (8 * D * ff + 4 * D * D),
            bytes_accessed=40 * MIB,
            transcendentals=2 * tokens * ff,
        ),
    )(table, x, ctx_a, ctx_b, cot, vectors, b_in, *in_pieces, *down_pieces)


def grad_in_kernel(where_ref, y1_ref, dinner_ref, *refs):
    send_ref, keep_ref = refs[-2:]
    z, y = where_ref[0], where_ref[1]
    step = pl.program_id(0)
    high = D // 8
    grad = mm_tn(y1_ref[...], dinner_ref[...]).astype(BF)
    for d in range(8):
        rows = grad[d * high : (d + 1) * high]
        far_y, far_z = y ^ (d & 1), (d >> 1) ^ z

        @pl.when(step < 2)
        def _():
            send_ref[0, far_y, far_z] = rows

        @pl.when(step >= 2)
        def _():
            keep_ref[0, far_y, far_z] = rows


def grad_in(where, y1, dinner, deps=()):
    tokens, ff = dinner.shape
    wide = ff // 4

    def columns(t, where):
        return (0, 2 * (where[2] ^ (t & 1)) + (where[3] ^ (1 - (t >> 1))))

    piece = (1, 2, 4, D // 8, wide)
    shape = jax.ShapeDtypeStruct((2, 2, 4, D // 8, wide), BF)
    return pl.pallas_call(
        grad_in_kernel,
        grid_spec=pltpu.PrefetchScalarGridSpec(
            num_scalar_prefetch=1,
            grid=(4,),
            in_specs=[
                pl.BlockSpec((tokens, D), lambda t, w: (0, 0)),
                pl.BlockSpec((tokens, wide), columns),
            ]
            + [ANY] * len(deps),
            out_specs=[
                pl.BlockSpec(piece, lambda t, w: (jnp.minimum(t, 1), 0, 0, 0, 0)),
                pl.BlockSpec(piece, lambda t, w: (jnp.maximum(t - 2, 0), 0, 0, 0, 0)),
            ],
        ),
        out_shape=[shape, shape],
        compiler_params=pltpu.CompilerParams(vmem_limit_bytes=GRANT),
        cost_estimate=pl.CostEstimate(
            flops=2 * tokens * D * ff, bytes_accessed=14 * MIB, transcendentals=0
        ),
    )(where, y1, dinner, *deps)


def grad_down_kernel(
    where_ref, dbranch_ref, act_ref, ctx_a_ref, ctx_b_ref, dattn_ref, send_ref, keep_ref, grad_out
):
    y, x, core = where_ref[1], where_ref[2], where_ref[3]
    step = pl.program_id(0)
    wide, down = D // 2, D // 4
    high, half = D // 8, D // 16

    @pl.when(step == 0)
    def _():
        part = ctx_a_ref.shape[0]
        grad_out[...] = mm_tn(ctx_a_ref[...], dattn_ref[:part]) + mm_tn(
            ctx_b_ref[...], dattn_ref[part:]
        )

    def put(far_y, far_x, rows, cols, even, odd):
        first = core == 0
        keep_ref[far_y, far_x, 0, rows, cols] = jnp.where(first, even, odd).astype(BF)
        send_ref[far_y, far_x, 0, rows, cols] = jnp.where(first, odd, even).astype(BF)

    grad = mm_tn(dbranch_ref[...], act_ref[...])
    for j in range(2):
        top = pl.multiple_of((2 * step + j) * high, high)
        upper, lower = grad_out[pl.ds(top, half), :], grad_out[pl.ds(top + half, half), :]
        for i in range(2):
            pair = [slice((2 * i + k) * down, (2 * i + k + 1) * down) for k in range(2)]
            side = slice(j * wide, (j + 1) * wide)
            far = (y ^ j, x ^ i)
            put(*far, slice(0, down), slice(None), grad[pair[0], side], grad[pair[1], side])
            tail = slice(down, down + half)
            put(*far, tail, slice(0, down), upper[:, pair[0]], upper[:, pair[1]])
            put(*far, tail, slice(down, 2 * down), lower[:, pair[0]], lower[:, pair[1]])


def grad_down(where, dbranch, act, ctx_a, ctx_b, dattn):
    tokens, ff = act.shape
    wide = ff // 4
    whole = pl.BlockSpec((tokens, D), lambda t, w: (0, 0))
    half = pl.BlockSpec((tokens // 2, D), lambda t, w: (0, 0))
    piece = (D // 4 + D // 16, ff // 8)
    spec = pl.BlockSpec((2, 2, 1) + piece, lambda t, w: (0, 0, t ^ w[0], 0, 0))
    shape = jax.ShapeDtypeStruct((2, 2, 4) + piece, BF)
    return pl.pallas_call(
        grad_down_kernel,
        grid_spec=pltpu.PrefetchScalarGridSpec(
            num_scalar_prefetch=1,
            grid=(4,),
            in_specs=[
                whole,
                pl.BlockSpec((tokens, wide), lambda t, w: (0, t)),
                half,
                half,
                whole,
            ],
            out_specs=[spec, spec],
            scratch_shapes=[pltpu.VMEM((D, D), F32)],
        ),
        out_shape=[shape, shape],
        compiler_params=pltpu.CompilerParams(vmem_limit_bytes=GRANT),
        cost_estimate=pl.CostEstimate(
            flops=2 * tokens * D * (ff + D), bytes_accessed=20 * MIB, transcendentals=0
        ),
    )(where, dbranch, act, ctx_a, ctx_b, dattn)


def grad_qkv_kernel(where_ref, x0_ref, *refs):
    x2_refs, refs = refs[:2], refs[2:]
    dq_refs, refs = refs[:2], refs[2:]
    own_refs, refs = refs[:4], refs[4:]
    far_refs, refs = refs[:4], refs[4:]
    dvec_ref, db_ref = refs[:2]
    send_ref, keep_ref, grad, dvec = refs[-4:]
    z, y, x, core = (where_ref[i] for i in range(4))
    step = pl.program_id(0)
    wide, high = 3 * D // 4, D // 8
    part = x2_refs[0].shape[0]
    x0 = lambda h: x0_ref[h * part : (h + 1) * part]

    @pl.when(step == 0)
    def _():
        grad[:, :D] = mm_tn(x0(0), dq_refs[0][...]) + mm_tn(x0(1), dq_refs[1][...])
        dvec[...] = dvec_ref[...]
        for ref in dq_refs:
            dvec[0:1, :] += jnp.sum(ref[...].astype(F32), 0, keepdims=True)

    for t in (1, 2):

        @pl.when(step == t)
        def _():
            total = None
            for h in range(2):
                own, far = (
                    low(add(refs[h][...], refs[2 + h][...])) for refs in (own_refs, far_refs)
                )
                if t == 2:
                    both = jnp.sum(own.astype(F32), 0, keepdims=True)
                    dvec[1:2, :] += both + jnp.sum(far.astype(F32), 0, keepdims=True)
                piece = mm_tn(x0(h), own) + mm_tn(x2_refs[h][...], far)
                total = piece if total is None else total + piece
            grad[:, t * D : (t + 1) * D] = total

    @pl.when(step == 2)
    def _():
        first = core == 0
        for i in range(2):
            even = grad[:, 2 * i * wide : (2 * i + 1) * wide]
            odd = grad[:, (2 * i + 1) * wide : (2 * i + 2) * wide]
            kept = jnp.where(first, even, odd).astype(BF)
            sent = jnp.where(first, odd, even).astype(BF)
            for d in range(8):
                rows = slice(d * high, (d + 1) * high)
                far = (y ^ (d & 1), x ^ i, (d >> 1) ^ z)
                keep_ref[far + (slice(0, high), slice(None))] = kept[rows]
                send_ref[far + (slice(0, high), slice(None))] = sent[rows]
                extra = []
                for k in range(2):
                    s = 2 * i + k
                    own = dvec[2 * s : 2 * s + 2, d * high : (d + 1) * high]
                    at = (4 * d + s) * high
                    rest = jnp.zeros((PAD - 3, high), F32)
                    extra.append(jnp.concatenate([own, db_ref[0:1, at : at + high], rest], 0))
                tail = far + (slice(high, high + PAD), slice(0, high))
                keep_ref[tail] = jnp.where(first, extra[0], extra[1]).astype(BF)
                send_ref[tail] = jnp.where(first, extra[1], extra[0]).astype(BF)


def grad_qkv(where, x0, x2, dq, own, far, dvec, db_in, deps=()):
    tokens = x0.shape[0]
    fixed = lambda *shape: pl.BlockSpec(shape, lambda t, w: (0, 0))
    half = fixed(tokens // 2, D)
    part = pl.BlockSpec((tokens // 2, D), lambda t, w: (0, jnp.maximum(t - 1, 0)))
    dims = (2, 2, 4, D // 8 + PAD, 3 * D // 4)
    spec = pl.BlockSpec(dims, lambda t, w: (0, 0, 0, 0, 0))
    shape = jax.ShapeDtypeStruct(dims, BF)
    return pl.pallas_call(
        grad_qkv_kernel,
        grid_spec=pltpu.PrefetchScalarGridSpec(
            num_scalar_prefetch=1,
            grid=(3,),
            in_specs=[fixed(tokens, D)]
            + [half] * 4
            + [part] * 8
            + [fixed(8, D)]
            + [fixed(*db_in.shape)]
            + [ANY] * len(deps),
            out_specs=[spec, spec],
            scratch_shapes=[pltpu.VMEM((D, 3 * D), F32), pltpu.VMEM((8, D), F32)],
        ),
        out_shape=[shape, shape],
        compiler_params=pltpu.CompilerParams(vmem_limit_bytes=GRANT),
        cost_estimate=pl.CostEstimate(
            flops=2 * tokens * D * 5 * D, bytes_accessed=16 * MIB, transcendentals=0
        ),
    )(where, x0, *x2, *dq, *own, *far, dvec, db_in, *deps)


def grad_far_kernel(dkv_ref, got_ref, w_ref, *refs):
    total = low(add(dkv_ref[...], got_ref[...]))
    refs[-1][...] = mm_nt(total, w_ref[:, D:]).astype(BF)


def grad_far(dkv, got, w_qkv, deps=()):
    tokens = dkv.shape[0]
    step = 256
    rows = lambda width: pl.BlockSpec((step, width), lambda i: (i, 0))
    return pl.pallas_call(
        grad_far_kernel,
        grid=(tokens // step,),
        in_specs=[
            rows(2 * D),
            rows(2 * D),
            pl.BlockSpec((D, 3 * D), lambda i: (0, 0), pipeline_mode=pl.Buffered(1)),
        ]
        + [ANY] * len(deps),
        out_specs=rows(D),
        out_shape=jax.ShapeDtypeStruct((tokens, D), BF),
        compiler_params=pltpu.CompilerParams(vmem_limit_bytes=GRANT),
        cost_estimate=pl.CostEstimate(
            flops=2 * tokens * D * 2 * D, bytes_accessed=10 * MIB, transcendentals=0
        ),
    )(dkv, got, w_qkv, *deps)


def grad_own_kernel(*refs):
    dkv_refs, refs = refs[:2], refs[2:]
    got_refs, refs = refs[:2], refs[2:]
    dq_refs, refs = refs[:2], refs[2:]
    dh1_ref, w_ref = refs[:2]
    dx_ref = refs[-1]
    early = pl.program_id(0) < pl.num_programs(0) // 2
    pick = lambda pair: jnp.where(early, pair[0][...], pair[1][...])
    total = (pick(dkv_refs).astype(F32) + pick(got_refs).astype(F32)).astype(BF)
    dx = mm_nt(total, w_ref[:, D:]) + mm_nt(pick(dq_refs), w_ref[:, :D])
    dx_ref[...] = dx + dh1_ref[...]


def grad_own(dkv, got, dq, dh1, w_qkv, deps=()):
    tokens = dh1.shape[0]
    step = 256
    half = tokens // step // 2

    def pair(width):
        return [
            pl.BlockSpec((step, width), lambda i: (jnp.minimum(i, half - 1), 0)),
            pl.BlockSpec((step, width), lambda i: (jnp.maximum(i - half, 0), 0)),
        ]

    rows = pl.BlockSpec((step, D), lambda i: (i, 0))
    return pl.pallas_call(
        grad_own_kernel,
        grid=(tokens // step,),
        in_specs=pair(2 * D)
        + pair(2 * D)
        + pair(D)
        + [rows, pl.BlockSpec((D, 3 * D), lambda i: (0, 0), pipeline_mode=pl.Buffered(1))]
        + [ANY] * len(deps),
        out_specs=rows,
        out_shape=jax.ShapeDtypeStruct((tokens, D), F32),
        compiler_params=pltpu.CompilerParams(vmem_limit_bytes=GRANT),
        cost_estimate=pl.CostEstimate(
            flops=2 * tokens * D * 3 * D, bytes_accessed=20 * MIB, transcendentals=0
        ),
    )(*dkv, *got, *dq, dh1, w_qkv, *deps)


def gather_small(b_in, vectors):
    dp, seq = lax.axis_size("dp"), lax.axis_size("seq")
    small = jnp.concatenate([vectors.reshape(-1), b_in])
    whole = lax.all_gather(small, BOTH, axis=0, tiled=False)
    nv = vectors.size
    vec = whole[:, :nv].reshape((dp, seq) + vectors.shape).transpose(1, 2, 0, 3)
    return whole[:, nv:].reshape(1, -1), vec.reshape(8, D)


def reduce_small(g_b, g_vec):
    dp, seq = lax.axis_size("dp"), lax.axis_size("seq")
    vec = g_vec.reshape(seq, 8 // seq, dp, D // dp).transpose(2, 0, 1, 3)
    small = jnp.concatenate([vec.reshape(dp * seq, -1), g_b.reshape(dp * seq, -1)], 1)
    mine = lax.psum_scatter(small, BOTH, scatter_dimension=0, tiled=True)[0]
    nv = 8 * D // (dp * seq)
    return mine[nv:], mine[:nv].reshape(8 // seq, D // dp)


def gather_plain(w_qkv, w_out, w_in, w_down_t):
    both = lambda a, first, second: lax.all_gather(
        lax.all_gather(a, first, axis=0, tiled=True), second, axis=1, tiled=True
    )
    return (
        [both(w_qkv, "dp", "seq")],
        [both(w_in, "dp", "seq")],
        [both(w_down_t, "seq", "dp"), both(w_out, "dp", "seq")],
    )


def reduce_plain(a, first, second):
    part = lax.psum_scatter(a.astype(BF), first, scatter_dimension=0, tiled=True)
    return lax.psum_scatter(part, second, scatter_dimension=1, tiled=True).astype(F32)


def together(*parts):
    return lax.optimization_barrier(parts)


def forward_apart(order, lengths, table, x0, prev_logits, shape, weights):
    w_qkv, w_out, w_in, w_down, b_in, vectors = weights
    seqs, rows = shape
    half, part = seqs // 2, seqs * rows // 2
    x2_a, x1 = swap_x(x0[:part]), swap_core(x0)
    small = jnp.concatenate([vectors, b_in.reshape(1, -1)], 0)
    small = jnp.pad(small, ((0, PAD - small.shape[0]), (0, w_qkv.shape[1] - small.shape[1])))
    qkv = stack_z_direct(jnp.concatenate([w_qkv, small], 0))
    cut = w_out.shape[0] // 2
    turned = jnp.concatenate([w_out[:cut], w_out[cut:]], 1)
    down = jnp.concatenate([w_down.T, turned], 0)
    x1, qkv, w_in, down, x_b = together(x1, qkv, w_in, down, x0[part:])

    qkv_x, qkv_y = swap_x(qkv), swap_y(qkv)
    in_pair = jnp.stack([w_in, swap_z(w_in, 1)])
    down_pair = jnp.stack([down, swap_z(down, 1)])
    qkv, qkv_x, qkv_y, x2_a, in_pair, down_pair, x_b = together(
        qkv, qkv_x, qkv_y, x2_a, in_pair, down_pair, x_b
    )

    qkv_xy, x2_b = swap_y(qkv_x), swap_x(x_b)
    x3_a, qkv_far = swap_core(x2_a), swap_core(qkv)
    in_got = swap_z(in_pair, 2)
    qkv_xy, x2_b, in_pair, in_got, down_pair, x3_a, qkv_far = together(
        qkv_xy, x2_b, in_pair, in_got, down_pair, x3_a, qkv_far
    )
    in_own = jnp.concatenate([in_pair, in_got], 0)
    qkv_near = [qkv, qkv_x, qkv_y, qkv_xy]
    qkv_pieces = qkv_near + [qkv_far] + [swap_core(a) for a in qkv_near[1:]]

    project_half = lambda h, x2, x3, pieces, vec: project(
        table, (x0, x1, x2, x3), (h * part, h * part, 0, 0), part, pieces, vec
    )

    def attend_half(h, made):
        queries = made[0].reshape(half, rows, D)
        keys_values = made[1].reshape(4, half, rows, 2 * D)
        ctx, probs = attend(order, lengths, queries, keys_values, prev_logits, h * half)
        return queries, keys_values, ctx.reshape(part, D), probs

    in_x, in_y, x3_b = swap_x(in_own), swap_y(in_own), swap_core(x2_b)
    down_got = swap_z(down_pair, 2)
    q_a, kv_a, f_qkv, f_vec, f_b = project_half(0, x2_a, x3_a, qkv_pieces, None)
    in_own, in_x, in_y, x3_b, down_pair, down_got, q_a, kv_a, f_qkv = together(
        in_own, in_x, in_y, x3_b, down_pair, down_got, q_a, kv_a, f_qkv
    )
    down_own = jnp.concatenate([down_pair, down_got], 0)

    down_x, down_y = swap_x(down_own), swap_y(down_own)
    in_far = [swap_core(a) for a in (in_own, in_x, in_y)]
    q_a, kv_a, ctx_a, probs_a = attend_half(0, (q_a, kv_a))
    down_own, down_x, down_y, in_x, x3_b, ctx_a, probs_a, *in_far = together(
        down_own, down_x, down_y, in_x, x3_b, ctx_a, probs_a, *in_far
    )

    in_xy, down_xy = swap_y(in_x), swap_x(down_y)
    down_far = [swap_core(a) for a in (down_own, down_x, down_y)]
    second = attend_half(1, project_half(1, x2_b, x3_b, [f_qkv], f_vec))
    in_xy, down_xy, ctx_b, probs_b, *down_far = together(
        in_xy, down_xy, second[2], second[3], *down_far
    )
    in_pieces = [in_own, in_x, in_y, in_xy] + in_far + [swap_core(in_xy)]
    down_pieces = [down_own, down_x, down_y, down_xy] + down_far + [swap_core(down_xy)]
    first, second = (q_a, kv_a, ctx_a, probs_a), (second[0], second[1], ctx_b, probs_b)
    return first, second, f_qkv, f_vec, f_b, in_pieces, down_pieces, [x2_a, x2_b]


def shards_apart(
    hidden_states, prev_logits, lengths, w_qkv, w_out, w_in, w_down, b_in, vectors, cotangent
):
    seqs, rows, _ = hidden_states.shape
    tokens = seqs * rows
    half = seqs // 2
    order = jnp.arange(4, dtype=jnp.int32) ^ lax.axis_index("seq")
    table, where = piece_table(), jnp.stack(place()).astype(jnp.int32)
    x0 = hidden_states.reshape(tokens, D)
    first, second, f_qkv, f_vec, f_b, in_pieces, down_pieces, x2 = forward_apart(
        order, lengths, table, x0, prev_logits, (seqs, rows),
        (w_qkv, w_out, w_in, w_down, b_in, vectors),
    )
    ctx = [first[2], second[2]]
    out, dh1, dctx, act, dinner, dbranch, y1, dattn, dvec, db_in = middle(
        table, x0, *ctx, cotangent.reshape(tokens, D), f_vec, f_b, in_pieces, down_pieces
    )
    dctx = dctx.reshape(seqs, rows, D)

    d_send, d_keep = grad_down(where, dbranch, act, *ctx, dattn)
    d_core = swap_core(d_send)
    i_send, i_keep = grad_in(where, y1, dinner, [d_keep])
    i_core = swap_core(i_send)
    d_core = after(d_core, i_keep)
    d_sent = low(add(d_keep[1], d_core[1]))
    d_one = swap_y(d_sent)
    i_core = after(i_core, d_sent)
    i_sent = low(add(i_keep[1], i_core[1]))
    i_one = swap_x(i_sent)
    dlogits, dq_a, dkv_a = attend_back(
        order, first[0], first[1], first[3], dctx, None, 0, seqs, [d_sent, i_sent]
    )
    far_a, own_a = swap_core(dkv_a[3]), swap_core(dkv_a[1])
    dlogits, dq_b, dkv_b = attend_back(
        order, second[0], second[1], second[3], dctx, dlogits, half, seqs, [dq_a]
    )
    far_b, own_b = swap_core(dkv_b[3]), swap_core(dkv_b[1])
    far_a, own_a = after(far_a, dq_b), after(own_a, dq_b)
    d_one, i_one = after(d_one, dq_b), after(i_one, dq_b)
    d_sent = low(add(d_keep[0, 1], d_core[0, 1], d_one[1]))
    d_two = swap_x(d_sent)
    i_sent = low(add(i_keep[0, 1], i_core[0, 1], i_one[1]))
    i_two = swap_y(i_sent)
    dq, own, far = [dq_a, dq_b], [dkv_a[0], dkv_b[0], own_a, own_b], [dkv_a[2], dkv_b[2], far_a, far_b]
    q_send, q_keep = grad_qkv(where, x0, x2, dq, own, far, dvec, db_in, [d_sent, i_sent])
    d_two, i_two, q_send, q_keep = together(d_two, i_two, q_send, q_keep)
    q_core = swap_core(q_send)
    d_part = lambda k: add(d_keep[0, 0, k], d_core[0, 0, k], d_one[0, k], d_two[k])
    i_part = lambda k: add(i_keep[0, 0, k], i_core[0, 0, k], i_one[0, k], i_two[k])
    upper, lower = slice(2, 4), slice(0, 2)
    d_sent, i_sent = low(d_part(upper)), low(i_part(upper))
    i_far, d_far = swap_z(i_sent, 2), swap_z(d_sent, 2)
    q_core = after(q_core, d_sent, i_sent)
    q_sent = low(add(q_keep[1], q_core[1]))
    q_one = swap_y(q_sent)
    dx2_a = grad_far(far[0], far[2], f_qkv, [q_sent])
    got_a = swap_x(dx2_a)
    dx2_b = grad_far(far[1], far[3], f_qkv, [dx2_a])
    dx = grad_own(own[:2], own[2:], dq, dh1, f_qkv, [dx2_b])
    q_one, dx, got_a, dx2_b = together(q_one, dx, got_a, dx2_b)
    q_sent = low(add(q_keep[0, 1], q_core[0, 1], q_one[1]))
    q_two = swap_x(q_sent)
    i_far, d_far = after(i_far, q_sent), after(d_far, q_sent)
    d_last = d_part(lower) + d_far.astype(F32)
    i_last = i_part(lower) + i_far.astype(F32)
    d_end, i_end = swap_z(low(d_last[1]), 1), swap_z(low(i_last[1]), 1)
    q_two, d_end, i_end, d_last, i_last, dx2_b = together(
        q_two, d_end, i_end, d_last, i_last, dx2_b
    )
    got_b = swap_x(dx2_b)
    q_part = lambda k: add(q_keep[0, 0, k], q_core[0, 0, k], q_one[0, k], q_two[k])
    q_sent = [low(q_part(k)) for k in range(1, 4)]
    q_far = [swap_z(q, k) for q, k in zip(q_sent, range(1, 4))]
    o_low, o_in = d_last[0] + d_end.astype(F32), i_last[0] + i_end.astype(F32)
    o_low, o_in, got_a, got_b = after((o_low, o_in, got_a, got_b), *q_sent)
    o_top = q_part(0) + add(*q_far)
    grad_hidden = low(dx + jnp.concatenate([got_a, got_b], 0).astype(F32))
    down, cut, (extra, high) = w_down.shape[1], w_qkv.shape[0], vectors.shape
    shape = hidden_states.shape
    return (
        out.reshape(shape),
        grad_hidden.reshape(shape),
        dlogits,
        o_top[:cut],
        jnp.concatenate([o_low[down:, :down], o_low[down:, down:]], 0),
        o_in,
        o_low[:down].T,
        o_top[cut + extra, : b_in.shape[0]],
        o_top[cut : cut + extra, :high],
    )


def shards_plain(
    hidden_states, prev_logits, lengths, w_qkv, w_out, w_in, w_down, b_in, vectors, cotangent
):
    seqs, rows, _ = hidden_states.shape
    tokens = seqs * rows
    seq = lax.axis_size("seq")
    order = jnp.arange(seq, dtype=jnp.int32) ^ lax.axis_index("seq")
    half, part = seqs // 2, tokens // 2
    x0 = hidden_states.reshape(tokens, D)
    x1, x2 = swap_core(x0), swap_x(x0)
    x3 = swap_core(x2)
    table = jnp.zeros((2,), jnp.int32)
    qkv, in_pieces, down_pieces = gather_plain(w_qkv, w_out, w_in, w_down.T)
    f_qkv = qkv[0]
    f_b, f_vec = gather_small(b_in, vectors)
    f_b, f_vec = f_b.astype(F32), f_vec.astype(F32)
    queries, keys_values, ctx, probs = [], [], [], []
    for h in range(2):
        made = project(table, (x0, x1, x2, x3), (h * part,) * 4, part, qkv, f_vec)
        queries.append(made[0].reshape(half, rows, D))
        keys_values.append(made[1].reshape(seq, half, rows, 2 * D))
        mixed = attend(order, lengths, queries[h], keys_values[h], prev_logits, h * half)
        ctx.append(mixed[0].reshape(part, D))
        probs.append(mixed[1])
    out, dh1, dctx, act, dinner, dbranch, y1, dattn, dvec, db_in = middle(
        table, x0, *ctx, cotangent.reshape(tokens, D), f_vec, f_b, in_pieces, down_pieces
    )
    dctx = dctx.reshape(seqs, rows, D)
    dlogits, dq, dkv = None, [], []
    for h in range(2):
        dlogits, dq_h, dkv_h = attend_back(
            order, queries[h], keys_values[h], probs[h], dctx, dlogits, h * half, seqs
        )
        dq.append(dq_h)
        dkv.append(dkv_h)
    got_far = [swap_core(dkv[h][3]) for h in range(2)]
    far = [grad_far(dkv[h][2], got_far[h], f_qkv) for h in range(2)]
    got_rows = [swap_x(f) for f in far]
    got_kv = [swap_core(dkv[h][1]) for h in range(2)]
    dkv0 = [dkv[h][0] for h in range(2)]
    dx = grad_own(dkv0, got_kv, dq, dh1, f_qkv)
    whole = lambda pair: jnp.concatenate(pair, 0)
    grad_hidden = low(dx + whole(got_rows).astype(F32))
    sum0 = whole([low(add(a, b)) for a, b in zip(dkv0, got_kv)])
    sum2 = whole([low(add(dkv[h][2], got_far[h])) for h in range(2)])
    dq = whole(dq)
    g_kv = mm_tn(x0, sum0) + mm_tn(x2, sum2)
    g_qkv = jnp.concatenate([mm_tn(x0, dq), g_kv], 1)
    dvec = dvec.at[0].add(jnp.sum(dq, 0, dtype=F32))
    dvec = dvec.at[1].add(jnp.sum(add(sum0[:, D:], sum2[:, D:]), 0))
    o_b, o_vec = reduce_small(db_in, dvec)
    shape = hidden_states.shape
    return (
        out.reshape(shape),
        grad_hidden.reshape(shape),
        dlogits,
        reduce_plain(g_qkv, "dp", "seq"),
        reduce_plain(mm_tn(whole(ctx), dattn), "dp", "seq"),
        reduce_plain(mm_tn(y1, dinner), "dp", "seq"),
        reduce_plain(mm_tn(act, dbranch), "dp", "seq"),
        o_b,
        o_vec,
    )


def shards(*args):
    return (shards_apart if by_pieces() else shards_plain)(*args)


def solution(mesh):
    return jax.shard_map(
        shards,
        mesh=mesh,
        in_specs=(
            P("dp", "seq", None),
            P("dp", None, "seq", None),
            P("dp"),
            P("dp", "seq"),
            P("dp", "seq"),
            P("dp", "seq"),
            P("dp", "seq"),
            P(("dp", "seq")),
            P("seq", "dp"),
            P("dp", "seq", None),
        ),
        out_specs=(
            P("dp", "seq", None),
            P("dp", "seq", None),
            P("dp", None, "seq", None),
            P("dp", "seq"),
            P("dp", "seq"),
            P("dp", "seq"),
            P("dp", "seq"),
            P(("dp", "seq")),
            P("seq", "dp"),
        ),
        check_vma=False,
    )
```

```python
import functools

import jax
import jax.numpy as jnp
from jax import lax
from jax.experimental import pallas as pl
from jax.experimental.pallas import tpu as pltpu
from jax.sharding import PartitionSpec as P

D = 768
HEADS = 12
HEAD_DIM = 64
PAIRS = HEADS // 2
PAIR = 2 * HEAD_DIM
SCALE = HEAD_DIM ** (-0.5)
BF = jnp.bfloat16
F32 = jnp.float32
BOTH = ("dp", "seq")
MIB = 1 << 20
PAD = 16
SUB = 256
ANY = pl.BlockSpec(memory_space=pl.ANY)
GRANT = 60 * MIB


def mm(a, b):
    return lax.dot_general(a, b, (((1,), (0,)), ((), ())), preferred_element_type=F32)


def mm_nt(a, b):
    return lax.dot_general(a, b, (((1,), (1,)), ((), ())), preferred_element_type=F32)


def mm_tn(a, b):
    return lax.dot_general(a, b, (((0,), (0,)), ((), ())), preferred_element_type=F32)


def stack_heads(pair):
    lane = lax.broadcasted_iota(jnp.int32, pair.shape, 1)
    zero = jnp.zeros_like(pair)
    return jnp.concatenate(
        [jnp.where(lane < HEAD_DIM, pair, zero), jnp.where(lane < HEAD_DIM, zero, pair)], 0
    )


def pick_heads(stacked):
    rows = stacked.shape[0] // 2
    lane = lax.broadcasted_iota(jnp.int32, (rows, PAIR), 1)
    return jnp.where(lane < HEAD_DIM, stacked[:rows], stacked[rows:])


def swap(a, axis, bit):
    size = lax.axis_size(axis)
    return lax.ppermute(a, axis, [(i, i ^ bit) for i in range(size)])


def swap_core(a):
    return swap(a, "seq", 1)


def swap_x(a):
    return swap(a, "seq", 2)


def swap_y(a):
    return swap(a, "dp", 1)


def swap_z(a, places):
    return swap(a, "dp", 2 * places)


def by_pieces():
    return lax.axis_size("dp") == 8 and lax.axis_size("seq") == 4


def place():
    dp, seq = lax.axis_index("dp"), lax.axis_index("seq")
    return dp >> 1, dp & 1, seq >> 1, seq & 1


def stack_z(a):
    pair = jnp.stack([a, swap_z(a, 1)])
    return jnp.concatenate([pair, swap_z(pair, 2)], 0)


def stack_z_direct(a):
    return jnp.stack([a] + [swap_z(a, k) for k in range(1, 4)])


def spread(own, own_x, own_y, own_xy):
    half = [own, own_x, own_y, own_xy]
    return half + [swap_core(b) for b in half]


def piece_table():
    z, y, x, core = place()
    table = []
    for far in range(8):
        for k in range(4):
            table.append(2 * (z ^ k) + (y ^ (far >> 1 & 1)))
            table.append(2 * (x ^ (far & 1)) + (core ^ (far >> 2)))
    return jnp.stack(table).astype(jnp.int32)


def pieces_of(refs, table_ref):
    for a, ref in enumerate(refs):
        depth = ref.shape[0]
        for k in range(depth):
            n = a * depth + k
            yield ref.at[k], table_ref[2 * n], table_ref[2 * n + 1]


def wait_whole(ref, sem):
    pltpu.make_async_copy(ref, ref, sem).wait()


def add(*parts):
    return sum(p.astype(F32) for p in parts)


def low(a):
    return a.astype(BF)


def after(a, *done):
    return lax.optimization_barrier((a,) + done)[0]


def load_qkv(table_ref, piece_refs, w_all, vec_ref, b_ref, stage, sems):
    high, wide = D // 8 + PAD, 3 * D // 4
    for piece, dp, seq in pieces_of(piece_refs, table_ref):
        rows = pl.ds(pl.multiple_of(dp * high, PAD), high)
        pltpu.make_async_copy(piece, stage.at[seq, rows], sems.at[0]).start()
    wait_whole(stage, sems.at[0])
    body, width = D // 8, D // 8
    for s in range(4):
        for d in range(8):
            top = d * high
            w_all[d * body : (d + 1) * body, s * wide : (s + 1) * wide] = stage[
                s, top : top + body
            ]
            extra = stage[s, top + body : top + high, :width].astype(F32)
            vec_ref[2 * s : 2 * s + 2, d * width : (d + 1) * width] = extra[0:2]
            place_of = (4 * d + s) * width
            b_ref[0:1, place_of : place_of + width] = extra[2:3]


def lead_kernel(count, assemble, first, table_ref, order_ref, len_ref, *refs):
    x_refs, refs = refs[:4], refs[4:]
    piece_refs, refs = refs[:count], refs[count:]
    if assemble:
        prev_ref, q_ref, kv_ref, ctx_ref, probs_ref, w_ref, vec_ref, b_ref = refs[:8]
    else:
        vec_ref, prev_ref, q_ref, kv_ref, ctx_ref, probs_ref = refs[:6]
    w_all, x_all, stage, sems = refs[-4:]
    rows, total = q_ref.shape[1], x_all.shape[0]

    @pl.when(pl.program_id(0) == 0)
    def _():
        if assemble:
            load_qkv(table_ref, piece_refs, w_all, vec_ref, b_ref, stage, sems)
            pltpu.make_async_copy(w_all, w_ref, sems.at[1]).start()
        else:
            pltpu.make_async_copy(piece_refs[0], w_all, sems.at[0]).start()
            wait_whole(w_all, sems.at[0])

    for j in range(4):
        start = pl.multiple_of(order_ref[j] * rows, rows)
        x_all[pl.ds(start, rows), :] = x_refs[j][0]
    valid = len_ref[first + pl.program_id(0)]
    key_pos = lax.broadcasted_iota(jnp.int32, (1, total), 1)
    padding = jnp.where(key_pos < valid, 0.0, -1e9)

    def project(g):
        width = 2 * PAIR
        cols = slice(g * width, (g + 1) * width)
        part = lambda n: slice(n * D + g * width, n * D + (g + 1) * width)
        query = (mm(x_refs[0][0], w_all[:, cols]) + vec_ref[0:1, cols]).astype(BF)
        q_ref[0, :, cols] = query * SCALE
        kv_ref[0, :, cols] = mm(x_all[...], w_all[:, part(1)]).astype(BF)
        value = mm(x_all[...], w_all[:, part(2)]) + vec_ref[1:2, cols]
        kv_ref[0, :, part(1)] = value.astype(BF)

    def score(i):
        cols = slice(i * PAIR, (i + 1) * PAIR)
        raw = mm_nt(stack_heads(q_ref[0, :, cols]), kv_ref[0, :, cols])
        prev = prev_ref[0, 2 * i : 2 * i + 2].reshape(2 * rows, total).astype(F32)
        return raw + (prev + padding)

    def mix(i, raw):
        cols = slice(i * PAIR, (i + 1) * PAIR)
        vcols = slice(D + i * PAIR, D + (i + 1) * PAIR)
        largest = jnp.max(raw, -1, keepdims=True)
        expo = jnp.exp(raw - largest)
        summed = jnp.sum(expo, -1, keepdims=True)
        probs = (expo * (1.0 / summed)).astype(BF)
        probs_ref[0, 2 * i : 2 * i + 2] = probs.reshape(2, rows, total)
        ctx_ref[0, :, cols] = pick_heads(mm(probs, kv_ref[0, :, vcols])).astype(BF)

    project(0)
    raw = score(0)
    for i in range(PAIRS):
        if i % 2 == 0 and i + 2 < PAIRS:
            project(i // 2 + 1)
        later = score(i + 1) if i + 1 < PAIRS else None
        mix(i, raw)
        raw = later

    if assemble:

        @pl.when(pl.program_id(0) == pl.num_programs(0) - 1)
        def _():
            pltpu.make_async_copy(w_all, w_ref, sems.at[1]).wait()


def lead(table, order, lengths, x_blocks, starts, seqs, first, pieces, prev_logits, vec=None):
    assemble = vec is None
    rows = x_blocks[0].shape[1]
    total = prev_logits.shape[-1]
    ff = 4 * D

    def x_spec(j):
        return pl.BlockSpec((1, rows, D), lambda b, *_: (starts[j] + b, 0, 0))

    fixed = lambda *shape: pl.BlockSpec(shape, lambda b, *_: (0, 0))
    row_spec = pl.BlockSpec((1, rows, D), lambda b, *_: (b, 0, 0))
    sds = jax.ShapeDtypeStruct
    out_specs = [
        row_spec,
        pl.BlockSpec((1, total, 2 * D), lambda b, *_: (b, 0, 0)),
        row_spec,
        pl.BlockSpec((1, HEADS, rows, total), lambda b, *_: (b, 0, 0, 0)),
    ]
    out_shape = [
        sds((seqs, rows, D), BF),
        sds((seqs, total, 2 * D), BF),
        sds((seqs, rows, D), BF),
        sds((seqs, HEADS, rows, total), BF),
    ]
    if assemble:
        out_specs += [ANY, fixed(8, D), fixed(1, ff)]
        out_shape += [sds((D, 3 * D), BF), sds((8, D), F32), sds((1, ff), F32)]
    stage = (4, 8 * (D // 8 + PAD), 3 * D // 4) if assemble else (1, PAD, 128)
    return pl.pallas_call(
        functools.partial(lead_kernel, len(pieces), assemble, first),
        grid_spec=pltpu.PrefetchScalarGridSpec(
            num_scalar_prefetch=3,
            grid=(seqs,),
            in_specs=[x_spec(j) for j in range(4)]
            + [ANY] * len(pieces)
            + ([] if assemble else [fixed(8, D)])
            + [
                pl.BlockSpec(
                    (1, HEADS, rows, total), lambda b, *_: (first + b, 0, 0, 0)
                )
            ],
            out_specs=out_specs,
            scratch_shapes=[
                pltpu.VMEM((D, 3 * D), BF),
                pltpu.VMEM((total, D), BF),
                pltpu.VMEM(stage, BF),
                pltpu.SemaphoreType.DMA((2,)),
            ],
        ),
        out_shape=out_shape,
        compiler_params=pltpu.CompilerParams(vmem_limit_bytes=GRANT),
        cost_estimate=pl.CostEstimate(
            flops=seqs * rows * D * (18 * D + 4 * total),
            bytes_accessed=seqs * 8 * MIB,
            transcendentals=seqs * HEADS * rows * total,
        ),
    )(table, order, lengths, *x_blocks, *pieces, *([] if assemble else [vec]), prev_logits)


def attend_back_kernel(order_ref, q_ref, kv_ref, probs_ref, dctx_ref, *refs):
    dlogits_ref, dq_ref, *dkv_refs, dkv_all = refs[-7:]
    rows = q_ref.shape[1]
    total = dkv_all.shape[0]

    def ahead(i):
        cols = slice(i * PAIR, (i + 1) * PAIR)
        vcols = slice(D + i * PAIR, D + (i + 1) * PAIR)
        dctx = stack_heads(dctx_ref[0, :, cols])
        return dctx, mm_nt(dctx, kv_ref[0, :, vcols])

    dctx, dprobs = ahead(0)
    for i in range(PAIRS):
        later = ahead(i + 1) if i + 1 < PAIRS else (None, None)
        cols = slice(i * PAIR, (i + 1) * PAIR)
        vcols = slice(D + i * PAIR, D + (i + 1) * PAIR)
        probs = probs_ref[0, 2 * i : 2 * i + 2].reshape(2 * rows, total)
        dkv_all[:, vcols] = mm_tn(probs, dctx).astype(BF)
        wide = probs.astype(F32)
        prod = wide * dprobs
        weighted = jnp.sum(prod, -1, keepdims=True)
        dlogits = (prod - wide * weighted).astype(BF)
        dlogits_ref[0, 2 * i : 2 * i + 2] = dlogits.reshape(2, rows, total)
        dq_ref[0, :, cols] = (pick_heads(mm(dlogits, kv_ref[0, :, cols])) * SCALE).astype(BF)
        dkv_all[:, cols] = mm_tn(dlogits, stack_heads(q_ref[0, :, cols])).astype(BF)
        dctx, dprobs = later
    for j in range(4):
        start = pl.multiple_of(order_ref[j] * rows, rows)
        dkv_refs[j][0] = dkv_all[pl.ds(start, rows), :]


def attend_back(order, queries, keys_values, probs, dctx, dlogits, first, seqs_all, deps=()):
    seqs, rows, _ = queries.shape
    blocks = 4
    total = probs.shape[-1]
    row_spec = lambda width: pl.BlockSpec((1, rows, width), lambda b, *_: (b, 0, 0))
    late_spec = lambda width: pl.BlockSpec((1, rows, width), lambda b, *_: (first + b, 0, 0))
    head_spec = pl.BlockSpec((1, HEADS, rows, total), lambda b, *_: (b, 0, 0, 0))
    late_head = pl.BlockSpec((1, HEADS, rows, total), lambda b, *_: (first + b, 0, 0, 0))
    more = ([] if dlogits is None else [dlogits]) + list(deps)
    outs = pl.pallas_call(
        attend_back_kernel,
        grid_spec=pltpu.PrefetchScalarGridSpec(
            num_scalar_prefetch=1,
            grid=(seqs,),
            in_specs=[
                row_spec(D),
                pl.BlockSpec((1, total, 2 * D), lambda b, *_: (b, 0, 0)),
                head_spec,
                late_spec(D),
            ]
            + [ANY] * len(more),
            out_specs=[late_head, row_spec(D)] + [row_spec(2 * D)] * blocks,
            scratch_shapes=[pltpu.VMEM((total, 2 * D), BF)],
        ),
        out_shape=[
            jax.ShapeDtypeStruct((seqs_all, HEADS, rows, total), BF),
            jax.ShapeDtypeStruct(queries.shape, BF),
        ]
        + [jax.ShapeDtypeStruct((seqs, rows, 2 * D), BF)] * blocks,
        input_output_aliases={} if dlogits is None else {5: 0},
        compiler_params=pltpu.CompilerParams(vmem_limit_bytes=GRANT),
        cost_estimate=pl.CostEstimate(
            flops=8 * seqs * HEADS * rows * total * PAIR,
            bytes_accessed=4 * seqs * HEADS * rows * total,
            transcendentals=0,
        ),
    )(order, queries, keys_values, probs, dctx, *more)
    dkv = [b.reshape(seqs * rows, 2 * D) for b in outs[2:]]
    return outs[0], outs[1].reshape(seqs * rows, D), dkv


def gelu_and_slope(values):
    cdf = 0.5 * lax.erf(values * 0.7071067811865476) + 0.5
    bell = jnp.exp(values * values * -0.5)
    return values * cdf, cdf + values * bell * 0.3989422804014327


def norm(values):
    average = jnp.mean(values, -1, keepdims=True)
    centred = values - average
    inverse = lax.rsqrt(jnp.mean(centred * centred, -1, keepdims=True) + 1e-06)
    return centred * inverse, inverse


def norm_back(grad, normed, inverse):
    first = jnp.mean(grad, -1, keepdims=True)
    second = jnp.mean(grad * normed, -1, keepdims=True)
    return inverse * (grad - first - normed * second)


def load_middle(table_ref, in_refs, down_refs, w_out_ref, w_in_ref, w_down_ref, stage, sems):
    if len(in_refs) == 1:
        ff = w_in_ref.shape[1]
        pltpu.make_async_copy(down_refs[1], w_out_ref, sems.at[0]).start()
        for c in range(4):
            cols = pl.ds(c * (ff // 4), ff // 4)
            pltpu.make_async_copy(
                in_refs[0].at[:, cols], w_in_ref.at[:, cols], sems.at[1 + c]
            ).start()
            pltpu.make_async_copy(
                down_refs[0].at[:, cols], w_down_ref.at[:, cols], sems.at[5 + c]
            ).start()
        wait_whole(w_out_ref, sems.at[0])
    else:
        down = w_down_ref.shape[0] // 4
        wide = w_down_ref.shape[1] // 8
        high, half = D // 8, D // 16
        for piece, dp, seq in pieces_of(down_refs, table_ref):
            pltpu.make_async_copy(
                piece.at[pl.ds(down, half)], stage.at[seq, dp], sems.at[0]
            ).start()
        for piece, dp, seq in pieces_of(in_refs, table_ref):
            rows = pl.ds(pl.multiple_of(dp * high, high), high)
            cols = pl.ds(pl.multiple_of(seq * D, D), D)
            pltpu.make_async_copy(piece, w_in_ref.at[rows, cols], sems.at[1 + seq]).start()
        for piece, dp, seq in pieces_of(down_refs, table_ref):
            rows = pl.ds(pl.multiple_of(seq * down, down), down)
            cols = pl.ds(pl.multiple_of(dp * wide, wide), wide)
            pltpu.make_async_copy(
                piece.at[pl.ds(0, down)], w_down_ref.at[rows, cols], sems.at[5 + (dp >> 1)]
            ).start()
        wait_whole(stage, sems.at[0])
        for s in range(4):
            for d in range(8):
                cols = slice(s * down, (s + 1) * down)
                w_out_ref[d * high : d * high + half, cols] = stage[s, d][:, :down]
                w_out_ref[d * high + half : (d + 1) * high, cols] = stage[s, d][:, down:]


def middle_kernel(
    counts, table_ref, x_ref, ctx_a_ref, ctx_b_ref, cot_ref, vec_ref, b_in_ref, *refs
):
    in_refs, refs = refs[: counts[0]], refs[counts[0] :]
    down_refs, refs = refs[: counts[1]], refs[counts[1] :]
    (
        out_ref, dh1_ref, dctx_ref, act_ref, dinner_ref, dbranch_ref, y1_ref, dattn_ref,
        dvec_ref, db_in_ref, w_out_ref, w_in_ref, w_down_ref, stage, sems,
    ) = refs

    @pl.when(pl.program_id(0) == 0)
    def _():
        load_middle(
            table_ref, in_refs, down_refs, w_out_ref, w_in_ref, w_down_ref, stage, sems
        )
        dvec_ref[...] = jnp.zeros_like(dvec_ref)
        db_in_ref[...] = jnp.zeros_like(db_in_ref)

    vec = lambda i: vec_ref[i : i + 1, :]
    total = lambda v: jnp.sum(v, 0, keepdims=True)
    tokens, ff = act_ref.shape
    wide = ff // 4
    size = min(tokens, SUB)
    blocks = [slice(i, i + size) for i in range(0, tokens, size)]
    early = pl.program_id(0) < pl.num_programs(0) // 2

    def arrived(ref, cols, sem):
        @pl.when(pl.program_id(0) == 0)
        def _():
            wait_whole(ref.at[:, cols], sems.at[sem])

    y1, y1_low, normed1, inverse1, h2 = [], [], [], [], []
    for r in blocks:
        ctx = jnp.where(early, ctx_a_ref[r], ctx_b_ref[r])
        h1 = x_ref[r].astype(F32) + (mm(ctx, w_out_ref[...]) + vec(2))
        normed, inverse = norm(h1)
        first = normed * vec(3) + vec(4)
        normed1.append(normed)
        inverse1.append(inverse)
        y1.append(first)
        y1_low.append(first.astype(BF))
        y1_ref[r] = first.astype(BF)
        h2.append(first + vec(5))
    slopes = []
    for c in range(4):
        cols = slice(c * wide, (c + 1) * wide)
        arrived(w_in_ref, pl.ds(c * wide, wide), 1 + c)
        arrived(w_down_ref, pl.ds(c * wide, wide), 5 + c)
        for i, r in enumerate(blocks):
            inner = mm(y1_low[i], w_in_ref[:, cols]) + b_in_ref[:, cols]
            act, slope = gelu_and_slope(inner)
            act = act.astype(BF)
            act_ref[r, cols] = act
            slopes.append(slope)
            h2[i] = h2[i] + mm_nt(act, w_down_ref[:, cols])
    dh2, dbranch = [], []
    for i, r in enumerate(blocks):
        normed2, inverse2 = norm(h2[i])
        out_ref[r] = (normed2 * vec(6) + vec(7)).astype(BF)
        cot = cot_ref[r].astype(F32)
        dh2.append(norm_back(cot * vec(6), normed2, inverse2))
        dbranch.append(dh2[i].astype(BF))
        dbranch_ref[r] = dbranch[i]
        dvec_ref[5:6, :] += total(dbranch[i].astype(F32))
        dvec_ref[6:7, :] += total(cot * normed2)
        dvec_ref[7:8, :] += total(cot)
    dy1 = list(dh2)
    for c in range(4):
        cols = slice(c * wide, (c + 1) * wide)
        for i, r in enumerate(blocks):
            slope = slopes[c * len(blocks) + i]
            dinner = (mm(dbranch[i], w_down_ref[:, cols]) * slope).astype(BF)
            dinner_ref[r, cols] = dinner
            db_in_ref[:, cols] += total(dinner.astype(F32))
            dy1[i] = dy1[i] + mm_nt(dinner, w_in_ref[:, cols])
    for i, r in enumerate(blocks):
        dh1 = norm_back(dy1[i] * vec(3), normed1[i], inverse1[i])
        dh1_ref[r] = dh1
        dattn = dh1.astype(BF)
        dattn_ref[r] = dattn
        dctx_ref[r] = mm_nt(dattn, w_out_ref[...]).astype(BF)
        dvec_ref[2:3, :] += total(dattn.astype(F32))
        dvec_ref[3:4, :] += total(dy1[i] * normed1[i])
        dvec_ref[4:5, :] += total(dy1[i])


def middle(table, x, ctx_a, ctx_b, cot, vectors, b_in, in_pieces, down_pieces):
    tokens = x.shape[0]
    ff = b_in.shape[1]
    step = 512
    half = tokens // step // 2
    rows = lambda width: pl.BlockSpec((step, width), lambda i, *_: (i, 0))
    ctx_specs = [
        pl.BlockSpec((step, D), lambda i, *_: (jnp.minimum(i, half - 1), 0)),
        pl.BlockSpec((step, D), lambda i, *_: (jnp.maximum(i - half, 0), 0)),
    ]
    whole = lambda a: pl.BlockSpec(a.shape, lambda i, *_: (0, 0))
    fixed = lambda *shape: pl.BlockSpec(shape, lambda i, *_: (0, 0))
    sds = jax.ShapeDtypeStruct
    counts = (len(in_pieces), len(down_pieces))
    return pl.pallas_call(
        functools.partial(middle_kernel, counts),
        grid_spec=pltpu.PrefetchScalarGridSpec(
            num_scalar_prefetch=1,
            grid=(tokens // step,),
            in_specs=[rows(D)]
            + ctx_specs
            + [rows(D)]
            + [whole(vectors), whole(b_in)]
            + [pl.BlockSpec(memory_space=pl.ANY)] * sum(counts),
            out_specs=[rows(D)] * 3
            + [rows(ff)] * 2
            + [rows(D)] * 3
            + [fixed(8, D), fixed(1, ff)],
            scratch_shapes=[
                pltpu.VMEM((D, D), BF),
                pltpu.VMEM((D, ff), BF),
                pltpu.VMEM((D, ff), BF),
                pltpu.VMEM((4, 8, D // 16, ff // 8), BF),
                pltpu.SemaphoreType.DMA((9,)),
            ],
        ),
        out_shape=[
            sds((tokens, D), BF),
            sds((tokens, D), F32),
            sds((tokens, D), BF),
            sds((tokens, ff), BF),
            sds((tokens, ff), BF),
            sds((tokens, D), BF),
            sds((tokens, D), BF),
            sds((tokens, D), BF),
            sds((8, D), F32),
            sds((1, ff), F32),
        ],
        compiler_params=pltpu.CompilerParams(vmem_limit_bytes=GRANT),
        cost_estimate=pl.CostEstimate(
            flops=tokens * (8 * D * ff + 4 * D * D),
            bytes_accessed=40 * MIB,
            transcendentals=2 * tokens * ff,
        ),
    )(table, x, ctx_a, ctx_b, cot, vectors, b_in, *in_pieces, *down_pieces)


def grad_in_kernel(where_ref, y1_ref, dinner_ref, *refs):
    send_ref, keep_ref = refs[-2:]
    z, y = where_ref[0], where_ref[1]
    step = pl.program_id(0)
    high = D // 8
    grad = mm_tn(y1_ref[...], dinner_ref[...]).astype(BF)
    for d in range(8):
        rows = grad[d * high : (d + 1) * high]
        far_y, far_z = y ^ (d & 1), (d >> 1) ^ z

        @pl.when(step < 2)
        def _():
            send_ref[0, far_y, far_z] = rows

        @pl.when(step >= 2)
        def _():
            keep_ref[0, far_y, far_z] = rows


def grad_in(where, y1, dinner, deps=()):
    tokens, ff = dinner.shape
    wide = ff // 4

    def columns(t, where):
        return (0, 2 * (where[2] ^ (t & 1)) + (where[3] ^ (1 - (t >> 1))))

    piece = (1, 2, 4, D // 8, wide)
    shape = jax.ShapeDtypeStruct((2, 2, 4, D // 8, wide), BF)
    return pl.pallas_call(
        grad_in_kernel,
        grid_spec=pltpu.PrefetchScalarGridSpec(
            num_scalar_prefetch=1,
            grid=(4,),
            in_specs=[
                pl.BlockSpec((tokens, D), lambda t, w: (0, 0)),
                pl.BlockSpec((tokens, wide), columns),
            ]
            + [ANY] * len(deps),
            out_specs=[
                pl.BlockSpec(piece, lambda t, w: (jnp.minimum(t, 1), 0, 0, 0, 0)),
                pl.BlockSpec(piece, lambda t, w: (jnp.maximum(t - 2, 0), 0, 0, 0, 0)),
            ],
        ),
        out_shape=[shape, shape],
        compiler_params=pltpu.CompilerParams(vmem_limit_bytes=GRANT),
        cost_estimate=pl.CostEstimate(
            flops=2 * tokens * D * ff, bytes_accessed=14 * MIB, transcendentals=0
        ),
    )(where, y1, dinner, *deps)


def grad_down_kernel(
    where_ref, dbranch_ref, act_ref, ctx_a_ref, ctx_b_ref, dattn_ref, send_ref, keep_ref, grad_out
):
    y, x, core = where_ref[1], where_ref[2], where_ref[3]
    step = pl.program_id(0)
    wide, down = D // 2, D // 4
    high, half = D // 8, D // 16

    @pl.when(step == 0)
    def _():
        part = ctx_a_ref.shape[0]
        grad_out[...] = mm_tn(ctx_a_ref[...], dattn_ref[:part]) + mm_tn(
            ctx_b_ref[...], dattn_ref[part:]
        )

    def put(far_y, far_x, rows, cols, even, odd):
        first = core == 0
        keep_ref[far_y, far_x, 0, rows, cols] = jnp.where(first, even, odd).astype(BF)
        send_ref[far_y, far_x, 0, rows, cols] = jnp.where(first, odd, even).astype(BF)

    grad = mm_tn(dbranch_ref[...], act_ref[...])
    for j in range(2):
        top = pl.multiple_of((2 * step + j) * high, high)
        upper, lower = grad_out[pl.ds(top, half), :], grad_out[pl.ds(top + half, half), :]
        for i in range(2):
            pair = [slice((2 * i + k) * down, (2 * i + k + 1) * down) for k in range(2)]
            side = slice(j * wide, (j + 1) * wide)
            far = (y ^ j, x ^ i)
            put(*far, slice(0, down), slice(None), grad[pair[0], side], grad[pair[1], side])
            tail = slice(down, down + half)
            put(*far, tail, slice(0, down), upper[:, pair[0]], upper[:, pair[1]])
            put(*far, tail, slice(down, 2 * down), lower[:, pair[0]], lower[:, pair[1]])


def grad_down(where, dbranch, act, ctx_a, ctx_b, dattn):
    tokens, ff = act.shape
    wide = ff // 4
    whole = pl.BlockSpec((tokens, D), lambda t, w: (0, 0))
    half = pl.BlockSpec((tokens // 2, D), lambda t, w: (0, 0))
    piece = (D // 4 + D // 16, ff // 8)
    spec = pl.BlockSpec((2, 2, 1) + piece, lambda t, w: (0, 0, t ^ w[0], 0, 0))
    shape = jax.ShapeDtypeStruct((2, 2, 4) + piece, BF)
    return pl.pallas_call(
        grad_down_kernel,
        grid_spec=pltpu.PrefetchScalarGridSpec(
            num_scalar_prefetch=1,
            grid=(4,),
            in_specs=[
                whole,
                pl.BlockSpec((tokens, wide), lambda t, w: (0, t)),
                half,
                half,
                whole,
            ],
            out_specs=[spec, spec],
            scratch_shapes=[pltpu.VMEM((D, D), F32)],
        ),
        out_shape=[shape, shape],
        compiler_params=pltpu.CompilerParams(vmem_limit_bytes=GRANT),
        cost_estimate=pl.CostEstimate(
            flops=2 * tokens * D * (ff + D), bytes_accessed=20 * MIB, transcendentals=0
        ),
    )(where, dbranch, act, ctx_a, ctx_b, dattn)


def grad_qkv_kernel(where_ref, x0_ref, *refs):
    x2_refs, refs = refs[:2], refs[2:]
    dq_refs, refs = refs[:2], refs[2:]
    own_refs, refs = refs[:4], refs[4:]
    far_refs, refs = refs[:4], refs[4:]
    dvec_ref, db_ref = refs[:2]
    send_ref, keep_ref, grad, dvec = refs[-4:]
    z, y, x, core = (where_ref[i] for i in range(4))
    step = pl.program_id(0)
    wide, high = 3 * D // 4, D // 8
    part = x2_refs[0].shape[0]
    x0 = lambda h: x0_ref[h * part : (h + 1) * part]

    @pl.when(step == 0)
    def _():
        grad[:, :D] = mm_tn(x0(0), dq_refs[0][...]) + mm_tn(x0(1), dq_refs[1][...])
        dvec[...] = dvec_ref[...]
        for ref in dq_refs:
            dvec[0:1, :] += jnp.sum(ref[...].astype(F32), 0, keepdims=True)

    for t in (1, 2):

        @pl.when(step == t)
        def _():
            total = None
            for h in range(2):
                own, far = (
                    low(add(refs[h][...], refs[2 + h][...])) for refs in (own_refs, far_refs)
                )
                if t == 2:
                    both = jnp.sum(own.astype(F32), 0, keepdims=True)
                    dvec[1:2, :] += both + jnp.sum(far.astype(F32), 0, keepdims=True)
                piece = mm_tn(x0(h), own) + mm_tn(x2_refs[h][...], far)
                total = piece if total is None else total + piece
            grad[:, t * D : (t + 1) * D] = total

    @pl.when(step == 2)
    def _():
        first = core == 0
        for i in range(2):
            even = grad[:, 2 * i * wide : (2 * i + 1) * wide]
            odd = grad[:, (2 * i + 1) * wide : (2 * i + 2) * wide]
            kept = jnp.where(first, even, odd).astype(BF)
            sent = jnp.where(first, odd, even).astype(BF)
            for d in range(8):
                rows = slice(d * high, (d + 1) * high)
                far = (y ^ (d & 1), x ^ i, (d >> 1) ^ z)
                keep_ref[far + (slice(0, high), slice(None))] = kept[rows]
                send_ref[far + (slice(0, high), slice(None))] = sent[rows]
                extra = []
                for k in range(2):
                    s = 2 * i + k
                    own = dvec[2 * s : 2 * s + 2, d * high : (d + 1) * high]
                    at = (4 * d + s) * high
                    rest = jnp.zeros((PAD - 3, high), F32)
                    extra.append(jnp.concatenate([own, db_ref[0:1, at : at + high], rest], 0))
                tail = far + (slice(high, high + PAD), slice(0, high))
                keep_ref[tail] = jnp.where(first, extra[0], extra[1]).astype(BF)
                send_ref[tail] = jnp.where(first, extra[1], extra[0]).astype(BF)


def grad_qkv(where, x0, x2, dq, own, far, dvec, db_in, deps=()):
    tokens = x0.shape[0]
    fixed = lambda *shape: pl.BlockSpec(shape, lambda t, w: (0, 0))
    half = fixed(tokens // 2, D)
    part = pl.BlockSpec((tokens // 2, D), lambda t, w: (0, jnp.maximum(t - 1, 0)))
    dims = (2, 2, 4, D // 8 + PAD, 3 * D // 4)
    spec = pl.BlockSpec(dims, lambda t, w: (0, 0, 0, 0, 0))
    shape = jax.ShapeDtypeStruct(dims, BF)
    return pl.pallas_call(
        grad_qkv_kernel,
        grid_spec=pltpu.PrefetchScalarGridSpec(
            num_scalar_prefetch=1,
            grid=(3,),
            in_specs=[fixed(tokens, D)]
            + [half] * 4
            + [part] * 8
            + [fixed(8, D)]
            + [fixed(*db_in.shape)]
            + [ANY] * len(deps),
            out_specs=[spec, spec],
            scratch_shapes=[pltpu.VMEM((D, 3 * D), F32), pltpu.VMEM((8, D), F32)],
        ),
        out_shape=[shape, shape],
        compiler_params=pltpu.CompilerParams(vmem_limit_bytes=GRANT),
        cost_estimate=pl.CostEstimate(
            flops=2 * tokens * D * 5 * D, bytes_accessed=16 * MIB, transcendentals=0
        ),
    )(where, x0, *x2, *dq, *own, *far, dvec, db_in, *deps)


def grad_far_kernel(dkv_ref, got_ref, w_ref, *refs):
    total = low(add(dkv_ref[...], got_ref[...]))
    refs[-1][...] = mm_nt(total, w_ref[:, D:]).astype(BF)


def grad_far(dkv, got, w_qkv, deps=()):
    tokens = dkv.shape[0]
    step = 256
    rows = lambda width: pl.BlockSpec((step, width), lambda i: (i, 0))
    return pl.pallas_call(
        grad_far_kernel,
        grid=(tokens // step,),
        in_specs=[
            rows(2 * D),
            rows(2 * D),
            pl.BlockSpec((D, 3 * D), lambda i: (0, 0), pipeline_mode=pl.Buffered(1)),
        ]
        + [ANY] * len(deps),
        out_specs=rows(D),
        out_shape=jax.ShapeDtypeStruct((tokens, D), BF),
        compiler_params=pltpu.CompilerParams(vmem_limit_bytes=GRANT),
        cost_estimate=pl.CostEstimate(
            flops=2 * tokens * D * 2 * D, bytes_accessed=10 * MIB, transcendentals=0
        ),
    )(dkv, got, w_qkv, *deps)


def grad_own_kernel(*refs):
    dkv_refs, refs = refs[:2], refs[2:]
    got_refs, refs = refs[:2], refs[2:]
    dq_refs, refs = refs[:2], refs[2:]
    dh1_ref, w_ref = refs[:2]
    dx_ref = refs[-1]
    early = pl.program_id(0) < pl.num_programs(0) // 2
    pick = lambda pair: jnp.where(early, pair[0][...], pair[1][...])
    total = (pick(dkv_refs).astype(F32) + pick(got_refs).astype(F32)).astype(BF)
    dx = mm_nt(total, w_ref[:, D:]) + mm_nt(pick(dq_refs), w_ref[:, :D])
    dx_ref[...] = dx + dh1_ref[...]


def grad_own(dkv, got, dq, dh1, w_qkv, deps=()):
    tokens = dh1.shape[0]
    step = 256
    half = tokens // step // 2

    def pair(width):
        return [
            pl.BlockSpec((step, width), lambda i: (jnp.minimum(i, half - 1), 0)),
            pl.BlockSpec((step, width), lambda i: (jnp.maximum(i - half, 0), 0)),
        ]

    rows = pl.BlockSpec((step, D), lambda i: (i, 0))
    return pl.pallas_call(
        grad_own_kernel,
        grid=(tokens // step,),
        in_specs=pair(2 * D)
        + pair(2 * D)
        + pair(D)
        + [rows, pl.BlockSpec((D, 3 * D), lambda i: (0, 0), pipeline_mode=pl.Buffered(1))]
        + [ANY] * len(deps),
        out_specs=rows,
        out_shape=jax.ShapeDtypeStruct((tokens, D), F32),
        compiler_params=pltpu.CompilerParams(vmem_limit_bytes=GRANT),
        cost_estimate=pl.CostEstimate(
            flops=2 * tokens * D * 3 * D, bytes_accessed=20 * MIB, transcendentals=0
        ),
    )(*dkv, *got, *dq, dh1, w_qkv, *deps)


def gather_small(b_in, vectors):
    dp, seq = lax.axis_size("dp"), lax.axis_size("seq")
    small = jnp.concatenate([vectors.reshape(-1), b_in])
    whole = lax.all_gather(small, BOTH, axis=0, tiled=False)
    nv = vectors.size
    vec = whole[:, :nv].reshape((dp, seq) + vectors.shape).transpose(1, 2, 0, 3)
    return whole[:, nv:].reshape(1, -1), vec.reshape(8, D)


def reduce_small(g_b, g_vec):
    dp, seq = lax.axis_size("dp"), lax.axis_size("seq")
    vec = g_vec.reshape(seq, 8 // seq, dp, D // dp).transpose(2, 0, 1, 3)
    small = jnp.concatenate([vec.reshape(dp * seq, -1), g_b.reshape(dp * seq, -1)], 1)
    mine = lax.psum_scatter(small, BOTH, scatter_dimension=0, tiled=True)[0]
    nv = 8 * D // (dp * seq)
    return mine[nv:], mine[:nv].reshape(8 // seq, D // dp)


def gather_plain(w_qkv, w_out, w_in, w_down_t):
    both = lambda a, first, second: lax.all_gather(
        lax.all_gather(a, first, axis=0, tiled=True), second, axis=1, tiled=True
    )
    return (
        [both(w_qkv, "dp", "seq")],
        [both(w_in, "dp", "seq")],
        [both(w_down_t, "seq", "dp"), both(w_out, "dp", "seq")],
    )


def reduce_plain(a, first, second):
    part = lax.psum_scatter(a.astype(BF), first, scatter_dimension=0, tiled=True)
    return lax.psum_scatter(part, second, scatter_dimension=1, tiled=True).astype(F32)


def together(*parts):
    return lax.optimization_barrier(parts)


def forward_apart(order, lengths, table, x0, prev_logits, weights):
    w_qkv, w_out, w_in, w_down, b_in, vectors = weights
    seqs = x0.shape[0]
    half = seqs // 2
    x2_a, x1 = swap_x(x0[:half]), swap_core(x0)
    small = jnp.concatenate([vectors, b_in.reshape(1, -1)], 0)
    small = jnp.pad(small, ((0, PAD - small.shape[0]), (0, w_qkv.shape[1] - small.shape[1])))
    qkv = stack_z_direct(jnp.concatenate([w_qkv, small], 0))
    cut = w_out.shape[0] // 2
    turned = jnp.concatenate([w_out[:cut], w_out[cut:]], 1)
    down = jnp.concatenate([w_down.T, turned], 0)
    x1, qkv, w_in, down, x_b = together(x1, qkv, w_in, down, x0[half:])

    qkv_x, qkv_y = swap_x(qkv), swap_y(qkv)
    in_pair = jnp.stack([w_in, swap_z(w_in, 1)])
    down_pair = jnp.stack([down, swap_z(down, 1)])
    qkv, qkv_x, qkv_y, x2_a, in_pair, down_pair, x_b = together(
        qkv, qkv_x, qkv_y, x2_a, in_pair, down_pair, x_b
    )

    qkv_xy, x2_b = swap_y(qkv_x), swap_x(x_b)
    x3_a, qkv_far = swap_core(x2_a), swap_core(qkv)
    in_got = swap_z(in_pair, 2)
    qkv_xy, x2_b, in_pair, in_got, down_pair, x3_a, qkv_far = together(
        qkv_xy, x2_b, in_pair, in_got, down_pair, x3_a, qkv_far
    )
    in_own = jnp.concatenate([in_pair, in_got], 0)
    qkv_near = [qkv, qkv_x, qkv_y, qkv_xy]
    qkv_pieces = qkv_near + [qkv_far] + [swap_core(a) for a in qkv_near[1:]]

    in_x, in_y, x3_b = swap_x(in_own), swap_y(in_own), swap_core(x2_b)
    down_got = swap_z(down_pair, 2)
    q_a, kv_a, ctx_a, probs_a, f_qkv, f_vec, f_b = lead(
        table, order, lengths, (x0, x1, x2_a, x3_a), (0, 0, 0, 0), half, 0,
        qkv_pieces, prev_logits,
    )
    in_own, in_x, in_y, x3_b, down_pair, down_got, f_qkv, ctx_a, f_b = together(
        in_own, in_x, in_y, x3_b, down_pair, down_got, f_qkv, ctx_a, f_b
    )
    down_own = jnp.concatenate([down_pair, down_got], 0)

    down_x, down_y = swap_x(down_own), swap_y(down_own)
    in_far = [swap_core(a) for a in (in_own, in_x, in_y)]
    q_b, kv_b, ctx_b, probs_b = lead(
        table, order, lengths, (x0, x1, x2_b, x3_b), (half, half, 0, 0), half, half,
        [f_qkv], prev_logits, f_vec,
    )
    down_own, down_x, down_y, in_x, ctx_b, *in_far = together(
        down_own, down_x, down_y, in_x, ctx_b, *in_far
    )

    in_xy, down_xy = swap_y(in_x), swap_x(down_y)
    down_far = [swap_core(a) for a in (down_own, down_x, down_y)]
    in_pieces = [in_own, in_x, in_y, in_xy] + in_far + [swap_core(in_xy)]
    down_pieces = [down_own, down_x, down_y, down_xy] + down_far + [swap_core(down_xy)]
    first, second = (q_a, kv_a, ctx_a, probs_a), (q_b, kv_b, ctx_b, probs_b)
    return first, second, f_qkv, f_vec, f_b, in_pieces, down_pieces, [x2_a, x2_b]


def shards_apart(
    hidden_states, prev_logits, lengths, w_qkv, w_out, w_in, w_down, b_in, vectors, cotangent
):
    seqs, rows, _ = hidden_states.shape
    tokens = seqs * rows
    half = seqs // 2
    order = jnp.arange(4, dtype=jnp.int32) ^ lax.axis_index("seq")
    table, where = piece_table(), jnp.stack(place()).astype(jnp.int32)
    x0 = hidden_states.reshape(tokens, D)
    first, second, f_qkv, f_vec, f_b, in_pieces, down_pieces, x2 = forward_apart(
        order, lengths, table, hidden_states, prev_logits,
        (w_qkv, w_out, w_in, w_down, b_in, vectors),
    )
    rows_of = lambda a: a.reshape(-1, D)
    ctx, x2 = [rows_of(first[2]), rows_of(second[2])], [rows_of(a) for a in x2]
    out, dh1, dctx, act, dinner, dbranch, y1, dattn, dvec, db_in = middle(
        table, x0, *ctx, cotangent.reshape(tokens, D), f_vec, f_b, in_pieces, down_pieces
    )
    dctx = dctx.reshape(seqs, rows, D)

    d_send, d_keep = grad_down(where, dbranch, act, *ctx, dattn)
    d_core = swap_core(d_send)
    i_send, i_keep = grad_in(where, y1, dinner, [d_keep])
    i_core = swap_core(i_send)
    d_core = after(d_core, i_keep)
    d_sent = low(add(d_keep[1], d_core[1]))
    d_one = swap_y(d_sent)
    i_core = after(i_core, d_sent)
    i_sent = low(add(i_keep[1], i_core[1]))
    i_one = swap_x(i_sent)
    dlogits, dq_a, dkv_a = attend_back(
        order, first[0], first[1], first[3], dctx, None, 0, seqs, [d_sent, i_sent]
    )
    far_a, own_a = swap_core(dkv_a[3]), swap_core(dkv_a[1])
    dlogits, dq_b, dkv_b = attend_back(
        order, second[0], second[1], second[3], dctx, dlogits, half, seqs, [dq_a]
    )
    far_b, own_b = swap_core(dkv_b[3]), swap_core(dkv_b[1])
    far_a, own_a = after(far_a, dq_b), after(own_a, dq_b)
    d_one, i_one = after(d_one, dq_b), after(i_one, dq_b)
    d_sent = low(add(d_keep[0, 1], d_core[0, 1], d_one[1]))
    d_two = swap_x(d_sent)
    i_sent = low(add(i_keep[0, 1], i_core[0, 1], i_one[1]))
    i_two = swap_y(i_sent)
    dq, own, far = [dq_a, dq_b], [dkv_a[0], dkv_b[0], own_a, own_b], [dkv_a[2], dkv_b[2], far_a, far_b]
    q_send, q_keep = grad_qkv(where, x0, x2, dq, own, far, dvec, db_in, [d_sent, i_sent])
    d_two, i_two, q_send, q_keep = together(d_two, i_two, q_send, q_keep)
    q_core = swap_core(q_send)
    d_part = lambda k: add(d_keep[0, 0, k], d_core[0, 0, k], d_one[0, k], d_two[k])
    i_part = lambda k: add(i_keep[0, 0, k], i_core[0, 0, k], i_one[0, k], i_two[k])
    upper, lower = slice(2, 4), slice(0, 2)
    d_sent, i_sent = low(d_part(upper)), low(i_part(upper))
    i_far, d_far = swap_z(i_sent, 2), swap_z(d_sent, 2)
    q_core = after(q_core, d_sent, i_sent)
    q_sent = low(add(q_keep[1], q_core[1]))
    q_one = swap_y(q_sent)
    dx2_a = grad_far(far[0], far[2], f_qkv, [q_sent])
    got_a = swap_x(dx2_a)
    dx2_b = grad_far(far[1], far[3], f_qkv, [dx2_a])
    dx = grad_own(own[:2], own[2:], dq, dh1, f_qkv, [dx2_b])
    q_one, dx, got_a, dx2_b = together(q_one, dx, got_a, dx2_b)
    q_sent = low(add(q_keep[0, 1], q_core[0, 1], q_one[1]))
    q_two = swap_x(q_sent)
    i_far, d_far = after(i_far, q_sent), after(d_far, q_sent)
    d_last = d_part(lower) + d_far.astype(F32)
    i_last = i_part(lower) + i_far.astype(F32)
    d_end, i_end = swap_z(low(d_last[1]), 1), swap_z(low(i_last[1]), 1)
    q_two, d_end, i_end, d_last, i_last, dx2_b = together(
        q_two, d_end, i_end, d_last, i_last, dx2_b
    )
    got_b = swap_x(dx2_b)
    q_part = lambda k: add(q_keep[0, 0, k], q_core[0, 0, k], q_one[0, k], q_two[k])
    q_sent = [low(q_part(k)) for k in range(1, 4)]
    q_far = [swap_z(q, k) for q, k in zip(q_sent, range(1, 4))]
    o_low, o_in = d_last[0] + d_end.astype(F32), i_last[0] + i_end.astype(F32)
    o_low, o_in, got_a, got_b = after((o_low, o_in, got_a, got_b), *q_sent)
    o_top = q_part(0) + add(*q_far)
    grad_hidden = low(dx + jnp.concatenate([got_a, got_b], 0).astype(F32))
    down, cut, (extra, high) = w_down.shape[1], w_qkv.shape[0], vectors.shape
    shape = hidden_states.shape
    return (
        out.reshape(shape),
        grad_hidden.reshape(shape),
        dlogits,
        o_top[:cut],
        jnp.concatenate([o_low[down:, :down], o_low[down:, down:]], 0),
        o_in,
        o_low[:down].T,
        o_top[cut + extra, : b_in.shape[0]],
        o_top[cut : cut + extra, :high],
    )


def shards_plain(
    hidden_states, prev_logits, lengths, w_qkv, w_out, w_in, w_down, b_in, vectors, cotangent
):
    seqs, rows, _ = hidden_states.shape
    tokens = seqs * rows
    order = jnp.arange(4, dtype=jnp.int32) ^ lax.axis_index("seq")
    half = seqs // 2
    x0 = hidden_states.reshape(tokens, D)
    x1, x2 = swap_core(hidden_states), swap_x(hidden_states)
    x_blocks = (hidden_states, x1, x2, swap_core(x2))
    table = jnp.zeros((2,), jnp.int32)
    qkv, in_pieces, down_pieces = gather_plain(w_qkv, w_out, w_in, w_down.T)
    f_qkv = qkv[0]
    f_b, f_vec = gather_small(b_in, vectors)
    f_b, f_vec = f_b.astype(F32), f_vec.astype(F32)
    made = [
        lead(
            table, order, lengths, x_blocks, (h * half,) * 4, half, h * half, qkv,
            prev_logits, f_vec,
        )
        for h in range(2)
    ]
    ctx = [m[2].reshape(-1, D) for m in made]
    out, dh1, dctx, act, dinner, dbranch, y1, dattn, dvec, db_in = middle(
        table, x0, *ctx, cotangent.reshape(tokens, D), f_vec, f_b, in_pieces, down_pieces
    )
    dctx = dctx.reshape(seqs, rows, D)
    dlogits, dq, dkv = None, [], []
    for h in range(2):
        dlogits, dq_h, dkv_h = attend_back(
            order, made[h][0], made[h][1], made[h][3], dctx, dlogits, h * half, seqs
        )
        dq.append(dq_h)
        dkv.append(dkv_h)
    got_far = [swap_core(dkv[h][3]) for h in range(2)]
    far = [grad_far(dkv[h][2], got_far[h], f_qkv) for h in range(2)]
    got_rows = [swap_x(f) for f in far]
    got_kv = [swap_core(dkv[h][1]) for h in range(2)]
    dkv0 = [dkv[h][0] for h in range(2)]
    dx = grad_own(dkv0, got_kv, dq, dh1, f_qkv)
    whole = lambda pair: jnp.concatenate(pair, 0)
    grad_hidden = low(dx + whole(got_rows).astype(F32))
    sum0 = whole([low(add(a, b)) for a, b in zip(dkv0, got_kv)])
    sum2 = whole([low(add(dkv[h][2], got_far[h])) for h in range(2)])
    dq = whole(dq)
    g_kv = mm_tn(x0, sum0) + mm_tn(x2.reshape(tokens, D), sum2)
    g_qkv = jnp.concatenate([mm_tn(x0, dq), g_kv], 1)
    dvec = dvec.at[0].add(jnp.sum(dq, 0, dtype=F32))
    dvec = dvec.at[1].add(jnp.sum(add(sum0[:, D:], sum2[:, D:]), 0))
    o_b, o_vec = reduce_small(db_in, dvec)
    shape = hidden_states.shape
    return (
        out.reshape(shape),
        grad_hidden.reshape(shape),
        dlogits,
        reduce_plain(g_qkv, "dp", "seq"),
        reduce_plain(mm_tn(whole(ctx), dattn), "dp", "seq"),
        reduce_plain(mm_tn(y1, dinner), "dp", "seq"),
        reduce_plain(mm_tn(act, dbranch), "dp", "seq"),
        o_b,
        o_vec,
    )


def shards(*args):
    return (shards_apart if by_pieces() else shards_plain)(*args)


def solution(mesh):
    return jax.shard_map(
        shards,
        mesh=mesh,
        in_specs=(
            P("dp", "seq", None),
            P("dp", None, "seq", None),
            P("dp"),
            P("dp", "seq"),
            P("dp", "seq"),
            P("dp", "seq"),
            P("dp", "seq"),
            P(("dp", "seq")),
            P("seq", "dp"),
            P("dp", "seq", None),
        ),
        out_specs=(
            P("dp", "seq", None),
            P("dp", "seq", None),
            P("dp", None, "seq", None),
            P("dp", "seq"),
            P("dp", "seq"),
            P("dp", "seq"),
            P("dp", "seq"),
            P(("dp", "seq")),
            P("seq", "dp"),
        ),
        check_vma=False,
    )
```

```python
import functools

import jax
import jax.numpy as jnp
from jax import lax
from jax.experimental import pallas as pl
from jax.experimental.pallas import tpu as pltpu
from jax.sharding import PartitionSpec as P

D = 768
HEADS = 12
HEAD_DIM = 64
PAIRS = HEADS // 2
PAIR = 2 * HEAD_DIM
SCALE = HEAD_DIM ** (-0.5)
BF = jnp.bfloat16
F32 = jnp.float32
BOTH = ("dp", "seq")
MIB = 1 << 20
PAD = 16
SUB = 256
ANY = pl.BlockSpec(memory_space=pl.ANY)
GRANT = 60 * MIB


def mm(a, b):
    return lax.dot_general(a, b, (((1,), (0,)), ((), ())), preferred_element_type=F32)


def mm_nt(a, b):
    return lax.dot_general(a, b, (((1,), (1,)), ((), ())), preferred_element_type=F32)


def mm_tn(a, b):
    return lax.dot_general(a, b, (((0,), (0,)), ((), ())), preferred_element_type=F32)


def stack_heads(pair):
    lane = lax.broadcasted_iota(jnp.int32, pair.shape, 1)
    zero = jnp.zeros_like(pair)
    return jnp.concatenate(
        [jnp.where(lane < HEAD_DIM, pair, zero), jnp.where(lane < HEAD_DIM, zero, pair)], 0
    )


def pick_heads(stacked):
    rows = stacked.shape[0] // 2
    lane = lax.broadcasted_iota(jnp.int32, (rows, PAIR), 1)
    return jnp.where(lane < HEAD_DIM, stacked[:rows], stacked[rows:])


def swap(a, axis, bit):
    size = lax.axis_size(axis)
    return lax.ppermute(a, axis, [(i, i ^ bit) for i in range(size)])


def swap_core(a):
    return swap(a, "seq", 1)


def swap_x(a):
    return swap(a, "seq", 2)


def swap_y(a):
    return swap(a, "dp", 1)


def swap_z(a, places):
    return swap(a, "dp", 2 * places)


def by_pieces():
    return lax.axis_size("dp") == 8 and lax.axis_size("seq") == 4


def place():
    dp, seq = lax.axis_index("dp"), lax.axis_index("seq")
    return dp >> 1, dp & 1, seq >> 1, seq & 1


def stack_z(a):
    pair = jnp.stack([a, swap_z(a, 1)])
    return jnp.concatenate([pair, swap_z(pair, 2)], 0)


def stack_z_direct(a):
    return jnp.stack([a] + [swap_z(a, k) for k in range(1, 4)])


def spread(own, own_x, own_y, own_xy):
    half = [own, own_x, own_y, own_xy]
    return half + [swap_core(b) for b in half]


def piece_table():
    z, y, x, core = place()
    table = []
    for far in range(8):
        for k in range(4):
            table.append(2 * (z ^ k) + (y ^ (far >> 1 & 1)))
            table.append(2 * (x ^ (far & 1)) + (core ^ (far >> 2)))
    return jnp.stack(table).astype(jnp.int32)


def pieces_of(refs, table_ref):
    for a, ref in enumerate(refs):
        depth = ref.shape[0]
        for k in range(depth):
            n = a * depth + k
            yield ref.at[k], table_ref[2 * n], table_ref[2 * n + 1]


def wait_whole(ref, sem):
    pltpu.make_async_copy(ref, ref, sem).wait()


def add(*parts):
    return sum(p.astype(F32) for p in parts)


def low(a):
    return a.astype(BF)


def after(a, *done):
    return lax.optimization_barrier((a,) + done)[0]


def load_qkv(table_ref, piece_refs, w_all, vec_ref, b_ref, stage, sems):
    high, wide = D // 8 + PAD, 3 * D // 4
    for piece, dp, seq in pieces_of(piece_refs, table_ref):
        rows = pl.ds(pl.multiple_of(dp * high, PAD), high)
        pltpu.make_async_copy(piece, stage.at[seq, rows], sems.at[0]).start()
    wait_whole(stage, sems.at[0])
    body, width = D // 8, D // 8
    for s in range(4):
        for d in range(8):
            top = d * high
            w_all[d * body : (d + 1) * body, s * wide : (s + 1) * wide] = stage[
                s, top : top + body
            ]
            extra = stage[s, top + body : top + high, :width].astype(F32)
            vec_ref[2 * s : 2 * s + 2, d * width : (d + 1) * width] = extra[0:2]
            place_of = (4 * d + s) * width
            b_ref[0:1, place_of : place_of + width] = extra[2:3]


def lead_kernel(count, assemble, first, table_ref, order_ref, len_ref, *refs):
    x_refs, refs = refs[:4], refs[4:]
    piece_refs, refs = refs[:count], refs[count:]
    if assemble:
        prev_ref, q_ref, kv_ref, ctx_ref, probs_ref, w_ref, vec_ref, b_ref = refs[:8]
    else:
        vec_ref, prev_ref, q_ref, kv_ref, ctx_ref, probs_ref = refs[:6]
    w_all, x_all, stage, sems = refs[-4:]
    rows, total = q_ref.shape[1], x_all.shape[0]

    @pl.when(pl.program_id(0) == 0)
    def _():
        if assemble:
            load_qkv(table_ref, piece_refs, w_all, vec_ref, b_ref, stage, sems)
            pltpu.make_async_copy(w_all, w_ref, sems.at[1]).start()
        else:
            pltpu.make_async_copy(piece_refs[0], w_all, sems.at[0]).start()
            wait_whole(w_all, sems.at[0])

    for j in range(4):
        start = pl.multiple_of(order_ref[j] * rows, rows)
        x_all[pl.ds(start, rows), :] = x_refs[j][0]
    valid = len_ref[first + pl.program_id(0)]
    key_pos = lax.broadcasted_iota(jnp.int32, (1, total), 1)
    padding = jnp.where(key_pos < valid, 0.0, -1e9)

    def project(g):
        width = 2 * PAIR
        cols = slice(g * width, (g + 1) * width)
        part = lambda n: slice(n * D + g * width, n * D + (g + 1) * width)
        query = (mm(x_refs[0][0], w_all[:, cols]) + vec_ref[0:1, cols]).astype(BF)
        q_ref[0, :, cols] = query * SCALE
        kv_ref[0, :, cols] = mm(x_all[...], w_all[:, part(1)]).astype(BF)
        value = mm(x_all[...], w_all[:, part(2)]) + vec_ref[1:2, cols]
        kv_ref[0, :, part(1)] = value.astype(BF)

    def score(i):
        cols = slice(i * PAIR, (i + 1) * PAIR)
        raw = mm_nt(stack_heads(q_ref[0, :, cols]), kv_ref[0, :, cols])
        prev = prev_ref[0, 2 * i : 2 * i + 2].reshape(2 * rows, total).astype(F32)
        return raw + (prev + padding)

    def mix(i, raw):
        cols = slice(i * PAIR, (i + 1) * PAIR)
        vcols = slice(D + i * PAIR, D + (i + 1) * PAIR)
        largest = jnp.max(raw, -1, keepdims=True)
        expo = jnp.exp(raw - largest)
        summed = jnp.sum(expo, -1, keepdims=True)
        probs = (expo * (1.0 / summed)).astype(BF)
        probs_ref[0, 2 * i : 2 * i + 2] = probs.reshape(2, rows, total)
        ctx_ref[0, :, cols] = pick_heads(mm(probs, kv_ref[0, :, vcols])).astype(BF)

    project(0)
    raw = score(0)
    for i in range(PAIRS):
        if i % 2 == 0 and i + 2 < PAIRS:
            project(i // 2 + 1)
        later = score(i + 1) if i + 1 < PAIRS else None
        mix(i, raw)
        raw = later

    if assemble:

        @pl.when(pl.program_id(0) == pl.num_programs(0) - 1)
        def _():
            pltpu.make_async_copy(w_all, w_ref, sems.at[1]).wait()


def lead(table, order, lengths, x_blocks, starts, seqs, first, pieces, prev_logits, vec=None):
    assemble = vec is None
    rows = x_blocks[0].shape[1]
    total = prev_logits.shape[-1]
    ff = 4 * D

    def x_spec(j):
        return pl.BlockSpec((1, rows, D), lambda b, *_: (starts[j] + b, 0, 0))

    fixed = lambda *shape: pl.BlockSpec(shape, lambda b, *_: (0, 0))
    row_spec = pl.BlockSpec((1, rows, D), lambda b, *_: (b, 0, 0))
    sds = jax.ShapeDtypeStruct
    out_specs = [
        row_spec,
        pl.BlockSpec((1, total, 2 * D), lambda b, *_: (b, 0, 0)),
        row_spec,
        pl.BlockSpec((1, HEADS, rows, total), lambda b, *_: (b, 0, 0, 0)),
    ]
    out_shape = [
        sds((seqs, rows, D), BF),
        sds((seqs, total, 2 * D), BF),
        sds((seqs, rows, D), BF),
        sds((seqs, HEADS, rows, total), BF),
    ]
    if assemble:
        out_specs += [ANY, fixed(8, D), fixed(1, ff)]
        out_shape += [sds((D, 3 * D), BF), sds((8, D), F32), sds((1, ff), F32)]
    stage = (4, 8 * (D // 8 + PAD), 3 * D // 4) if assemble else (1, PAD, 128)
    return pl.pallas_call(
        functools.partial(lead_kernel, len(pieces), assemble, first),
        grid_spec=pltpu.PrefetchScalarGridSpec(
            num_scalar_prefetch=3,
            grid=(seqs,),
            in_specs=[x_spec(j) for j in range(4)]
            + [ANY] * len(pieces)
            + ([] if assemble else [fixed(8, D)])
            + [
                pl.BlockSpec(
                    (1, HEADS, rows, total), lambda b, *_: (first + b, 0, 0, 0)
                )
            ],
            out_specs=out_specs,
            scratch_shapes=[
                pltpu.VMEM((D, 3 * D), BF),
                pltpu.VMEM((total, D), BF),
                pltpu.VMEM(stage, BF),
                pltpu.SemaphoreType.DMA((2,)),
            ],
        ),
        out_shape=out_shape,
        compiler_params=pltpu.CompilerParams(vmem_limit_bytes=GRANT),
        cost_estimate=pl.CostEstimate(
            flops=seqs * rows * D * (18 * D + 4 * total),
            bytes_accessed=seqs * 8 * MIB,
            transcendentals=seqs * HEADS * rows * total,
        ),
    )(table, order, lengths, *x_blocks, *pieces, *([] if assemble else [vec]), prev_logits)


def attend_back_kernel(order_ref, q_ref, kv_ref, probs_ref, dctx_ref, *refs):
    dlogits_ref, dq_ref, *dkv_refs, dkv_all = refs[-7:]
    rows = q_ref.shape[1]
    total = dkv_all.shape[0]

    def ahead(i):
        cols = slice(i * PAIR, (i + 1) * PAIR)
        vcols = slice(D + i * PAIR, D + (i + 1) * PAIR)
        dctx = stack_heads(dctx_ref[0, :, cols])
        return dctx, mm_nt(dctx, kv_ref[0, :, vcols])

    dctx, dprobs = ahead(0)
    for i in range(PAIRS):
        later = ahead(i + 1) if i + 1 < PAIRS else (None, None)
        cols = slice(i * PAIR, (i + 1) * PAIR)
        vcols = slice(D + i * PAIR, D + (i + 1) * PAIR)
        probs = probs_ref[0, 2 * i : 2 * i + 2].reshape(2 * rows, total)
        dkv_all[:, vcols] = mm_tn(probs, dctx).astype(BF)
        wide = probs.astype(F32)
        prod = wide * dprobs
        weighted = jnp.sum(prod, -1, keepdims=True)
        dlogits = (prod - wide * weighted).astype(BF)
        dlogits_ref[0, 2 * i : 2 * i + 2] = dlogits.reshape(2, rows, total)
        dq_ref[0, :, cols] = (pick_heads(mm(dlogits, kv_ref[0, :, cols])) * SCALE).astype(BF)
        dkv_all[:, cols] = mm_tn(dlogits, stack_heads(q_ref[0, :, cols])).astype(BF)
        dctx, dprobs = later
    for j in range(4):
        start = pl.multiple_of(order_ref[j] * rows, rows)
        dkv_refs[j][0] = dkv_all[pl.ds(start, rows), :]


def attend_back(order, queries, keys_values, probs, dctx, dlogits, first, seqs_all, deps=()):
    seqs, rows, _ = queries.shape
    blocks = 4
    total = probs.shape[-1]
    row_spec = lambda width: pl.BlockSpec((1, rows, width), lambda b, *_: (b, 0, 0))
    late_spec = lambda width: pl.BlockSpec((1, rows, width), lambda b, *_: (first + b, 0, 0))
    head_spec = pl.BlockSpec((1, HEADS, rows, total), lambda b, *_: (b, 0, 0, 0))
    late_head = pl.BlockSpec((1, HEADS, rows, total), lambda b, *_: (first + b, 0, 0, 0))
    more = ([] if dlogits is None else [dlogits]) + list(deps)
    outs = pl.pallas_call(
        attend_back_kernel,
        grid_spec=pltpu.PrefetchScalarGridSpec(
            num_scalar_prefetch=1,
            grid=(seqs,),
            in_specs=[
                row_spec(D),
                pl.BlockSpec((1, total, 2 * D), lambda b, *_: (b, 0, 0)),
                head_spec,
                late_spec(D),
            ]
            + [ANY] * len(more),
            out_specs=[late_head, row_spec(D)] + [row_spec(2 * D)] * blocks,
            scratch_shapes=[pltpu.VMEM((total, 2 * D), BF)],
        ),
        out_shape=[
            jax.ShapeDtypeStruct((seqs_all, HEADS, rows, total), BF),
            jax.ShapeDtypeStruct(queries.shape, BF),
        ]
        + [jax.ShapeDtypeStruct((seqs, rows, 2 * D), BF)] * blocks,
        input_output_aliases={} if dlogits is None else {5: 0},
        compiler_params=pltpu.CompilerParams(vmem_limit_bytes=GRANT),
        cost_estimate=pl.CostEstimate(
            flops=8 * seqs * HEADS * rows * total * PAIR,
            bytes_accessed=4 * seqs * HEADS * rows * total,
            transcendentals=0,
        ),
    )(order, queries, keys_values, probs, dctx, *more)
    dkv = [b.reshape(seqs * rows, 2 * D) for b in outs[2:]]
    return outs[0], outs[1].reshape(seqs * rows, D), dkv


def gelu_and_slope(values):
    cdf = 0.5 * lax.erf(values * 0.7071067811865476) + 0.5
    bell = jnp.exp(values * values * -0.5)
    return values * cdf, cdf + values * bell * 0.3989422804014327


def norm(values):
    average = jnp.mean(values, -1, keepdims=True)
    centred = values - average
    inverse = lax.rsqrt(jnp.mean(centred * centred, -1, keepdims=True) + 1e-06)
    return centred * inverse, inverse


def norm_back(grad, normed, inverse):
    first = jnp.mean(grad, -1, keepdims=True)
    second = jnp.mean(grad * normed, -1, keepdims=True)
    return inverse * (grad - first - normed * second)


def load_middle(table_ref, in_refs, down_refs, w_out_ref, w_in_ref, w_down_ref, stage, sems):
    if len(in_refs) == 1:
        ff = w_in_ref.shape[1]
        pltpu.make_async_copy(down_refs[1], w_out_ref, sems.at[0]).start()
        for c in range(4):
            cols = pl.ds(c * (ff // 4), ff // 4)
            pltpu.make_async_copy(
                in_refs[0].at[:, cols], w_in_ref.at[:, cols], sems.at[1 + c]
            ).start()
            pltpu.make_async_copy(
                down_refs[0].at[:, cols], w_down_ref.at[:, cols], sems.at[5 + c]
            ).start()
        wait_whole(w_out_ref, sems.at[0])
    else:
        down = w_down_ref.shape[0] // 4
        wide = w_down_ref.shape[1] // 8
        high, half = D // 8, D // 16
        for piece, dp, seq in pieces_of(down_refs, table_ref):
            pltpu.make_async_copy(
                piece.at[pl.ds(down, half)], stage.at[seq, dp], sems.at[0]
            ).start()
        for piece, dp, seq in pieces_of(in_refs, table_ref):
            rows = pl.ds(pl.multiple_of(dp * high, high), high)
            cols = pl.ds(pl.multiple_of(seq * D, D), D)
            pltpu.make_async_copy(piece, w_in_ref.at[rows, cols], sems.at[1 + seq]).start()
        for piece, dp, seq in pieces_of(down_refs, table_ref):
            rows = pl.ds(pl.multiple_of(seq * down, down), down)
            cols = pl.ds(pl.multiple_of(dp * wide, wide), wide)
            pltpu.make_async_copy(
                piece.at[pl.ds(0, down)], w_down_ref.at[rows, cols], sems.at[5 + (dp >> 1)]
            ).start()
        wait_whole(stage, sems.at[0])
        for s in range(4):
            for d in range(8):
                cols = slice(s * down, (s + 1) * down)
                w_out_ref[d * high : d * high + half, cols] = stage[s, d][:, :down]
                w_out_ref[d * high + half : (d + 1) * high, cols] = stage[s, d][:, down:]


def middle_kernel(
    counts, table_ref, x_ref, ctx_a_ref, ctx_b_ref, cot_ref, vec_ref, b_in_ref, *refs
):
    in_refs, refs = refs[: counts[0]], refs[counts[0] :]
    down_refs, refs = refs[: counts[1]], refs[counts[1] :]
    (
        out_ref, dh1_ref, dctx_ref, act_ref, dinner_ref, dbranch_ref, y1_ref, dattn_ref,
        dvec_ref, db_in_ref, w_out_ref, w_in_ref, w_down_ref, stage, sems,
    ) = refs

    @pl.when(pl.program_id(0) == 0)
    def _():
        load_middle(
            table_ref, in_refs, down_refs, w_out_ref, w_in_ref, w_down_ref, stage, sems
        )
        dvec_ref[...] = jnp.zeros_like(dvec_ref)
        db_in_ref[...] = jnp.zeros_like(db_in_ref)

    vec = lambda i: vec_ref[i : i + 1, :]
    total = lambda v: jnp.sum(v, 0, keepdims=True)
    tokens, ff = act_ref.shape
    wide = ff // 4
    size = min(tokens, SUB)
    blocks = [slice(i, i + size) for i in range(0, tokens, size)]
    early = pl.program_id(0) < pl.num_programs(0) // 2

    def arrived(ref, cols, sem):
        @pl.when(pl.program_id(0) == 0)
        def _():
            wait_whole(ref.at[:, cols], sems.at[sem])

    y1, y1_low, normed1, inverse1, h2 = [], [], [], [], []
    for r in blocks:
        ctx = jnp.where(early, ctx_a_ref[r], ctx_b_ref[r])
        h1 = x_ref[r].astype(F32) + (mm(ctx, w_out_ref[...]) + vec(2))
        normed, inverse = norm(h1)
        first = normed * vec(3) + vec(4)
        normed1.append(normed)
        inverse1.append(inverse)
        y1.append(first)
        y1_low.append(first.astype(BF))
        y1_ref[r] = first.astype(BF)
        h2.append(first + vec(5))
    slopes = []
    for c in range(4):
        cols = slice(c * wide, (c + 1) * wide)
        arrived(w_in_ref, pl.ds(c * wide, wide), 1 + c)
        arrived(w_down_ref, pl.ds(c * wide, wide), 5 + c)
        for i, r in enumerate(blocks):
            inner = mm(y1_low[i], w_in_ref[:, cols]) + b_in_ref[:, cols]
            act, slope = gelu_and_slope(inner)
            act = act.astype(BF)
            act_ref[r, cols] = act
            slopes.append(slope)
            h2[i] = h2[i] + mm_nt(act, w_down_ref[:, cols])
    dh2, dbranch = [], []
    for i, r in enumerate(blocks):
        normed2, inverse2 = norm(h2[i])
        out_ref[r] = (normed2 * vec(6) + vec(7)).astype(BF)
        cot = cot_ref[r].astype(F32)
        dh2.append(norm_back(cot * vec(6), normed2, inverse2))
        dbranch.append(dh2[i].astype(BF))
        dbranch_ref[r] = dbranch[i]
        dvec_ref[5:6, :] += total(dbranch[i].astype(F32))
        dvec_ref[6:7, :] += total(cot * normed2)
        dvec_ref[7:8, :] += total(cot)
    dy1 = list(dh2)
    for c in range(4):
        cols = slice(c * wide, (c + 1) * wide)
        for i, r in enumerate(blocks):
            slope = slopes[c * len(blocks) + i]
            dinner = (mm(dbranch[i], w_down_ref[:, cols]) * slope).astype(BF)
            dinner_ref[r, cols] = dinner
            db_in_ref[:, cols] += total(dinner.astype(F32))
            dy1[i] = dy1[i] + mm_nt(dinner, w_in_ref[:, cols])
    for i, r in enumerate(blocks):
        dh1 = norm_back(dy1[i] * vec(3), normed1[i], inverse1[i])
        dh1_ref[r] = dh1
        dattn = dh1.astype(BF)
        dattn_ref[r] = dattn
        dctx_ref[r] = mm_nt(dattn, w_out_ref[...]).astype(BF)
        dvec_ref[2:3, :] += total(dattn.astype(F32))
        dvec_ref[3:4, :] += total(dy1[i] * normed1[i])
        dvec_ref[4:5, :] += total(dy1[i])


def middle(table, x, ctx_a, ctx_b, cot, vectors, b_in, in_pieces, down_pieces):
    tokens = x.shape[0]
    ff = b_in.shape[1]
    step = 256
    half = tokens // step // 2
    rows = lambda width: pl.BlockSpec((step, width), lambda i, *_: (i, 0))
    ctx_specs = [
        pl.BlockSpec((step, D), lambda i, *_: (jnp.minimum(i, half - 1), 0)),
        pl.BlockSpec((step, D), lambda i, *_: (jnp.maximum(i - half, 0), 0)),
    ]
    whole = lambda a: pl.BlockSpec(a.shape, lambda i, *_: (0, 0))
    fixed = lambda *shape: pl.BlockSpec(shape, lambda i, *_: (0, 0))
    sds = jax.ShapeDtypeStruct
    counts = (len(in_pieces), len(down_pieces))
    return pl.pallas_call(
        functools.partial(middle_kernel, counts),
        grid_spec=pltpu.PrefetchScalarGridSpec(
            num_scalar_prefetch=1,
            grid=(tokens // step,),
            in_specs=[rows(D)]
            + ctx_specs
            + [rows(D)]
            + [whole(vectors), whole(b_in)]
            + [pl.BlockSpec(memory_space=pl.ANY)] * sum(counts),
            out_specs=[rows(D)] * 3
            + [rows(ff)] * 2
            + [rows(D)] * 3
            + [fixed(8, D), fixed(1, ff)],
            scratch_shapes=[
                pltpu.VMEM((D, D), BF),
                pltpu.VMEM((D, ff), BF),
                pltpu.VMEM((D, ff), BF),
                pltpu.VMEM((4, 8, D // 16, ff // 8), BF),
                pltpu.SemaphoreType.DMA((9,)),
            ],
        ),
        out_shape=[
            sds((tokens, D), BF),
            sds((tokens, D), F32),
            sds((tokens, D), BF),
            sds((tokens, ff), BF),
            sds((tokens, ff), BF),
            sds((tokens, D), BF),
            sds((tokens, D), BF),
            sds((tokens, D), BF),
            sds((8, D), F32),
            sds((1, ff), F32),
        ],
        compiler_params=pltpu.CompilerParams(vmem_limit_bytes=GRANT),
        cost_estimate=pl.CostEstimate(
            flops=tokens * (8 * D * ff + 4 * D * D),
            bytes_accessed=40 * MIB,
            transcendentals=2 * tokens * ff,
        ),
    )(table, x, ctx_a, ctx_b, cot, vectors, b_in, *in_pieces, *down_pieces)


def grad_in_kernel(where_ref, y1_ref, dinner_ref, *refs):
    send_ref, keep_ref = refs[-2:]
    z, y = where_ref[0], where_ref[1]
    step = pl.program_id(0)
    high = D // 8
    grad = mm_tn(y1_ref[...], dinner_ref[...]).astype(BF)

    def put(ref):
        for d in range(8):
            ref[0, y ^ (d & 1), (d >> 1) ^ z] = grad[d * high : (d + 1) * high]

    @pl.when(step < 2)
    def _():
        put(send_ref)

    @pl.when(step >= 2)
    def _():
        put(keep_ref)


def grad_in(where, y1, dinner, deps=()):
    tokens, ff = dinner.shape
    wide = ff // 4

    def columns(t, where):
        return (0, 2 * (where[2] ^ (t & 1)) + (where[3] ^ (1 - (t >> 1))))

    piece = (1, 2, 4, D // 8, wide)
    shape = jax.ShapeDtypeStruct((2, 2, 4, D // 8, wide), BF)
    return pl.pallas_call(
        grad_in_kernel,
        grid_spec=pltpu.PrefetchScalarGridSpec(
            num_scalar_prefetch=1,
            grid=(4,),
            in_specs=[
                pl.BlockSpec((tokens, D), lambda t, w: (0, 0)),
                pl.BlockSpec((tokens, wide), columns),
            ]
            + [ANY] * len(deps),
            out_specs=[
                pl.BlockSpec(piece, lambda t, w: (jnp.minimum(t, 1), 0, 0, 0, 0)),
                pl.BlockSpec(piece, lambda t, w: (jnp.maximum(t - 2, 0), 0, 0, 0, 0)),
            ],
        ),
        out_shape=[shape, shape],
        compiler_params=pltpu.CompilerParams(vmem_limit_bytes=GRANT),
        cost_estimate=pl.CostEstimate(
            flops=2 * tokens * D * ff, bytes_accessed=14 * MIB, transcendentals=0
        ),
    )(where, y1, dinner, *deps)


def grad_down_kernel(
    where_ref, dbranch_ref, act_ref, ctx_a_ref, ctx_b_ref, dattn_ref, send_ref, keep_ref, grad_out
):
    y, x, core = where_ref[1], where_ref[2], where_ref[3]
    step = pl.program_id(0)
    wide, down = D // 2, D // 4
    high, half = D // 8, D // 16

    @pl.when(step == 0)
    def _():
        part = ctx_a_ref.shape[0]
        grad_out[...] = mm_tn(ctx_a_ref[...], dattn_ref[:part]) + mm_tn(
            ctx_b_ref[...], dattn_ref[part:]
        )

    def put(far_y, far_x, rows, cols, even, odd):
        first = core == 0
        keep_ref[far_y, far_x, 0, rows, cols] = jnp.where(first, even, odd).astype(BF)
        send_ref[far_y, far_x, 0, rows, cols] = jnp.where(first, odd, even).astype(BF)

    grad = mm_tn(dbranch_ref[...], act_ref[...])
    for j in range(2):
        top = pl.multiple_of((2 * step + j) * high, high)
        upper, lower = grad_out[pl.ds(top, half), :], grad_out[pl.ds(top + half, half), :]
        for i in range(2):
            pair = [slice((2 * i + k) * down, (2 * i + k + 1) * down) for k in range(2)]
            side = slice(j * wide, (j + 1) * wide)
            far = (y ^ j, x ^ i)
            put(*far, slice(0, down), slice(None), grad[pair[0], side], grad[pair[1], side])
            tail = slice(down, down + half)
            put(*far, tail, slice(0, down), upper[:, pair[0]], upper[:, pair[1]])
            put(*far, tail, slice(down, 2 * down), lower[:, pair[0]], lower[:, pair[1]])


def grad_down(where, dbranch, act, ctx_a, ctx_b, dattn):
    tokens, ff = act.shape
    wide = ff // 4
    whole = pl.BlockSpec((tokens, D), lambda t, w: (0, 0))
    half = pl.BlockSpec((tokens // 2, D), lambda t, w: (0, 0))
    piece = (D // 4 + D // 16, ff // 8)
    spec = pl.BlockSpec((2, 2, 1) + piece, lambda t, w: (0, 0, t ^ w[0], 0, 0))
    shape = jax.ShapeDtypeStruct((2, 2, 4) + piece, BF)
    return pl.pallas_call(
        grad_down_kernel,
        grid_spec=pltpu.PrefetchScalarGridSpec(
            num_scalar_prefetch=1,
            grid=(4,),
            in_specs=[
                whole,
                pl.BlockSpec((tokens, wide), lambda t, w: (0, t)),
                half,
                half,
                whole,
            ],
            out_specs=[spec, spec],
            scratch_shapes=[pltpu.VMEM((D, D), F32)],
        ),
        out_shape=[shape, shape],
        compiler_params=pltpu.CompilerParams(vmem_limit_bytes=GRANT),
        cost_estimate=pl.CostEstimate(
            flops=2 * tokens * D * (ff + D), bytes_accessed=20 * MIB, transcendentals=0
        ),
    )(where, dbranch, act, ctx_a, ctx_b, dattn)


def grad_qkv_kernel(where_ref, x0_ref, *refs):
    x2_refs, refs = refs[:2], refs[2:]
    dq_refs, refs = refs[:2], refs[2:]
    own_refs, refs = refs[:4], refs[4:]
    far_refs, refs = refs[:4], refs[4:]
    dvec_ref, db_ref = refs[:2]
    send_ref, keep_ref, grad, dvec = refs[-4:]
    z, y, x, core = (where_ref[i] for i in range(4))
    step = pl.program_id(0)
    wide, high = 3 * D // 4, D // 8
    part = x2_refs[0].shape[0]
    x0 = lambda h: x0_ref[h * part : (h + 1) * part]

    @pl.when(step == 0)
    def _():
        grad[:, :D] = mm_tn(x0(0), dq_refs[0][...]) + mm_tn(x0(1), dq_refs[1][...])
        dvec[...] = dvec_ref[...]
        for ref in dq_refs:
            dvec[0:1, :] += jnp.sum(ref[...].astype(F32), 0, keepdims=True)

    for t in (1, 2):

        @pl.when(step == t)
        def _():
            total = None
            for h in range(2):
                own, far = (
                    low(add(refs[h][...], refs[2 + h][...])) for refs in (own_refs, far_refs)
                )
                if t == 2:
                    both = jnp.sum(own.astype(F32), 0, keepdims=True)
                    dvec[1:2, :] += both + jnp.sum(far.astype(F32), 0, keepdims=True)
                piece = mm_tn(x0(h), own) + mm_tn(x2_refs[h][...], far)
                total = piece if total is None else total + piece
            grad[:, t * D : (t + 1) * D] = total

    @pl.when(step == 2)
    def _():
        first = core == 0
        for i in range(2):
            even = grad[:, 2 * i * wide : (2 * i + 1) * wide]
            odd = grad[:, (2 * i + 1) * wide : (2 * i + 2) * wide]
            kept = jnp.where(first, even, odd).astype(BF)
            sent = jnp.where(first, odd, even).astype(BF)
            for d in range(8):
                rows = slice(d * high, (d + 1) * high)
                far = (y ^ (d & 1), x ^ i, (d >> 1) ^ z)
                keep_ref[far + (slice(0, high), slice(None))] = kept[rows]
                send_ref[far + (slice(0, high), slice(None))] = sent[rows]
                extra = []
                for k in range(2):
                    s = 2 * i + k
                    own = dvec[2 * s : 2 * s + 2, d * high : (d + 1) * high]
                    at = (4 * d + s) * high
                    rest = jnp.zeros((PAD - 3, high), F32)
                    extra.append(jnp.concatenate([own, db_ref[0:1, at : at + high], rest], 0))
                tail = far + (slice(high, high + PAD), slice(0, high))
                keep_ref[tail] = jnp.where(first, extra[0], extra[1]).astype(BF)
                send_ref[tail] = jnp.where(first, extra[1], extra[0]).astype(BF)


def grad_qkv(where, x0, x2, dq, own, far, dvec, db_in, deps=()):
    tokens = x0.shape[0]
    fixed = lambda *shape: pl.BlockSpec(shape, lambda t, w: (0, 0))
    half = fixed(tokens // 2, D)
    part = pl.BlockSpec((tokens // 2, D), lambda t, w: (0, jnp.maximum(t - 1, 0)))
    dims = (2, 2, 4, D // 8 + PAD, 3 * D // 4)
    spec = pl.BlockSpec(dims, lambda t, w: (0, 0, 0, 0, 0))
    shape = jax.ShapeDtypeStruct(dims, BF)
    return pl.pallas_call(
        grad_qkv_kernel,
        grid_spec=pltpu.PrefetchScalarGridSpec(
            num_scalar_prefetch=1,
            grid=(3,),
            in_specs=[fixed(tokens, D)]
            + [half] * 4
            + [part] * 8
            + [fixed(8, D)]
            + [fixed(*db_in.shape)]
            + [ANY] * len(deps),
            out_specs=[spec, spec],
            scratch_shapes=[pltpu.VMEM((D, 3 * D), F32), pltpu.VMEM((8, D), F32)],
        ),
        out_shape=[shape, shape],
        compiler_params=pltpu.CompilerParams(vmem_limit_bytes=GRANT),
        cost_estimate=pl.CostEstimate(
            flops=2 * tokens * D * 5 * D, bytes_accessed=16 * MIB, transcendentals=0
        ),
    )(where, x0, *x2, *dq, *own, *far, dvec, db_in, *deps)


def grad_far_kernel(dkv_ref, got_ref, w_ref, *refs):
    total = low(add(dkv_ref[...], got_ref[...]))
    refs[-1][...] = mm_nt(total, w_ref[:, D:]).astype(BF)


def grad_far(dkv, got, w_qkv, deps=()):
    tokens = dkv.shape[0]
    step = 256
    rows = lambda width: pl.BlockSpec((step, width), lambda i: (i, 0))
    return pl.pallas_call(
        grad_far_kernel,
        grid=(tokens // step,),
        in_specs=[
            rows(2 * D),
            rows(2 * D),
            pl.BlockSpec((D, 3 * D), lambda i: (0, 0), pipeline_mode=pl.Buffered(1)),
        ]
        + [ANY] * len(deps),
        out_specs=rows(D),
        out_shape=jax.ShapeDtypeStruct((tokens, D), BF),
        compiler_params=pltpu.CompilerParams(vmem_limit_bytes=GRANT),
        cost_estimate=pl.CostEstimate(
            flops=2 * tokens * D * 2 * D, bytes_accessed=10 * MIB, transcendentals=0
        ),
    )(dkv, got, w_qkv, *deps)


def grad_own_kernel(*refs):
    dkv_refs, refs = refs[:2], refs[2:]
    got_refs, refs = refs[:2], refs[2:]
    dq_refs, refs = refs[:2], refs[2:]
    dh1_ref, w_ref = refs[:2]
    dx_ref = refs[-1]
    early = pl.program_id(0) < pl.num_programs(0) // 2
    pick = lambda pair: jnp.where(early, pair[0][...], pair[1][...])
    total = (pick(dkv_refs).astype(F32) + pick(got_refs).astype(F32)).astype(BF)
    dx = mm_nt(total, w_ref[:, D:]) + mm_nt(pick(dq_refs), w_ref[:, :D])
    dx_ref[...] = dx + dh1_ref[...]


def grad_own(dkv, got, dq, dh1, w_qkv, deps=()):
    tokens = dh1.shape[0]
    step = 256
    half = tokens // step // 2

    def pair(width):
        return [
            pl.BlockSpec((step, width), lambda i: (jnp.minimum(i, half - 1), 0)),
            pl.BlockSpec((step, width), lambda i: (jnp.maximum(i - half, 0), 0)),
        ]

    rows = pl.BlockSpec((step, D), lambda i: (i, 0))
    return pl.pallas_call(
        grad_own_kernel,
        grid=(tokens // step,),
        in_specs=pair(2 * D)
        + pair(2 * D)
        + pair(D)
        + [rows, pl.BlockSpec((D, 3 * D), lambda i: (0, 0), pipeline_mode=pl.Buffered(1))]
        + [ANY] * len(deps),
        out_specs=rows,
        out_shape=jax.ShapeDtypeStruct((tokens, D), F32),
        compiler_params=pltpu.CompilerParams(vmem_limit_bytes=GRANT),
        cost_estimate=pl.CostEstimate(
            flops=2 * tokens * D * 3 * D, bytes_accessed=20 * MIB, transcendentals=0
        ),
    )(*dkv, *got, *dq, dh1, w_qkv, *deps)


def gather_small(b_in, vectors):
    dp, seq = lax.axis_size("dp"), lax.axis_size("seq")
    small = jnp.concatenate([vectors.reshape(-1), b_in])
    whole = lax.all_gather(small, BOTH, axis=0, tiled=False)
    nv = vectors.size
    vec = whole[:, :nv].reshape((dp, seq) + vectors.shape).transpose(1, 2, 0, 3)
    return whole[:, nv:].reshape(1, -1), vec.reshape(8, D)


def reduce_small(g_b, g_vec):
    dp, seq = lax.axis_size("dp"), lax.axis_size("seq")
    vec = g_vec.reshape(seq, 8 // seq, dp, D // dp).transpose(2, 0, 1, 3)
    small = jnp.concatenate([vec.reshape(dp * seq, -1), g_b.reshape(dp * seq, -1)], 1)
    mine = lax.psum_scatter(small, BOTH, scatter_dimension=0, tiled=True)[0]
    nv = 8 * D // (dp * seq)
    return mine[nv:], mine[:nv].reshape(8 // seq, D // dp)


def gather_plain(w_qkv, w_out, w_in, w_down_t):
    both = lambda a, first, second: lax.all_gather(
        lax.all_gather(a, first, axis=0, tiled=True), second, axis=1, tiled=True
    )
    return (
        [both(w_qkv, "dp", "seq")],
        [both(w_in, "dp", "seq")],
        [both(w_down_t, "seq", "dp"), both(w_out, "dp", "seq")],
    )


def reduce_plain(a, first, second):
    part = lax.psum_scatter(a.astype(BF), first, scatter_dimension=0, tiled=True)
    return lax.psum_scatter(part, second, scatter_dimension=1, tiled=True).astype(F32)


def together(*parts):
    return lax.optimization_barrier(parts)


def forward_apart(order, lengths, table, x0, prev_logits, weights):
    w_qkv, w_out, w_in, w_down, b_in, vectors = weights
    seqs = x0.shape[0]
    half = seqs // 2
    x2_a, x1 = swap_x(x0[:half]), swap_core(x0)
    small = jnp.concatenate([vectors, b_in.reshape(1, -1)], 0)
    small = jnp.pad(small, ((0, PAD - small.shape[0]), (0, w_qkv.shape[1] - small.shape[1])))
    qkv = stack_z_direct(jnp.concatenate([w_qkv, small], 0))
    cut = w_out.shape[0] // 2
    turned = jnp.concatenate([w_out[:cut], w_out[cut:]], 1)
    down = jnp.concatenate([w_down.T, turned], 0)
    x1, qkv, w_in, down, x_b = together(x1, qkv, w_in, down, x0[half:])

    qkv_x, qkv_y = swap_x(qkv), swap_y(qkv)
    in_pair = jnp.stack([w_in, swap_z(w_in, 1)])
    down_pair = jnp.stack([down, swap_z(down, 1)])
    qkv, qkv_x, qkv_y, x2_a, in_pair, down_pair, x_b = together(
        qkv, qkv_x, qkv_y, x2_a, in_pair, down_pair, x_b
    )

    qkv_xy, x2_b = swap_y(qkv_x), swap_x(x_b)
    x3_a, qkv_far = swap_core(x2_a), swap_core(qkv)
    in_got = swap_z(in_pair, 2)
    qkv_xy, x2_b, in_pair, in_got, down_pair, x3_a, qkv_far = together(
        qkv_xy, x2_b, in_pair, in_got, down_pair, x3_a, qkv_far
    )
    in_own = jnp.concatenate([in_pair, in_got], 0)
    qkv_near = [qkv, qkv_x, qkv_y, qkv_xy]
    qkv_pieces = qkv_near + [qkv_far] + [swap_core(a) for a in qkv_near[1:]]

    in_x, in_y, x3_b = swap_x(in_own), swap_y(in_own), swap_core(x2_b)
    down_got = swap_z(down_pair, 2)
    q_a, kv_a, ctx_a, probs_a, f_qkv, f_vec, f_b = lead(
        table, order, lengths, (x0, x1, x2_a, x3_a), (0, 0, 0, 0), half, 0,
        qkv_pieces, prev_logits,
    )
    in_own, in_x, in_y, x3_b, down_pair, down_got, f_qkv, ctx_a, f_b = together(
        in_own, in_x, in_y, x3_b, down_pair, down_got, f_qkv, ctx_a, f_b
    )
    down_own = jnp.concatenate([down_pair, down_got], 0)

    down_x, down_y = swap_x(down_own), swap_y(down_own)
    in_far = [swap_core(a) for a in (in_own, in_x, in_y)]
    q_b, kv_b, ctx_b, probs_b = lead(
        table, order, lengths, (x0, x1, x2_b, x3_b), (half, half, 0, 0), half, half,
        [f_qkv], prev_logits, f_vec,
    )
    down_own, down_x, down_y, in_x, ctx_b, *in_far = together(
        down_own, down_x, down_y, in_x, ctx_b, *in_far
    )

    in_xy, down_xy = swap_y(in_x), swap_x(down_y)
    down_far = [swap_core(a) for a in (down_own, down_x, down_y)]
    in_pieces = [in_own, in_x, in_y, in_xy] + in_far + [swap_core(in_xy)]
    down_pieces = [down_own, down_x, down_y, down_xy] + down_far + [swap_core(down_xy)]
    first, second = (q_a, kv_a, ctx_a, probs_a), (q_b, kv_b, ctx_b, probs_b)
    return first, second, f_qkv, f_vec, f_b, in_pieces, down_pieces, [x2_a, x2_b]


def shards_apart(
    hidden_states, prev_logits, lengths, w_qkv, w_out, w_in, w_down, b_in, vectors, cotangent
):
    seqs, rows, _ = hidden_states.shape
    tokens = seqs * rows
    half = seqs // 2
    order = jnp.arange(4, dtype=jnp.int32) ^ lax.axis_index("seq")
    table, where = piece_table(), jnp.stack(place()).astype(jnp.int32)
    x0 = hidden_states.reshape(tokens, D)
    first, second, f_qkv, f_vec, f_b, in_pieces, down_pieces, x2 = forward_apart(
        order, lengths, table, hidden_states, prev_logits,
        (w_qkv, w_out, w_in, w_down, b_in, vectors),
    )
    rows_of = lambda a: a.reshape(-1, D)
    ctx, x2 = [rows_of(first[2]), rows_of(second[2])], [rows_of(a) for a in x2]
    out, dh1, dctx, act, dinner, dbranch, y1, dattn, dvec, db_in = middle(
        table, x0, *ctx, cotangent.reshape(tokens, D), f_vec, f_b, in_pieces, down_pieces
    )
    dctx = dctx.reshape(seqs, rows, D)

    d_send, d_keep = grad_down(where, dbranch, act, *ctx, dattn)
    d_core = swap_core(d_send)
    i_send, i_keep = grad_in(where, y1, dinner, [d_keep])
    i_core = swap_core(i_send)
    d_core = after(d_core, i_keep)
    d_sent = low(add(d_keep[1], d_core[1]))
    d_one = swap_y(d_sent)
    i_core = after(i_core, d_sent)
    i_sent = low(add(i_keep[1], i_core[1]))
    i_one = swap_x(i_sent)
    dlogits, dq_a, dkv_a = attend_back(
        order, first[0], first[1], first[3], dctx, None, 0, seqs, [d_sent, i_sent]
    )
    far_a, own_a = swap_core(dkv_a[3]), swap_core(dkv_a[1])
    dlogits, dq_b, dkv_b = attend_back(
        order, second[0], second[1], second[3], dctx, dlogits, half, seqs, [dq_a]
    )
    far_b, own_b = swap_core(dkv_b[3]), swap_core(dkv_b[1])
    far_a, own_a = after(far_a, dq_b), after(own_a, dq_b)
    d_one, i_one = after(d_one, dq_b), after(i_one, dq_b)
    d_sent = low(add(d_keep[0, 1], d_core[0, 1], d_one[1]))
    d_two = swap_x(d_sent)
    i_sent = low(add(i_keep[0, 1], i_core[0, 1], i_one[1]))
    i_two = swap_y(i_sent)
    dq, own, far = [dq_a, dq_b], [dkv_a[0], dkv_b[0], own_a, own_b], [dkv_a[2], dkv_b[2], far_a, far_b]
    q_send, q_keep = grad_qkv(where, x0, x2, dq, own, far, dvec, db_in, [d_sent, i_sent])
    d_two, i_two, q_send, q_keep = together(d_two, i_two, q_send, q_keep)
    q_core = swap_core(q_send)
    d_part = lambda k: add(d_keep[0, 0, k], d_core[0, 0, k], d_one[0, k], d_two[k])
    i_part = lambda k: add(i_keep[0, 0, k], i_core[0, 0, k], i_one[0, k], i_two[k])
    upper, lower = slice(2, 4), slice(0, 2)
    d_sent, i_sent = low(d_part(upper)), low(i_part(upper))
    i_far, d_far = swap_z(i_sent, 2), swap_z(d_sent, 2)
    q_core = after(q_core, d_sent, i_sent)
    q_sent = low(add(q_keep[1], q_core[1]))
    q_one = swap_y(q_sent)
    dx2_a = grad_far(far[0], far[2], f_qkv, [q_sent])
    got_a = swap_x(dx2_a)
    dx2_b = grad_far(far[1], far[3], f_qkv, [dx2_a])
    dx = grad_own(own[:2], own[2:], dq, dh1, f_qkv, [dx2_b])
    q_one, dx, dx2_b, got_a = together(q_one, dx, dx2_b, got_a)
    q_sent = low(add(q_keep[0, 1], q_core[0, 1], q_one[1]))
    q_two = swap_x(q_sent)
    got_b = swap_x(after(dx2_b, q_sent))
    i_far, d_far = after(i_far, q_sent), after(d_far, q_sent)
    i_last = i_part(lower) + i_far.astype(F32)
    i_end = swap_z(low(i_last[1]), 1)
    d_last = d_part(lower) + d_far.astype(F32)
    d_end = swap_z(low(d_last[1]), 1)
    q_two, i_last, d_last = together(q_two, i_last, d_last)
    q_part = lambda k: add(q_keep[0, 0, k], q_core[0, 0, k], q_one[0, k], q_two[k])
    q_sent = [low(q_part(k)) for k in range(1, 4)]
    q_far = [swap_z(q, k) for q, k in zip(q_sent, range(1, 4))]
    i_end, d_end, dx = after((i_end, d_end, dx), *q_sent)
    o_in = i_last[0] + i_end.astype(F32)
    o_low = d_last[0] + d_end.astype(F32)
    o_top = q_part(0) + add(*q_far)
    got_b = after(got_b, o_top)
    grad_hidden = low(dx + jnp.concatenate([got_a, got_b], 0).astype(F32))
    down, cut, (extra, high) = w_down.shape[1], w_qkv.shape[0], vectors.shape
    shape = hidden_states.shape
    return (
        out.reshape(shape),
        grad_hidden.reshape(shape),
        dlogits,
        o_top[:cut],
        jnp.concatenate([o_low[down:, :down], o_low[down:, down:]], 0),
        o_in,
        o_low[:down].T,
        o_top[cut + extra, : b_in.shape[0]],
        o_top[cut : cut + extra, :high],
    )


def shards_plain(
    hidden_states, prev_logits, lengths, w_qkv, w_out, w_in, w_down, b_in, vectors, cotangent
):
    seqs, rows, _ = hidden_states.shape
    tokens = seqs * rows
    order = jnp.arange(4, dtype=jnp.int32) ^ lax.axis_index("seq")
    half = seqs // 2
    x0 = hidden_states.reshape(tokens, D)
    x1, x2 = swap_core(hidden_states), swap_x(hidden_states)
    x_blocks = (hidden_states, x1, x2, swap_core(x2))
    table = jnp.zeros((2,), jnp.int32)
    qkv, in_pieces, down_pieces = gather_plain(w_qkv, w_out, w_in, w_down.T)
    f_qkv = qkv[0]
    f_b, f_vec = gather_small(b_in, vectors)
    f_b, f_vec = f_b.astype(F32), f_vec.astype(F32)
    made = [
        lead(
            table, order, lengths, x_blocks, (h * half,) * 4, half, h * half, qkv,
            prev_logits, f_vec,
        )
        for h in range(2)
    ]
    ctx = [m[2].reshape(-1, D) for m in made]
    out, dh1, dctx, act, dinner, dbranch, y1, dattn, dvec, db_in = middle(
        table, x0, *ctx, cotangent.reshape(tokens, D), f_vec, f_b, in_pieces, down_pieces
    )
    dctx = dctx.reshape(seqs, rows, D)
    dlogits, dq, dkv = None, [], []
    for h in range(2):
        dlogits, dq_h, dkv_h = attend_back(
            order, made[h][0], made[h][1], made[h][3], dctx, dlogits, h * half, seqs
        )
        dq.append(dq_h)
        dkv.append(dkv_h)
    got_far = [swap_core(dkv[h][3]) for h in range(2)]
    far = [grad_far(dkv[h][2], got_far[h], f_qkv) for h in range(2)]
    got_rows = [swap_x(f) for f in far]
    got_kv = [swap_core(dkv[h][1]) for h in range(2)]
    dkv0 = [dkv[h][0] for h in range(2)]
    dx = grad_own(dkv0, got_kv, dq, dh1, f_qkv)
    whole = lambda pair: jnp.concatenate(pair, 0)
    grad_hidden = low(dx + whole(got_rows).astype(F32))
    sum0 = whole([low(add(a, b)) for a, b in zip(dkv0, got_kv)])
    sum2 = whole([low(add(dkv[h][2], got_far[h])) for h in range(2)])
    dq = whole(dq)
    g_kv = mm_tn(x0, sum0) + mm_tn(x2.reshape(tokens, D), sum2)
    g_qkv = jnp.concatenate([mm_tn(x0, dq), g_kv], 1)
    dvec = dvec.at[0].add(jnp.sum(dq, 0, dtype=F32))
    dvec = dvec.at[1].add(jnp.sum(add(sum0[:, D:], sum2[:, D:]), 0))
    o_b, o_vec = reduce_small(db_in, dvec)
    shape = hidden_states.shape
    return (
        out.reshape(shape),
        grad_hidden.reshape(shape),
        dlogits,
        reduce_plain(g_qkv, "dp", "seq"),
        reduce_plain(mm_tn(whole(ctx), dattn), "dp", "seq"),
        reduce_plain(mm_tn(y1, dinner), "dp", "seq"),
        reduce_plain(mm_tn(act, dbranch), "dp", "seq"),
        o_b,
        o_vec,
    )


def shards(*args):
    return (shards_apart if by_pieces() else shards_plain)(*args)


def solution(mesh):
    return jax.shard_map(
        shards,
        mesh=mesh,
        in_specs=(
            P("dp", "seq", None),
            P("dp", None, "seq", None),
            P("dp"),
            P("dp", "seq"),
            P("dp", "seq"),
            P("dp", "seq"),
            P("dp", "seq"),
            P(("dp", "seq")),
            P("seq", "dp"),
            P("dp", "seq", None),
        ),
        out_specs=(
            P("dp", "seq", None),
            P("dp", "seq", None),
            P("dp", None, "seq", None),
            P("dp", "seq"),
            P("dp", "seq"),
            P("dp", "seq"),
            P("dp", "seq"),
            P(("dp", "seq")),
            P("seq", "dp"),
        ),
        check_vma=False,
    )
```

```python
import functools

import jax
import jax.numpy as jnp
from jax import lax
from jax.experimental import pallas as pl
from jax.experimental.pallas import tpu as pltpu
from jax.sharding import PartitionSpec as P

D = 768
HEADS = 12
HEAD_DIM = 64
PAIRS = HEADS // 2
PAIR = 2 * HEAD_DIM
SCALE = HEAD_DIM ** (-0.5)
BF = jnp.bfloat16
F32 = jnp.float32
BOTH = ("dp", "seq")
MIB = 1 << 20
PAD = 16
ANY = pl.BlockSpec(memory_space=pl.ANY)
GRANT = 60 * MIB


def mm(a, b):
    return lax.dot_general(a, b, (((1,), (0,)), ((), ())), preferred_element_type=F32)


def mm_nt(a, b):
    return lax.dot_general(a, b, (((1,), (1,)), ((), ())), preferred_element_type=F32)


def mm_tn(a, b):
    return lax.dot_general(a, b, (((0,), (0,)), ((), ())), preferred_element_type=F32)


def stack_heads(pair):
    lane = lax.broadcasted_iota(jnp.int32, pair.shape, 1)
    zero = jnp.zeros_like(pair)
    return jnp.concatenate(
        [jnp.where(lane < HEAD_DIM, pair, zero), jnp.where(lane < HEAD_DIM, zero, pair)], 0
    )


def pick_heads(stacked):
    rows = stacked.shape[0] // 2
    lane = lax.broadcasted_iota(jnp.int32, (rows, PAIR), 1)
    return jnp.where(lane < HEAD_DIM, stacked[:rows], stacked[rows:])


def swap(a, axis, bit):
    size = lax.axis_size(axis)
    return lax.ppermute(a, axis, [(i, i ^ bit) for i in range(size)])


def swap_core(a):
    return swap(a, "seq", 1)


def swap_x(a):
    return swap(a, "seq", 2)


def swap_y(a):
    return swap(a, "dp", 1)


def swap_z(a, places):
    return swap(a, "dp", 2 * places)


def turn_z(a):
    size = lax.axis_size("dp")
    return lax.ppermute(a, "dp", [(i, (i + 2) % size) for i in range(size)])


def by_pieces():
    return lax.axis_size("dp") == 8 and lax.axis_size("seq") == 4


def place():
    dp, seq = lax.axis_index("dp"), lax.axis_index("seq")
    return dp >> 1, dp & 1, seq >> 1, seq & 1


def stack_z_direct(a):
    return jnp.stack([a] + [swap_z(a, k) for k in range(1, 4)])


def piece_table():
    z, y, x, core = place()
    table = []
    for far in range(8):
        for k in range(4):
            table.append(2 * (z ^ k) + (y ^ (far >> 1 & 1)))
            table.append(2 * (x ^ (far & 1)) + (core ^ (far >> 2)))
    return jnp.stack(table).astype(jnp.int32)


def turned_table():
    z, y, x, core = place()
    table = []
    for far in range(8):
        for k in range(4):
            table.append(2 * ((z - (far & 3)) & 3) + (y ^ (k >> 1)))
            table.append(2 * (x ^ (k & 1)) + (core ^ (far >> 2)))
    return jnp.stack(table).astype(jnp.int32)


def pieces_of(refs, table_ref):
    for a, ref in enumerate(refs):
        depth = ref.shape[0]
        for k in range(depth):
            n = a * depth + k
            yield ref.at[k], table_ref[2 * n], table_ref[2 * n + 1]


def wait_whole(ref, sem):
    pltpu.make_async_copy(ref, ref, sem).wait()


def add(*parts):
    return sum(p.astype(F32) for p in parts)


def low(a):
    return a.astype(BF)


def after(a, *done):
    return lax.optimization_barrier((a,) + done)[0]


def load_qkv(table_ref, piece_refs, w_all, vec_ref, b_ref, stage, sems):
    high, wide = D // 8 + PAD, 3 * D // 4
    for piece, dp, seq in pieces_of(piece_refs, table_ref):
        rows = pl.ds(pl.multiple_of(dp * high, PAD), high)
        pltpu.make_async_copy(piece, stage.at[seq, rows], sems.at[0]).start()
    wait_whole(stage, sems.at[0])
    body, width = D // 8, D // 8
    for s in range(4):
        for d in range(8):
            top = d * high
            w_all[d * body : (d + 1) * body, s * wide : (s + 1) * wide] = stage[
                s, top : top + body
            ]
            extra = stage[s, top + body : top + high, :width].astype(F32)
            vec_ref[2 * s : 2 * s + 2, d * width : (d + 1) * width] = extra[0:2]
            place_of = (4 * d + s) * width
            b_ref[0:1, place_of : place_of + width] = extra[2:3]


def lead_kernel(count, assemble, first, table_ref, order_ref, len_ref, *refs):
    x_refs, refs = refs[:4], refs[4:]
    piece_refs, refs = refs[:count], refs[count:]
    if assemble:
        prev_ref, q_ref, kv_ref, ctx_ref, probs_ref, w_ref, vec_ref, b_ref = refs[:8]
    else:
        vec_ref, prev_ref, q_ref, kv_ref, ctx_ref, probs_ref = refs[:6]
    w_all, x_all, stage, sems = refs[-4:]
    rows, total = q_ref.shape[1], x_all.shape[0]

    @pl.when(pl.program_id(0) == 0)
    def _():
        if assemble:
            load_qkv(table_ref, piece_refs, w_all, vec_ref, b_ref, stage, sems)
            pltpu.make_async_copy(w_all, w_ref, sems.at[1]).start()
        else:
            pltpu.make_async_copy(piece_refs[0], w_all, sems.at[0]).start()
            wait_whole(w_all, sems.at[0])

    for j in range(4):
        start = pl.multiple_of(order_ref[j] * rows, rows)
        x_all[pl.ds(start, rows), :] = x_refs[j][0]
    valid = len_ref[first + pl.program_id(0)]
    key_pos = lax.broadcasted_iota(jnp.int32, (1, total), 1)
    padding = jnp.where(key_pos < valid, 0.0, -1e9)

    def project(g):
        width = 2 * PAIR
        cols = slice(g * width, (g + 1) * width)
        part = lambda n: slice(n * D + g * width, n * D + (g + 1) * width)
        query = (mm(x_refs[0][0], w_all[:, cols]) + vec_ref[0:1, cols]).astype(BF)
        q_ref[0, :, cols] = query * SCALE
        kv_ref[0, :, cols] = mm(x_all[...], w_all[:, part(1)]).astype(BF)
        value = mm(x_all[...], w_all[:, part(2)]) + vec_ref[1:2, cols]
        kv_ref[0, :, part(1)] = value.astype(BF)

    def score(i):
        cols = slice(i * PAIR, (i + 1) * PAIR)
        raw = mm_nt(stack_heads(q_ref[0, :, cols]), kv_ref[0, :, cols])
        prev = prev_ref[0, 2 * i : 2 * i + 2].reshape(2 * rows, total).astype(F32)
        return raw + (prev + padding)

    def mix(i, raw):
        cols = slice(i * PAIR, (i + 1) * PAIR)
        vcols = slice(D + i * PAIR, D + (i + 1) * PAIR)
        largest = jnp.max(raw, -1, keepdims=True)
        expo = jnp.exp(raw - largest)
        summed = jnp.sum(expo, -1, keepdims=True)
        probs = (expo * (1.0 / summed)).astype(BF)
        probs_ref[0, 2 * i : 2 * i + 2] = probs.reshape(2, rows, total)
        ctx_ref[0, :, cols] = pick_heads(mm(probs, kv_ref[0, :, vcols])).astype(BF)

    project(0)
    raw = score(0)
    for i in range(PAIRS):
        if i % 2 == 0 and i + 2 < PAIRS:
            project(i // 2 + 1)
        later = score(i + 1) if i + 1 < PAIRS else None
        mix(i, raw)
        raw = later

    if assemble:

        @pl.when(pl.program_id(0) == pl.num_programs(0) - 1)
        def _():
            pltpu.make_async_copy(w_all, w_ref, sems.at[1]).wait()


def lead(table, order, lengths, x_blocks, starts, seqs, first, pieces, prev_logits, vec=None):
    assemble = vec is None
    rows = x_blocks[0].shape[1]
    total = prev_logits.shape[-1]
    ff = 4 * D

    def x_spec(j):
        return pl.BlockSpec((1, rows, D), lambda b, *_: (starts[j] + b, 0, 0))

    fixed = lambda *shape: pl.BlockSpec(shape, lambda b, *_: (0, 0))
    row_spec = pl.BlockSpec((1, rows, D), lambda b, *_: (b, 0, 0))
    sds = jax.ShapeDtypeStruct
    out_specs = [
        row_spec,
        pl.BlockSpec((1, total, 2 * D), lambda b, *_: (b, 0, 0)),
        row_spec,
        pl.BlockSpec((1, HEADS, rows, total), lambda b, *_: (b, 0, 0, 0)),
    ]
    out_shape = [
        sds((seqs, rows, D), BF),
        sds((seqs, total, 2 * D), BF),
        sds((seqs, rows, D), BF),
        sds((seqs, HEADS, rows, total), BF),
    ]
    if assemble:
        out_specs += [ANY, fixed(8, D), fixed(1, ff)]
        out_shape += [sds((D, 3 * D), BF), sds((8, D), F32), sds((1, ff), F32)]
    stage = (4, 8 * (D // 8 + PAD), 3 * D // 4) if assemble else (1, PAD, 128)
    return pl.pallas_call(
        functools.partial(lead_kernel, len(pieces), assemble, first),
        grid_spec=pltpu.PrefetchScalarGridSpec(
            num_scalar_prefetch=3,
            grid=(seqs,),
            in_specs=[x_spec(j) for j in range(4)]
            + [ANY] * len(pieces)
            + ([] if assemble else [fixed(8, D)])
            + [
                pl.BlockSpec(
                    (1, HEADS, rows, total), lambda b, *_: (first + b, 0, 0, 0)
                )
            ],
            out_specs=out_specs,
            scratch_shapes=[
                pltpu.VMEM((D, 3 * D), BF),
                pltpu.VMEM((total, D), BF),
                pltpu.VMEM(stage, BF),
                pltpu.SemaphoreType.DMA((2,)),
            ],
        ),
        out_shape=out_shape,
        compiler_params=pltpu.CompilerParams(vmem_limit_bytes=GRANT),
        cost_estimate=pl.CostEstimate(
            flops=seqs * rows * D * (18 * D + 4 * total),
            bytes_accessed=seqs * 8 * MIB,
            transcendentals=seqs * HEADS * rows * total,
        ),
    )(table, order, lengths, *x_blocks, *pieces, *([] if assemble else [vec]), prev_logits)


def attend_back_kernel(order_ref, q_ref, kv_ref, probs_ref, dctx_ref, *refs):
    dlogits_ref, dq_ref, *dkv_refs, dkv_all = refs[-7:]
    rows = q_ref.shape[1]
    total = dkv_all.shape[0]

    def ahead(i):
        cols = slice(i * PAIR, (i + 1) * PAIR)
        vcols = slice(D + i * PAIR, D + (i + 1) * PAIR)
        dctx = stack_heads(dctx_ref[0, :, cols])
        return dctx, mm_nt(dctx, kv_ref[0, :, vcols])

    dctx, dprobs = ahead(0)
    for i in range(PAIRS):
        later = ahead(i + 1) if i + 1 < PAIRS else (None, None)
        cols = slice(i * PAIR, (i + 1) * PAIR)
        vcols = slice(D + i * PAIR, D + (i + 1) * PAIR)
        probs = probs_ref[0, 2 * i : 2 * i + 2].reshape(2 * rows, total)
        dkv_all[:, vcols] = mm_tn(probs, dctx).astype(BF)
        wide = probs.astype(F32)
        prod = wide * dprobs
        weighted = jnp.sum(prod, -1, keepdims=True)
        dlogits = (prod - wide * weighted).astype(BF)
        dlogits_ref[0, 2 * i : 2 * i + 2] = dlogits.reshape(2, rows, total)
        dq_ref[0, :, cols] = (pick_heads(mm(dlogits, kv_ref[0, :, cols])) * SCALE).astype(BF)
        dkv_all[:, cols] = mm_tn(dlogits, stack_heads(q_ref[0, :, cols])).astype(BF)
        dctx, dprobs = later
    for j in range(4):
        start = pl.multiple_of(order_ref[j] * rows, rows)
        dkv_refs[j][0] = dkv_all[pl.ds(start, rows), :]


def attend_back(order, queries, keys_values, probs, dctx, dlogits, first, seqs_all, deps=()):
    seqs, rows, _ = queries.shape
    blocks = 4
    total = probs.shape[-1]
    row_spec = lambda width: pl.BlockSpec((1, rows, width), lambda b, *_: (b, 0, 0))
    late_spec = lambda width: pl.BlockSpec((1, rows, width), lambda b, *_: (first + b, 0, 0))
    head_spec = pl.BlockSpec((1, HEADS, rows, total), lambda b, *_: (b, 0, 0, 0))
    late_head = pl.BlockSpec((1, HEADS, rows, total), lambda b, *_: (first + b, 0, 0, 0))
    more = ([] if dlogits is None else [dlogits]) + list(deps)
    outs = pl.pallas_call(
        attend_back_kernel,
        grid_spec=pltpu.PrefetchScalarGridSpec(
            num_scalar_prefetch=1,
            grid=(seqs,),
            in_specs=[
                row_spec(D),
                pl.BlockSpec((1, total, 2 * D), lambda b, *_: (b, 0, 0)),
                head_spec,
                late_spec(D),
            ]
            + [ANY] * len(more),
            out_specs=[late_head, row_spec(D)] + [row_spec(2 * D)] * blocks,
            scratch_shapes=[pltpu.VMEM((total, 2 * D), BF)],
        ),
        out_shape=[
            jax.ShapeDtypeStruct((seqs_all, HEADS, rows, total), BF),
            jax.ShapeDtypeStruct(queries.shape, BF),
        ]
        + [jax.ShapeDtypeStruct((seqs, rows, 2 * D), BF)] * blocks,
        input_output_aliases={} if dlogits is None else {5: 0},
        compiler_params=pltpu.CompilerParams(vmem_limit_bytes=GRANT),
        cost_estimate=pl.CostEstimate(
            flops=8 * seqs * HEADS * rows * total * PAIR,
            bytes_accessed=4 * seqs * HEADS * rows * total,
            transcendentals=0,
        ),
    )(order, queries, keys_values, probs, dctx, *more)
    dkv = [b.reshape(seqs * rows, 2 * D) for b in outs[2:]]
    return outs[0], outs[1].reshape(seqs * rows, D), dkv


def gelu_and_slope(values):
    cdf = 0.5 * lax.erf(values * 0.7071067811865476) + 0.5
    bell = jnp.exp(values * values * -0.5)
    return values * cdf, cdf + values * bell * 0.3989422804014327


def norm(values):
    average = jnp.mean(values, -1, keepdims=True)
    centred = values - average
    inverse = lax.rsqrt(jnp.mean(centred * centred, -1, keepdims=True) + 1e-06)
    return centred * inverse, inverse


def norm_back(grad, normed, inverse):
    first = jnp.mean(grad, -1, keepdims=True)
    second = jnp.mean(grad * normed, -1, keepdims=True)
    return inverse * (grad - first - normed * second)


def load_middle(table_ref, down_table_ref, in_refs, down_refs, w_out_ref, w_in_ref, w_down_ref, stage, sems):
    if len(in_refs) == 1:
        ff = w_in_ref.shape[1]
        pltpu.make_async_copy(down_refs[1], w_out_ref, sems.at[0]).start()
        for c in range(4):
            cols = pl.ds(c * (ff // 4), ff // 4)
            pltpu.make_async_copy(
                in_refs[0].at[:, cols], w_in_ref.at[:, cols], sems.at[1 + c]
            ).start()
            pltpu.make_async_copy(
                down_refs[0].at[:, cols], w_down_ref.at[:, cols], sems.at[5 + c]
            ).start()
        wait_whole(w_out_ref, sems.at[0])
    else:
        down = w_down_ref.shape[0] // 4
        wide = w_down_ref.shape[1] // 8
        high, half = D // 8, D // 16
        for piece, dp, seq in pieces_of(down_refs, down_table_ref):
            pltpu.make_async_copy(
                piece.at[pl.ds(down, half)], stage.at[seq, dp], sems.at[0]
            ).start()
        for piece, dp, seq in pieces_of(in_refs, table_ref):
            rows = pl.ds(pl.multiple_of(dp * high, high), high)
            cols = pl.ds(pl.multiple_of(seq * D, D), D)
            pltpu.make_async_copy(piece, w_in_ref.at[rows, cols], sems.at[1 + seq]).start()
        for piece, dp, seq in pieces_of(down_refs, down_table_ref):
            rows = pl.ds(pl.multiple_of(seq * down, down), down)
            cols = pl.ds(pl.multiple_of(dp * wide, wide), wide)
            pltpu.make_async_copy(
                piece.at[pl.ds(0, down)], w_down_ref.at[rows, cols], sems.at[5 + (dp >> 1)]
            ).start()
        wait_whole(stage, sems.at[0])
        for s in range(4):
            for d in range(8):
                cols = slice(s * down, (s + 1) * down)
                w_out_ref[d * high : d * high + half, cols] = stage[s, d][:, :down]
                w_out_ref[d * high + half : (d + 1) * high, cols] = stage[s, d][:, down:]


def middle_kernel(
    counts, fused, table_ref, down_table_ref, where_ref, x_ref, ctx_a_ref, ctx_b_ref, cot_ref,
    vec_ref, b_in_ref, *refs
):
    in_refs, refs = refs[: counts[0]], refs[counts[0] :]
    down_refs, refs = refs[: counts[1]], refs[counts[1] :]
    out_ref, dh1_ref, dctx_ref, dinner_ref, y1_ref, dvec_ref, db_in_ref = refs[:7]
    if fused:
        send_ref, keep_ref, act_all, dbranch_all, dattn_all, ctx_all, grad_out = refs[7:14]
    else:
        act_all, dbranch_all, dattn_all = refs[7:10]
    w_out_ref, w_in_ref, w_down_ref, stage, sems = refs[-5:]
    step = pl.program_id(0)
    rows = x_ref.shape[0]
    parts = pl.num_programs(0) - (4 if fused else 0)

    def token_rows():
        middle_rows(
            parts, table_ref, down_table_ref, x_ref, ctx_a_ref, ctx_b_ref, cot_ref, vec_ref,
            b_in_ref, in_refs, down_refs, out_ref, dh1_ref, dctx_ref, dinner_ref, y1_ref,
            dvec_ref, db_in_ref, act_all, dbranch_all, dattn_all, ctx_all if fused else None,
            w_out_ref, w_in_ref, w_down_ref, stage, sems,
        )

    if not fused:
        token_rows()
        return

    pl.when(step < parts)(token_rows)

    @pl.when(step == parts)
    def _():
        grad_out[...] = mm_tn(ctx_all[...], dattn_all[...]).astype(BF)

    @pl.when(step >= parts)
    def _():
        grad_down(where_ref, step - parts, dbranch_all, act_all, grad_out, send_ref, keep_ref)


def grad_down(where_ref, step, dbranch_ref, act_ref, grad_out, send_ref, keep_ref):
    y, x, core = where_ref[1], where_ref[2], where_ref[3]
    wide, down = D // 2, D // 4
    high, half = D // 8, D // 16
    first = core == 0

    def put(far_y, far_x, rows, cols, even, odd):
        keep_ref[far_y, far_x, 0, rows, cols] = jnp.where(first, even, odd)
        send_ref[far_y, far_x, 0, rows, cols] = jnp.where(first, odd, even)

    cols = pl.ds(pl.multiple_of(step * D, D), D)
    grad = mm_tn(dbranch_ref[...], act_ref[:, cols]).astype(BF)
    for j in range(2):
        top = pl.multiple_of((2 * step + j) * high, high)
        upper, lower = grad_out[pl.ds(top, half), :], grad_out[pl.ds(top + half, half), :]
        for i in range(2):
            pair = [slice((2 * i + k) * down, (2 * i + k + 1) * down) for k in range(2)]
            side = slice(j * wide, (j + 1) * wide)
            far = (y ^ j, x ^ i)
            put(*far, slice(0, down), slice(None), grad[pair[0], side], grad[pair[1], side])
            tail = slice(down, down + half)
            put(*far, tail, slice(0, down), upper[:, pair[0]], upper[:, pair[1]])
            put(*far, tail, slice(down, 2 * down), lower[:, pair[0]], lower[:, pair[1]])


def middle_rows(
    parts, table_ref, down_table_ref, x_ref, ctx_a_ref, ctx_b_ref, cot_ref, vec_ref,
    b_in_ref, in_refs, down_refs, out_ref, dh1_ref, dctx_ref, dinner_ref, y1_ref,
    dvec_ref, db_in_ref, act_all, dbranch_all, dattn_all, ctx_all,
    w_out_ref, w_in_ref, w_down_ref, stage, sems,
):
    step, rows = pl.program_id(0), x_ref.shape[0]
    here = pl.ds(pl.multiple_of(step * rows, rows), rows)

    @pl.when(step == 0)
    def _():
        load_middle(
            table_ref, down_table_ref, in_refs, down_refs,
            w_out_ref, w_in_ref, w_down_ref, stage, sems,
        )
        dvec_ref[...] = jnp.zeros_like(dvec_ref)
        db_in_ref[...] = jnp.zeros_like(db_in_ref)

    vec = lambda i: vec_ref[i : i + 1, :]
    total = lambda v: jnp.sum(v, 0, keepdims=True)
    wide = act_all.shape[1] // 4

    def arrived(ref, cols, sem):
        @pl.when(step == 0)
        def _():
            wait_whole(ref.at[:, cols], sems.at[sem])

    ctx = jnp.where(step < parts // 2, ctx_a_ref[...], ctx_b_ref[...])
    if ctx_all is not None:
        ctx_all[here, :] = ctx
    h1 = x_ref[...].astype(F32) + (mm(ctx, w_out_ref[...]) + vec(2))
    normed1, inverse1 = norm(h1)
    y1 = normed1 * vec(3) + vec(4)
    y1_low = y1.astype(BF)
    y1_ref[...] = y1_low
    h2 = y1 + vec(5)
    slopes = []
    for c in range(4):
        cols = slice(c * wide, (c + 1) * wide)
        arrived(w_in_ref, pl.ds(c * wide, wide), 1 + c)
        arrived(w_down_ref, pl.ds(c * wide, wide), 5 + c)
        inner = mm(y1_low, w_in_ref[:, cols]) + b_in_ref[:, cols]
        act, slope = gelu_and_slope(inner)
        act = act.astype(BF)
        act_all[here, cols] = act
        slopes.append(slope)
        h2 = h2 + mm_nt(act, w_down_ref[:, cols])
    normed2, inverse2 = norm(h2)
    out_ref[...] = (normed2 * vec(6) + vec(7)).astype(BF)
    cot = cot_ref[...].astype(F32)
    dh2 = norm_back(cot * vec(6), normed2, inverse2)
    dbranch = dh2.astype(BF)
    dbranch_all[here, :] = dbranch
    dvec_ref[5:6, :] += total(dbranch.astype(F32))
    dvec_ref[6:7, :] += total(cot * normed2)
    dvec_ref[7:8, :] += total(cot)
    dy1 = dh2
    for c in range(4):
        cols = slice(c * wide, (c + 1) * wide)
        dinner = (mm(dbranch, w_down_ref[:, cols]) * slopes[c]).astype(BF)
        dinner_ref[:, cols] = dinner
        db_in_ref[:, cols] += total(dinner.astype(F32))
        dy1 = dy1 + mm_nt(dinner, w_in_ref[:, cols])
    dh1 = norm_back(dy1 * vec(3), normed1, inverse1)
    dh1_ref[...] = dh1
    dattn = dh1.astype(BF)
    dattn_all[here, :] = dattn
    dctx_ref[...] = mm_nt(dattn, w_out_ref[...]).astype(BF)
    dvec_ref[2:3, :] += total(dattn.astype(F32))
    dvec_ref[3:4, :] += total(dy1 * normed1)
    dvec_ref[4:5, :] += total(dy1)


def middle(table, down_table, x, ctx_a, ctx_b, cot, vectors, b_in, in_pieces, down_pieces, where=None):
    tokens = x.shape[0]
    ff = b_in.shape[1]
    step = 256
    parts = tokens // step
    half = parts // 2
    fused = where is not None
    late = lambda i: jnp.minimum(i, parts - 1)
    rows = lambda width: pl.BlockSpec((step, width), lambda i, *_: (late(i), 0))
    ctx_specs = [
        pl.BlockSpec((step, D), lambda i, *_: (jnp.minimum(i, half - 1), 0)),
        pl.BlockSpec((step, D), lambda i, *_: (jnp.clip(i - half, 0, half - 1), 0)),
    ]
    whole = lambda *shape: pl.BlockSpec(shape, lambda i, *_: (0, 0))
    sds = jax.ShapeDtypeStruct
    counts = (len(in_pieces), len(down_pieces))
    out_specs = [rows(D)] * 3 + [rows(ff), rows(D), whole(8, D), whole(1, ff)]
    out_shape = [
        sds((tokens, D), BF),
        sds((tokens, D), F32),
        sds((tokens, D), BF),
        sds((tokens, ff), BF),
        sds((tokens, D), BF),
        sds((8, D), F32),
        sds((1, ff), F32),
    ]
    scratch = []
    if fused:
        piece = (D // 4 + D // 16, ff // 8)
        spec = pl.BlockSpec(
            (2, 2, 1) + piece,
            lambda i, t, d, w: (0, 0, jnp.maximum(i - parts, 0) ^ w[0], 0, 0),
        )
        out_specs += [spec, spec]
        out_shape += [sds((2, 2, 4) + piece, BF)] * 2
        scratch = [pltpu.VMEM((tokens, ff), BF)] + [pltpu.VMEM((tokens, D), BF)] * 3
        scratch += [pltpu.VMEM((D, D), BF)]
    else:
        out_specs += [whole(tokens, ff), whole(tokens, D), whole(tokens, D)]
        out_shape += [sds((tokens, ff), BF), sds((tokens, D), BF), sds((tokens, D), BF)]
        where = jnp.zeros((4,), jnp.int32)
    return pl.pallas_call(
        functools.partial(middle_kernel, counts, fused),
        grid_spec=pltpu.PrefetchScalarGridSpec(
            num_scalar_prefetch=3,
            grid=(parts + 4 if fused else parts,),
            in_specs=[rows(D)]
            + ctx_specs
            + [rows(D), whole(8, D), whole(1, ff)]
            + [ANY] * sum(counts),
            out_specs=out_specs,
            scratch_shapes=scratch
            + [
                pltpu.VMEM((D, D), BF),
                pltpu.VMEM((D, ff), BF),
                pltpu.VMEM((D, ff), BF),
                pltpu.VMEM((4, 8, D // 16, ff // 8), BF),
                pltpu.SemaphoreType.DMA((9,)),
            ],
        ),
        out_shape=out_shape,
        compiler_params=pltpu.CompilerParams(vmem_limit_bytes=GRANT),
        cost_estimate=pl.CostEstimate(
            flops=tokens * (10 * D * ff + 6 * D * D),
            bytes_accessed=30 * MIB,
            transcendentals=2 * tokens * ff,
        ),
    )(table, down_table, where, x, ctx_a, ctx_b, cot, vectors, b_in, *in_pieces, *down_pieces)


def grad_in_kernel(where_ref, y1_ref, dinner_ref, *refs):
    send_ref, keep_ref = refs[-2:]
    z, y = where_ref[0], where_ref[1]
    step = pl.program_id(0)
    high = D // 8
    grad = mm_tn(y1_ref[...], dinner_ref[...]).astype(BF)

    def put(ref):
        for d in range(8):
            ref[0, y ^ (d & 1), (d >> 1) ^ z] = grad[d * high : (d + 1) * high]

    @pl.when(step < 2)
    def _():
        put(send_ref)

    @pl.when(step >= 2)
    def _():
        put(keep_ref)


def grad_in(where, y1, dinner, deps=()):
    tokens, ff = dinner.shape
    wide = ff // 4

    def columns(t, where):
        return (0, 2 * (where[2] ^ (t & 1)) + (where[3] ^ (1 - (t >> 1))))

    piece = (1, 2, 4, D // 8, wide)
    shape = jax.ShapeDtypeStruct((2, 2, 4, D // 8, wide), BF)
    return pl.pallas_call(
        grad_in_kernel,
        grid_spec=pltpu.PrefetchScalarGridSpec(
            num_scalar_prefetch=1,
            grid=(4,),
            in_specs=[
                pl.BlockSpec((tokens, D), lambda t, w: (0, 0)),
                pl.BlockSpec((tokens, wide), columns),
            ]
            + [ANY] * len(deps),
            out_specs=[
                pl.BlockSpec(piece, lambda t, w: (jnp.minimum(t, 1), 0, 0, 0, 0)),
                pl.BlockSpec(piece, lambda t, w: (jnp.maximum(t - 2, 0), 0, 0, 0, 0)),
            ],
        ),
        out_shape=[shape, shape],
        compiler_params=pltpu.CompilerParams(vmem_limit_bytes=GRANT),
        cost_estimate=pl.CostEstimate(
            flops=2 * tokens * D * ff, bytes_accessed=14 * MIB, transcendentals=0
        ),
    )(where, y1, dinner, *deps)


def grad_qkv_kernel(where_ref, x0_ref, *refs):
    x2_refs, refs = refs[:2], refs[2:]
    dq_refs, refs = refs[:2], refs[2:]
    own_refs, refs = refs[:4], refs[4:]
    far_refs, refs = refs[:4], refs[4:]
    dvec_ref, db_ref = refs[:2]
    *out_refs, grad, dvec = refs[-6:]
    z, y, x, core = (where_ref[i] for i in range(4))
    step = pl.program_id(0)
    wide, high = 3 * D // 4, D // 8
    cut = out_refs[0].shape[3]
    part = x2_refs[0].shape[0]
    x0 = lambda h: x0_ref[h * part : (h + 1) * part]

    @pl.when(step == 0)
    def _():
        total = mm_tn(x0(0), dq_refs[0][...]) + mm_tn(x0(1), dq_refs[1][...])
        grad[:, :D] = total.astype(BF)
        dvec[...] = dvec_ref[...]
        for ref in dq_refs:
            dvec[0:1, :] += jnp.sum(ref[...].astype(F32), 0, keepdims=True)

    def emit():
        first = core == 0
        for i in range(2):
            even = grad[:, 2 * i * wide : (2 * i + 1) * wide]
            odd = grad[:, (2 * i + 1) * wide : (2 * i + 2) * wide]
            kept = jnp.where(first, even, odd)
            sent = jnp.where(first, odd, even)
            for d in range(8):
                top, far_z = d * high, (d >> 1) ^ z
                upper = (y ^ (d & 1), x ^ i, far_z)
                lower = (x ^ i, y ^ (d & 1), far_z)
                extra = []
                for k in range(2):
                    s = 2 * i + k
                    own = dvec[2 * s : 2 * s + 2, d * high : (d + 1) * high]
                    at = (4 * d + s) * high
                    rest = jnp.zeros((PAD - 3, high), F32)
                    extra.append(jnp.concatenate([own, db_ref[0:1, at : at + high], rest], 0))
                tail = lower + (slice(high - cut, high - cut + PAD), slice(0, high))
                pairs = ((sent, extra[1], extra[0]), (kept, extra[0], extra[1]))
                for n, (part, one, other) in enumerate(pairs):
                    out_refs[n][upper] = part[top : top + cut]
                    out_refs[2 + n][lower + (slice(0, high - cut), slice(None))] = part[
                        top + cut : top + high
                    ]
                    out_refs[2 + n][tail] = jnp.where(first, one, other).astype(BF)

    for t in (1, 2):

        @pl.when(step == t)
        def _():
            total = None
            for h in range(2):
                own, far = (
                    low(add(refs[h][...], refs[2 + h][...])) for refs in (own_refs, far_refs)
                )
                if t == 2:
                    both = jnp.sum(own.astype(F32), 0, keepdims=True)
                    dvec[1:2, :] += both + jnp.sum(far.astype(F32), 0, keepdims=True)
                piece = mm_tn(x0(h), own) + mm_tn(x2_refs[h][...], far)
                total = piece if total is None else total + piece
            grad[:, t * D : (t + 1) * D] = total.astype(BF)
            if t == 2:
                emit()


def grad_qkv(where, x0, x2, dq, own, far, dvec, db_in, deps=()):
    tokens = x0.shape[0]
    fixed = lambda *shape: pl.BlockSpec(shape, lambda t, w: (0, 0))
    half = fixed(tokens // 2, D)
    part = pl.BlockSpec((tokens // 2, D), lambda t, w: (0, jnp.maximum(t - 1, 0)))
    cut = D // 12
    dims = [(2, 2, 4, rows, 3 * D // 4) for rows in (cut, D // 8 - cut + PAD) for _ in range(2)]
    return pl.pallas_call(
        grad_qkv_kernel,
        grid_spec=pltpu.PrefetchScalarGridSpec(
            num_scalar_prefetch=1,
            grid=(3,),
            in_specs=[fixed(tokens, D)]
            + [half] * 4
            + [part] * 8
            + [fixed(8, D)]
            + [fixed(*db_in.shape)]
            + [ANY] * len(deps),
            out_specs=[pl.BlockSpec(d, lambda t, w: (0, 0, 0, 0, 0)) for d in dims],
            scratch_shapes=[pltpu.VMEM((D, 3 * D), BF), pltpu.VMEM((8, D), F32)],
        ),
        out_shape=[jax.ShapeDtypeStruct(d, BF) for d in dims],
        compiler_params=pltpu.CompilerParams(vmem_limit_bytes=GRANT),
        cost_estimate=pl.CostEstimate(
            flops=2 * tokens * D * 5 * D, bytes_accessed=16 * MIB, transcendentals=0
        ),
    )(where, x0, *x2, *dq, *own, *far, dvec, db_in, *deps)


def grad_far_kernel(dkv_ref, got_ref, w_ref, *refs):
    total = low(add(dkv_ref[...], got_ref[...]))
    refs[-1][...] = mm_nt(total, w_ref[:, D:]).astype(BF)


def grad_far(dkv, got, w_qkv, deps=()):
    tokens = dkv.shape[0]
    step = 256
    rows = lambda width: pl.BlockSpec((step, width), lambda i: (i, 0))
    return pl.pallas_call(
        grad_far_kernel,
        grid=(tokens // step,),
        in_specs=[
            rows(2 * D),
            rows(2 * D),
            pl.BlockSpec((D, 3 * D), lambda i: (0, 0), pipeline_mode=pl.Buffered(1)),
        ]
        + [ANY] * len(deps),
        out_specs=rows(D),
        out_shape=jax.ShapeDtypeStruct((tokens, D), BF),
        compiler_params=pltpu.CompilerParams(vmem_limit_bytes=GRANT),
        cost_estimate=pl.CostEstimate(
            flops=2 * tokens * D * 2 * D, bytes_accessed=10 * MIB, transcendentals=0
        ),
    )(dkv, got, w_qkv, *deps)


def grad_own_kernel(*refs):
    dkv_refs, refs = refs[:2], refs[2:]
    got_refs, refs = refs[:2], refs[2:]
    dq_refs, refs = refs[:2], refs[2:]
    dh1_ref, w_ref = refs[:2]
    dx_ref = refs[-1]
    early = pl.program_id(0) < pl.num_programs(0) // 2
    pick = lambda pair: jnp.where(early, pair[0][...], pair[1][...])
    total = (pick(dkv_refs).astype(F32) + pick(got_refs).astype(F32)).astype(BF)
    dx = mm_nt(total, w_ref[:, D:]) + mm_nt(pick(dq_refs), w_ref[:, :D])
    dx_ref[...] = dx + dh1_ref[...]


def grad_own(dkv, got, dq, dh1, w_qkv, deps=()):
    tokens = dh1.shape[0]
    step = 256
    half = tokens // step // 2

    def pair(width):
        return [
            pl.BlockSpec((step, width), lambda i: (jnp.minimum(i, half - 1), 0)),
            pl.BlockSpec((step, width), lambda i: (jnp.maximum(i - half, 0), 0)),
        ]

    rows = pl.BlockSpec((step, D), lambda i: (i, 0))
    return pl.pallas_call(
        grad_own_kernel,
        grid=(tokens // step,),
        in_specs=pair(2 * D)
        + pair(2 * D)
        + pair(D)
        + [rows, pl.BlockSpec((D, 3 * D), lambda i: (0, 0), pipeline_mode=pl.Buffered(1))]
        + [ANY] * len(deps),
        out_specs=rows,
        out_shape=jax.ShapeDtypeStruct((tokens, D), F32),
        compiler_params=pltpu.CompilerParams(vmem_limit_bytes=GRANT),
        cost_estimate=pl.CostEstimate(
            flops=2 * tokens * D * 3 * D, bytes_accessed=20 * MIB, transcendentals=0
        ),
    )(*dkv, *got, *dq, dh1, w_qkv, *deps)


def gather_small(b_in, vectors):
    dp, seq = lax.axis_size("dp"), lax.axis_size("seq")
    small = jnp.concatenate([vectors.reshape(-1), b_in])
    whole = lax.all_gather(small, BOTH, axis=0, tiled=False)
    nv = vectors.size
    vec = whole[:, :nv].reshape((dp, seq) + vectors.shape).transpose(1, 2, 0, 3)
    return whole[:, nv:].reshape(1, -1), vec.reshape(8, D)


def reduce_small(g_b, g_vec):
    dp, seq = lax.axis_size("dp"), lax.axis_size("seq")
    vec = g_vec.reshape(seq, 8 // seq, dp, D // dp).transpose(2, 0, 1, 3)
    small = jnp.concatenate([vec.reshape(dp * seq, -1), g_b.reshape(dp * seq, -1)], 1)
    mine = lax.psum_scatter(small, BOTH, scatter_dimension=0, tiled=True)[0]
    nv = 8 * D // (dp * seq)
    return mine[nv:], mine[:nv].reshape(8 // seq, D // dp)


def gather_plain(w_qkv, w_out, w_in, w_down_t):
    both = lambda a, first, second: lax.all_gather(
        lax.all_gather(a, first, axis=0, tiled=True), second, axis=1, tiled=True
    )
    return (
        [both(w_qkv, "dp", "seq")],
        [both(w_in, "dp", "seq")],
        [both(w_down_t, "seq", "dp"), both(w_out, "dp", "seq")],
    )


def reduce_plain(a, first, second):
    part = lax.psum_scatter(a.astype(BF), first, scatter_dimension=0, tiled=True)
    return lax.psum_scatter(part, second, scatter_dimension=1, tiled=True).astype(F32)


def together(*parts):
    return lax.optimization_barrier(parts)


def forward_apart(order, lengths, table, x0, prev_logits, weights):
    w_qkv, w_out, w_in, w_down, b_in, vectors = weights
    seqs = x0.shape[0]
    half = seqs // 2
    cut = w_out.shape[0] // 2
    turned = jnp.concatenate([w_out[:cut], w_out[cut:]], 1)
    down = jnp.concatenate([w_down.T, turned], 0)
    down_x = swap_x(down)
    few = half // 2
    x2_a = swap_x(x0[:few])
    small = jnp.concatenate([vectors, b_in.reshape(1, -1)], 0)
    small = jnp.pad(small, ((0, PAD - small.shape[0]), (0, w_qkv.shape[1] - small.shape[1])))
    qkv = stack_z_direct(jnp.concatenate([w_qkv, small], 0))
    qkv, w_in, x_late, x_b, x_all, down, down_x, x2_a = together(
        qkv, w_in, x0[few:half], x0[half:], x0, down, down_x, x2_a
    )

    qkv_x, qkv_y = swap_x(qkv), swap_y(qkv)
    down = jnp.stack([down, down_x])
    down_y = swap_y(down)
    x2_late = swap_x(x_late)
    in_pair = jnp.stack([w_in, swap_z(w_in, 1)])
    in_got = swap_z(in_pair, 2)
    qkv, qkv_x, qkv_y, x2_late, x_all, in_pair, in_got, x_b, down, down_y = together(
        qkv, qkv_x, qkv_y, x2_late, x_all, in_pair, in_got, x_b, down, down_y
    )
    x2_a = jnp.concatenate([x2_a, x2_late], 0)

    qkv_xy, x2_b = swap_y(qkv_x), swap_x(x_b)
    x1, x3_a, qkv_far = swap_core(x_all), swap_core(x2_a), swap_core(qkv)
    down = [jnp.concatenate([down, down_y], 0)]
    down.append(turn_z(down[0]))
    qkv_xy, x2_b, x1, x3_a, qkv_far, *down = together(qkv_xy, x2_b, x1, x3_a, qkv_far, *down)
    in_own = jnp.concatenate([in_pair, in_got], 0)
    qkv_near = [qkv, qkv_x, qkv_y, qkv_xy]
    qkv_pieces = qkv_near + [qkv_far] + [swap_core(a) for a in qkv_near[1:]]

    in_x, in_y, x3_b = swap_x(in_own), swap_y(in_own), swap_core(x2_b)
    down.append(turn_z(down[1]))
    q_a, kv_a, ctx_a, probs_a, f_qkv, f_vec, f_b = lead(
        table, order, lengths, (x0, x1, x2_a, x3_a), (0, 0, 0, 0), half, 0,
        qkv_pieces, prev_logits,
    )
    in_own, in_x, in_y, x3_b, f_qkv, ctx_a, f_b, *down = together(
        in_own, in_x, in_y, x3_b, f_qkv, ctx_a, f_b, *down
    )

    in_xy = swap_y(in_x)
    in_far = [swap_core(a) for a in (in_own, in_x, in_y)]
    down_far = [swap_core(a) for a in down]
    down.append(turn_z(down[2]))
    q_b, kv_b, ctx_b, probs_b = lead(
        table, order, lengths, (x0, x1, x2_b, x3_b), (half, half, 0, 0), half, half,
        [f_qkv], prev_logits, f_vec,
    )
    in_xy, ctx_b, *both = together(in_xy, ctx_b, *in_far, *down_far, *down)
    in_far, down_far, down = both[:3], both[3:6], both[6:]

    in_pieces = [in_own, in_x, in_y, in_xy] + in_far + [swap_core(in_xy)]
    down_pieces = down + down_far + [swap_core(down[3])]
    first, second = (q_a, kv_a, ctx_a, probs_a), (q_b, kv_b, ctx_b, probs_b)
    return first, second, f_qkv, f_vec, f_b, in_pieces, down_pieces, [x2_a, x2_b]


def shards_apart(
    hidden_states, prev_logits, lengths, w_qkv, w_out, w_in, w_down, b_in, vectors, cotangent
):
    seqs, rows, _ = hidden_states.shape
    tokens = seqs * rows
    half = seqs // 2
    order = jnp.arange(4, dtype=jnp.int32) ^ lax.axis_index("seq")
    table, down_table = piece_table(), turned_table()
    where = jnp.stack(place()).astype(jnp.int32)
    x0 = hidden_states.reshape(tokens, D)
    first, second, f_qkv, f_vec, f_b, in_pieces, down_pieces, x2 = forward_apart(
        order, lengths, table, hidden_states, prev_logits,
        (w_qkv, w_out, w_in, w_down, b_in, vectors),
    )
    rows_of = lambda a: a.reshape(-1, D)
    ctx, x2 = [rows_of(first[2]), rows_of(second[2])], [rows_of(a) for a in x2]
    out, dh1, dctx, dinner, y1, dvec, db_in, d_send, d_keep = middle(
        table, down_table, x0, *ctx, cotangent.reshape(tokens, D), f_vec, f_b,
        in_pieces, down_pieces, where,
    )
    dctx = dctx.reshape(seqs, rows, D)

    d_core = swap_core(d_send)
    i_send, i_keep = grad_in(where, y1, dinner, [d_keep])
    i_core = swap_core(i_send)
    d_core = after(d_core, i_keep)
    d_sent = low(add(d_keep[1], d_core[1]))
    d_one = swap_y(d_sent)
    i_core = after(i_core, d_sent)
    i_sent = low(add(i_keep[1], i_core[1]))
    i_one = swap_x(i_sent)
    dlogits, dq_a, dkv_a = attend_back(
        order, first[0], first[1], first[3], dctx, None, 0, seqs, [d_sent, i_sent]
    )
    far_a, own_a = swap_core(dkv_a[3]), swap_core(dkv_a[1])
    dlogits, dq_b, dkv_b = attend_back(
        order, second[0], second[1], second[3], dctx, dlogits, half, seqs, [dq_a]
    )
    far_b, own_b = swap_core(dkv_b[3]), swap_core(dkv_b[1])
    far_a, own_a = after(far_a, dq_b), after(own_a, dq_b)
    d_one, i_one = after(d_one, dq_b), after(i_one, dq_b)
    d_sent = low(add(d_keep[0, 1], d_core[0, 1], d_one[1]))
    d_two = swap_x(d_sent)
    i_sent = low(add(i_keep[0, 1], i_core[0, 1], i_one[1]))
    i_two = swap_y(i_sent)
    dq, own, far = [dq_a, dq_b], [dkv_a[0], dkv_b[0], own_a, own_b], [dkv_a[2], dkv_b[2], far_a, far_b]
    a_send, a_keep, b_send, b_keep = grad_qkv(where, x0, x2, dq, own, far, dvec, db_in, [d_sent, i_sent])
    d_two, i_two, a_send, b_send = together(d_two, i_two, a_send, b_send)
    a_core, b_core = swap_core(a_send), swap_core(b_send)
    d_part = lambda k: add(d_keep[0, 0, k], d_core[0, 0, k], d_one[0, k], d_two[k])
    i_part = lambda k: add(i_keep[0, 0, k], i_core[0, 0, k], i_one[0, k], i_two[k])
    upper, lower = slice(2, 4), slice(0, 2)
    d_sent, i_sent = low(d_part(upper)), low(i_part(upper))
    i_far, d_far = swap_z(i_sent, 2), swap_z(d_sent, 2)
    a_core, b_core = after(a_core, d_sent, i_sent), after(b_core, d_sent, i_sent)
    a_sent, b_sent = low(add(a_keep[1], a_core[1])), low(add(b_keep[1], b_core[1]))
    a_one, b_one = swap_y(a_sent), swap_x(b_sent)
    dx2_a = grad_far(far[0], far[2], f_qkv, [a_sent, b_sent])
    got_a = swap_x(dx2_a)
    dx2_b = grad_far(far[1], far[3], f_qkv, [dx2_a])
    dx = grad_own(own[:2], own[2:], dq, dh1, f_qkv, [dx2_b])
    a_one, b_one, dx, dx2_b = together(a_one, b_one, dx, dx2_b)
    a_sent = low(add(a_keep[0, 1], a_core[0, 1], a_one[1]))
    b_sent = low(add(b_keep[0, 1], b_core[0, 1], b_one[1]))
    a_two, b_two = swap_x(a_sent), swap_y(b_sent)
    got_b = swap_x(after(dx2_b, a_sent))
    i_far, d_far = after(i_far, a_sent, b_sent), after(d_far, a_sent, b_sent)
    i_last = i_part(lower) + i_far.astype(F32)
    i_end = swap_z(low(i_last[1]), 1)
    d_last = d_part(lower) + d_far.astype(F32)
    d_end = swap_z(low(d_last[1]), 1)
    a_two, b_two, i_last, d_last, got_a = together(a_two, b_two, i_last, d_last, got_a)
    a_part = lambda k: add(a_keep[0, 0, k], a_core[0, 0, k], a_one[0, k], a_two[k])
    b_part = lambda k: add(b_keep[0, 0, k], b_core[0, 0, k], b_one[0, k], b_two[k])
    q_part = lambda k: jnp.concatenate([a_part(k), b_part(k)], 0)
    q_sent = [low(q_part(k)) for k in range(1, 4)]
    q_far = [swap_z(q, k) for q, k in zip(q_sent, range(1, 4))]
    i_end, d_end, dx = after((i_end, d_end, dx), *q_sent)
    o_in = i_last[0] + i_end.astype(F32)
    o_low = d_last[0] + d_end.astype(F32)
    o_top = q_part(0) + add(*q_far)
    got_b = after(got_b, o_top)
    grad_hidden = low(dx + jnp.concatenate([got_a, got_b], 0).astype(F32))
    down, cut, (extra, high) = w_down.shape[1], w_qkv.shape[0], vectors.shape
    shape = hidden_states.shape
    return (
        out.reshape(shape),
        grad_hidden.reshape(shape),
        dlogits,
        o_top[:cut],
        jnp.concatenate([o_low[down:, :down], o_low[down:, down:]], 0),
        o_in,
        o_low[:down].T,
        o_top[cut + extra, : b_in.shape[0]],
        o_top[cut : cut + extra, :high],
    )


def shards_plain(
    hidden_states, prev_logits, lengths, w_qkv, w_out, w_in, w_down, b_in, vectors, cotangent
):
    seqs, rows, _ = hidden_states.shape
    tokens = seqs * rows
    order = jnp.arange(4, dtype=jnp.int32) ^ lax.axis_index("seq")
    half = seqs // 2
    x0 = hidden_states.reshape(tokens, D)
    x1, x2 = swap_core(hidden_states), swap_x(hidden_states)
    x_blocks = (hidden_states, x1, x2, swap_core(x2))
    table = down_table = jnp.zeros((2,), jnp.int32)
    qkv, in_pieces, down_pieces = gather_plain(w_qkv, w_out, w_in, w_down.T)
    f_qkv = qkv[0]
    f_b, f_vec = gather_small(b_in, vectors)
    f_b, f_vec = f_b.astype(F32), f_vec.astype(F32)
    made = [
        lead(
            table, order, lengths, x_blocks, (h * half,) * 4, half, h * half, qkv,
            prev_logits, f_vec,
        )
        for h in range(2)
    ]
    ctx = [m[2].reshape(-1, D) for m in made]
    out, dh1, dctx, dinner, y1, dvec, db_in, act, dbranch, dattn = middle(
        table, down_table, x0, *ctx, cotangent.reshape(tokens, D), f_vec, f_b, in_pieces, down_pieces
    )
    dctx = dctx.reshape(seqs, rows, D)
    dlogits, dq, dkv = None, [], []
    for h in range(2):
        dlogits, dq_h, dkv_h = attend_back(
            order, made[h][0], made[h][1], made[h][3], dctx, dlogits, h * half, seqs
        )
        dq.append(dq_h)
        dkv.append(dkv_h)
    got_far = [swap_core(dkv[h][3]) for h in range(2)]
    far = [grad_far(dkv[h][2], got_far[h], f_qkv) for h in range(2)]
    got_rows = [swap_x(f) for f in far]
    got_kv = [swap_core(dkv[h][1]) for h in range(2)]
    dkv0 = [dkv[h][0] for h in range(2)]
    dx = grad_own(dkv0, got_kv, dq, dh1, f_qkv)
    whole = lambda pair: jnp.concatenate(pair, 0)
    grad_hidden = low(dx + whole(got_rows).astype(F32))
    sum0 = whole([low(add(a, b)) for a, b in zip(dkv0, got_kv)])
    sum2 = whole([low(add(dkv[h][2], got_far[h])) for h in range(2)])
    dq = whole(dq)
    g_kv = mm_tn(x0, sum0) + mm_tn(x2.reshape(tokens, D), sum2)
    g_qkv = jnp.concatenate([mm_tn(x0, dq), g_kv], 1)
    dvec = dvec.at[0].add(jnp.sum(dq, 0, dtype=F32))
    dvec = dvec.at[1].add(jnp.sum(add(sum0[:, D:], sum2[:, D:]), 0))
    o_b, o_vec = reduce_small(db_in, dvec)
    shape = hidden_states.shape
    return (
        out.reshape(shape),
        grad_hidden.reshape(shape),
        dlogits,
        reduce_plain(g_qkv, "dp", "seq"),
        reduce_plain(mm_tn(whole(ctx), dattn), "dp", "seq"),
        reduce_plain(mm_tn(y1, dinner), "dp", "seq"),
        reduce_plain(mm_tn(act, dbranch), "dp", "seq"),
        o_b,
        o_vec,
    )


def shards(*args):
    return (shards_apart if by_pieces() else shards_plain)(*args)


def solution(mesh):
    return jax.shard_map(
        shards,
        mesh=mesh,
        in_specs=(
            P("dp", "seq", None),
            P("dp", None, "seq", None),
            P("dp"),
            P("dp", "seq"),
            P("dp", "seq"),
            P("dp", "seq"),
            P("dp", "seq"),
            P(("dp", "seq")),
            P("seq", "dp"),
            P("dp", "seq", None),
        ),
        out_specs=(
            P("dp", "seq", None),
            P("dp", "seq", None),
            P("dp", None, "seq", None),
            P("dp", "seq"),
            P("dp", "seq"),
            P("dp", "seq"),
            P("dp", "seq"),
            P(("dp", "seq")),
            P("seq", "dp"),
        ),
        check_vma=False,
    )
```

```python
import functools

import jax
import jax.numpy as jnp
from jax import lax
from jax.experimental import pallas as pl
from jax.experimental.pallas import tpu as pltpu
from jax.sharding import PartitionSpec as P

D = 768
HEADS = 12
HEAD_DIM = 64
PAIRS = HEADS // 2
PAIR = 2 * HEAD_DIM
SCALE = HEAD_DIM ** (-0.5)
BF = jnp.bfloat16
F32 = jnp.float32
BOTH = ("dp", "seq")
MIB = 1 << 20
PAD = 16
ANY = pl.BlockSpec(memory_space=pl.ANY)
GRANT = 60 * MIB


def mm(a, b):
    return lax.dot_general(a, b, (((1,), (0,)), ((), ())), preferred_element_type=F32)


def mm_nt(a, b):
    return lax.dot_general(a, b, (((1,), (1,)), ((), ())), preferred_element_type=F32)


def mm_tn(a, b):
    return lax.dot_general(a, b, (((0,), (0,)), ((), ())), preferred_element_type=F32)


def stack_heads(pair):
    lane = lax.broadcasted_iota(jnp.int32, pair.shape, 1)
    zero = jnp.zeros_like(pair)
    return jnp.concatenate(
        [jnp.where(lane < HEAD_DIM, pair, zero), jnp.where(lane < HEAD_DIM, zero, pair)], 0
    )


def pick_heads(stacked):
    rows = stacked.shape[0] // 2
    lane = lax.broadcasted_iota(jnp.int32, (rows, PAIR), 1)
    return jnp.where(lane < HEAD_DIM, stacked[:rows], stacked[rows:])


def swap(a, axis, bit):
    size = lax.axis_size(axis)
    return lax.ppermute(a, axis, [(i, i ^ bit) for i in range(size)])


def swap_core(a):
    return swap(a, "seq", 1)


def swap_x(a):
    return swap(a, "seq", 2)


def swap_y(a):
    return swap(a, "dp", 1)


def swap_z(a, places):
    return swap(a, "dp", 2 * places)


def turn_z(a):
    size = lax.axis_size("dp")
    return lax.ppermute(a, "dp", [(i, (i + 2) % size) for i in range(size)])


def by_pieces():
    return lax.axis_size("dp") == 8 and lax.axis_size("seq") == 4


def place():
    dp, seq = lax.axis_index("dp"), lax.axis_index("seq")
    return dp >> 1, dp & 1, seq >> 1, seq & 1


def stack_z_direct(a):
    return jnp.stack([a] + [swap_z(a, k) for k in range(1, 4)])


def piece_table():
    z, y, x, core = place()
    table = []
    for far in range(8):
        for k in range(4):
            table.append(2 * (z ^ k) + (y ^ (far >> 1 & 1)))
            table.append(2 * (x ^ (far & 1)) + (core ^ (far >> 2)))
    return jnp.stack(table).astype(jnp.int32)


def turned_table():
    z, y, x, core = place()
    table = []
    for far in range(8):
        for k in range(4):
            table.append(2 * ((z - (far & 3)) & 3) + (y ^ (k >> 1)))
            table.append(2 * (x ^ (k & 1)) + (core ^ (far >> 2)))
    return jnp.stack(table).astype(jnp.int32)


def pieces_of(refs, table_ref):
    for a, ref in enumerate(refs):
        depth = ref.shape[0]
        for k in range(depth):
            n = a * depth + k
            yield ref.at[k], table_ref[2 * n], table_ref[2 * n + 1]


def wait_whole(ref, sem):
    pltpu.make_async_copy(ref, ref, sem).wait()


def add(*parts):
    return sum(p.astype(F32) for p in parts)


def low(a):
    return a.astype(BF)


def after(a, *done):
    return lax.optimization_barrier((a,) + done)[0]


def load_qkv(table_ref, piece_refs, w_all, vec_ref, b_ref, stage, sems):
    high, wide = D // 8 + PAD, 3 * D // 4
    for piece, dp, seq in pieces_of(piece_refs, table_ref):
        rows = pl.ds(pl.multiple_of(dp * high, PAD), high)
        pltpu.make_async_copy(piece, stage.at[seq, rows], sems.at[0]).start()
    wait_whole(stage, sems.at[0])
    body, width = D // 8, D // 8
    for s in range(4):
        for d in range(8):
            top = d * high
            w_all[d * body : (d + 1) * body, s * wide : (s + 1) * wide] = stage[
                s, top : top + body
            ]
            extra = stage[s, top + body : top + high, :width].astype(F32)
            vec_ref[2 * s : 2 * s + 2, d * width : (d + 1) * width] = extra[0:2]
            place_of = (4 * d + s) * width
            b_ref[0:1, place_of : place_of + width] = extra[2:3]


def lead_kernel(count, assemble, first, table_ref, order_ref, len_ref, *refs):
    x_refs, refs = refs[:4], refs[4:]
    piece_refs, refs = refs[:count], refs[count:]
    if assemble:
        prev_ref, q_ref, kv_ref, ctx_ref, probs_ref, w_ref, vec_ref, b_ref = refs[:8]
    else:
        vec_ref, prev_ref, q_ref, kv_ref, ctx_ref, probs_ref = refs[:6]
    w_all, x_all, stage, sems = refs[-4:]
    rows, total = q_ref.shape[1], x_all.shape[0]

    @pl.when(pl.program_id(0) == 0)
    def _():
        if assemble:
            load_qkv(table_ref, piece_refs, w_all, vec_ref, b_ref, stage, sems)
            pltpu.make_async_copy(w_all, w_ref, sems.at[1]).start()
        else:
            pltpu.make_async_copy(piece_refs[0], w_all, sems.at[0]).start()
            wait_whole(w_all, sems.at[0])

    for j in range(4):
        start = pl.multiple_of(order_ref[j] * rows, rows)
        x_all[pl.ds(start, rows), :] = x_refs[j][0]
    valid = len_ref[first + pl.program_id(0)]
    key_pos = lax.broadcasted_iota(jnp.int32, (1, total), 1)
    padding = jnp.where(key_pos < valid, 0.0, -1e9)

    def project(g):
        width = 2 * PAIR
        cols = slice(g * width, (g + 1) * width)
        part = lambda n: slice(n * D + g * width, n * D + (g + 1) * width)
        query = (mm(x_refs[0][0], w_all[:, cols]) + vec_ref[0:1, cols]).astype(BF)
        q_ref[0, :, cols] = query * SCALE
        kv_ref[0, :, cols] = mm(x_all[...], w_all[:, part(1)]).astype(BF)
        value = mm(x_all[...], w_all[:, part(2)]) + vec_ref[1:2, cols]
        kv_ref[0, :, part(1)] = value.astype(BF)

    def score(i):
        cols = slice(i * PAIR, (i + 1) * PAIR)
        raw = mm_nt(stack_heads(q_ref[0, :, cols]), kv_ref[0, :, cols])
        prev = prev_ref[0, 2 * i : 2 * i + 2].reshape(2 * rows, total).astype(F32)
        return raw + (prev + padding)

    def mix(i, raw):
        cols = slice(i * PAIR, (i + 1) * PAIR)
        vcols = slice(D + i * PAIR, D + (i + 1) * PAIR)
        largest = jnp.max(raw, -1, keepdims=True)
        expo = jnp.exp(raw - largest)
        summed = jnp.sum(expo, -1, keepdims=True)
        probs = (expo * (1.0 / summed)).astype(BF)
        probs_ref[0, 2 * i : 2 * i + 2] = probs.reshape(2, rows, total)
        ctx_ref[0, :, cols] = pick_heads(mm(probs, kv_ref[0, :, vcols])).astype(BF)

    project(0)
    raw = score(0)
    for i in range(PAIRS):
        if i % 2 == 0 and i + 2 < PAIRS:
            project(i // 2 + 1)
        later = score(i + 1) if i + 1 < PAIRS else None
        mix(i, raw)
        raw = later

    if assemble:

        @pl.when(pl.program_id(0) == pl.num_programs(0) - 1)
        def _():
            pltpu.make_async_copy(w_all, w_ref, sems.at[1]).wait()


def lead(table, order, lengths, x_blocks, starts, seqs, first, pieces, prev_logits, vec=None):
    assemble = vec is None
    rows = x_blocks[0].shape[1]
    total = prev_logits.shape[-1]
    ff = 4 * D

    def x_spec(j):
        return pl.BlockSpec((1, rows, D), lambda b, *_: (starts[j] + b, 0, 0))

    fixed = lambda *shape: pl.BlockSpec(shape, lambda b, *_: (0, 0))
    row_spec = pl.BlockSpec((1, rows, D), lambda b, *_: (b, 0, 0))
    sds = jax.ShapeDtypeStruct
    out_specs = [
        row_spec,
        pl.BlockSpec((1, total, 2 * D), lambda b, *_: (b, 0, 0)),
        row_spec,
        pl.BlockSpec((1, HEADS, rows, total), lambda b, *_: (b, 0, 0, 0)),
    ]
    out_shape = [
        sds((seqs, rows, D), BF),
        sds((seqs, total, 2 * D), BF),
        sds((seqs, rows, D), BF),
        sds((seqs, HEADS, rows, total), BF),
    ]
    if assemble:
        out_specs += [ANY, fixed(8, D), fixed(1, ff)]
        out_shape += [sds((D, 3 * D), BF), sds((8, D), F32), sds((1, ff), F32)]
    stage = (4, 8 * (D // 8 + PAD), 3 * D // 4) if assemble else (1, PAD, 128)
    return pl.pallas_call(
        functools.partial(lead_kernel, len(pieces), assemble, first),
        grid_spec=pltpu.PrefetchScalarGridSpec(
            num_scalar_prefetch=3,
            grid=(seqs,),
            in_specs=[x_spec(j) for j in range(4)]
            + [ANY] * len(pieces)
            + ([] if assemble else [fixed(8, D)])
            + [
                pl.BlockSpec(
                    (1, HEADS, rows, total), lambda b, *_: (first + b, 0, 0, 0)
                )
            ],
            out_specs=out_specs,
            scratch_shapes=[
                pltpu.VMEM((D, 3 * D), BF),
                pltpu.VMEM((total, D), BF),
                pltpu.VMEM(stage, BF),
                pltpu.SemaphoreType.DMA((2,)),
            ],
        ),
        out_shape=out_shape,
        compiler_params=pltpu.CompilerParams(vmem_limit_bytes=GRANT),
        cost_estimate=pl.CostEstimate(
            flops=seqs * rows * D * (18 * D + 4 * total),
            bytes_accessed=seqs * 8 * MIB,
            transcendentals=seqs * HEADS * rows * total,
        ),
    )(table, order, lengths, *x_blocks, *pieces, *([] if assemble else [vec]), prev_logits)


def attend_back_kernel(order_ref, q_ref, kv_ref, probs_ref, dctx_ref, *refs):
    dlogits_ref, dq_ref, *dkv_refs, dkv_all = refs[-7:]
    rows = q_ref.shape[1]
    total = dkv_all.shape[0]

    def ahead(i):
        cols = slice(i * PAIR, (i + 1) * PAIR)
        vcols = slice(D + i * PAIR, D + (i + 1) * PAIR)
        dctx = stack_heads(dctx_ref[0, :, cols])
        return dctx, mm_nt(dctx, kv_ref[0, :, vcols])

    dctx, dprobs = ahead(0)
    for i in range(PAIRS):
        later = ahead(i + 1) if i + 1 < PAIRS else (None, None)
        cols = slice(i * PAIR, (i + 1) * PAIR)
        vcols = slice(D + i * PAIR, D + (i + 1) * PAIR)
        probs = probs_ref[0, 2 * i : 2 * i + 2].reshape(2 * rows, total)
        dkv_all[:, vcols] = mm_tn(probs, dctx).astype(BF)
        wide = probs.astype(F32)
        prod = wide * dprobs
        weighted = jnp.sum(prod, -1, keepdims=True)
        dlogits = (prod - wide * weighted).astype(BF)
        dlogits_ref[0, 2 * i : 2 * i + 2] = dlogits.reshape(2, rows, total)
        dq_ref[0, :, cols] = (pick_heads(mm(dlogits, kv_ref[0, :, cols])) * SCALE).astype(BF)
        dkv_all[:, cols] = mm_tn(dlogits, stack_heads(q_ref[0, :, cols])).astype(BF)
        dctx, dprobs = later
    for j in range(4):
        start = pl.multiple_of(order_ref[j] * rows, rows)
        dkv_refs[j][0] = dkv_all[pl.ds(start, rows), :]


def attend_back(order, queries, keys_values, probs, dctx, dlogits, first, seqs_all, deps=()):
    seqs, rows, _ = queries.shape
    blocks = 4
    total = probs.shape[-1]
    row_spec = lambda width: pl.BlockSpec((1, rows, width), lambda b, *_: (b, 0, 0))
    late_spec = lambda width: pl.BlockSpec((1, rows, width), lambda b, *_: (first + b, 0, 0))
    head_spec = pl.BlockSpec((1, HEADS, rows, total), lambda b, *_: (b, 0, 0, 0))
    late_head = pl.BlockSpec((1, HEADS, rows, total), lambda b, *_: (first + b, 0, 0, 0))
    more = ([] if dlogits is None else [dlogits]) + list(deps)
    outs = pl.pallas_call(
        attend_back_kernel,
        grid_spec=pltpu.PrefetchScalarGridSpec(
            num_scalar_prefetch=1,
            grid=(seqs,),
            in_specs=[
                row_spec(D),
                pl.BlockSpec((1, total, 2 * D), lambda b, *_: (b, 0, 0)),
                head_spec,
                late_spec(D),
            ]
            + [ANY] * len(more),
            out_specs=[late_head, row_spec(D)] + [row_spec(2 * D)] * blocks,
            scratch_shapes=[pltpu.VMEM((total, 2 * D), BF)],
        ),
        out_shape=[
            jax.ShapeDtypeStruct((seqs_all, HEADS, rows, total), BF),
            jax.ShapeDtypeStruct(queries.shape, BF),
        ]
        + [jax.ShapeDtypeStruct((seqs, rows, 2 * D), BF)] * blocks,
        input_output_aliases={} if dlogits is None else {5: 0},
        compiler_params=pltpu.CompilerParams(vmem_limit_bytes=GRANT),
        cost_estimate=pl.CostEstimate(
            flops=8 * seqs * HEADS * rows * total * PAIR,
            bytes_accessed=4 * seqs * HEADS * rows * total,
            transcendentals=0,
        ),
    )(order, queries, keys_values, probs, dctx, *more)
    dkv = [b.reshape(seqs * rows, 2 * D) for b in outs[2:]]
    return outs[0], outs[1].reshape(seqs * rows, D), dkv


def gelu_and_slope(values):
    cdf = 0.5 * lax.erf(values * 0.7071067811865476) + 0.5
    bell = jnp.exp(values * values * -0.5)
    return values * cdf, cdf + values * bell * 0.3989422804014327


def norm(values):
    average = jnp.mean(values, -1, keepdims=True)
    centred = values - average
    inverse = lax.rsqrt(jnp.mean(centred * centred, -1, keepdims=True) + 1e-06)
    return centred * inverse, inverse


def norm_back(grad, normed, inverse):
    first = jnp.mean(grad, -1, keepdims=True)
    second = jnp.mean(grad * normed, -1, keepdims=True)
    return inverse * (grad - first - normed * second)


def load_middle(table_ref, down_table_ref, in_refs, down_refs, w_out_ref, w_in_ref, w_down_ref, stage, sems):
    if len(in_refs) == 1:
        ff = w_in_ref.shape[1]
        pltpu.make_async_copy(down_refs[1], w_out_ref, sems.at[0]).start()
        for c in range(4):
            cols = pl.ds(c * (ff // 4), ff // 4)
            pltpu.make_async_copy(
                in_refs[0].at[:, cols], w_in_ref.at[:, cols], sems.at[1 + c]
            ).start()
            pltpu.make_async_copy(
                down_refs[0].at[:, cols], w_down_ref.at[:, cols], sems.at[5 + c]
            ).start()
        wait_whole(w_out_ref, sems.at[0])
    else:
        down = w_down_ref.shape[0] // 4
        wide = w_down_ref.shape[1] // 8
        high, half = D // 8, D // 16
        for piece, dp, seq in pieces_of(down_refs, down_table_ref):
            pltpu.make_async_copy(
                piece.at[pl.ds(down, half)], stage.at[seq, dp], sems.at[0]
            ).start()
        for piece, dp, seq in pieces_of(in_refs, table_ref):
            rows = pl.ds(pl.multiple_of(dp * high, high), high)
            cols = pl.ds(pl.multiple_of(seq * D, D), D)
            pltpu.make_async_copy(piece, w_in_ref.at[rows, cols], sems.at[1 + seq]).start()
        for piece, dp, seq in pieces_of(down_refs, down_table_ref):
            rows = pl.ds(pl.multiple_of(seq * down, down), down)
            cols = pl.ds(pl.multiple_of(dp * wide, wide), wide)
            pltpu.make_async_copy(
                piece.at[pl.ds(0, down)], w_down_ref.at[rows, cols], sems.at[5 + (dp >> 1)]
            ).start()
        wait_whole(stage, sems.at[0])
        for s in range(4):
            for d in range(8):
                cols = slice(s * down, (s + 1) * down)
                w_out_ref[d * high : d * high + half, cols] = stage[s, d][:, :down]
                w_out_ref[d * high + half : (d + 1) * high, cols] = stage[s, d][:, down:]


def middle_kernel(
    counts, fused, table_ref, down_table_ref, where_ref, x_ref, ctx_a_ref, ctx_b_ref, cot_ref,
    vec_ref, b_in_ref, *refs
):
    in_refs, refs = refs[: counts[0]], refs[counts[0] :]
    down_refs, refs = refs[: counts[1]], refs[counts[1] :]
    out_ref, dh1_ref, dctx_ref, dinner_ref, y1_ref, dvec_ref, db_in_ref = refs[:7]
    if fused:
        send_ref, keep_ref, act_all, dbranch_all, dattn_all, ctx_all, grad_out = refs[7:14]
    else:
        act_all, dbranch_all, dattn_all = refs[7:10]
    w_out_ref, w_in_ref, w_down_ref, stage, sems = refs[-5:]
    step = pl.program_id(0)
    rows = x_ref.shape[0]
    parts = pl.num_programs(0) - (4 if fused else 0)

    def token_rows():
        middle_rows(
            parts, table_ref, down_table_ref, x_ref, ctx_a_ref, ctx_b_ref, cot_ref, vec_ref,
            b_in_ref, in_refs, down_refs, out_ref, dh1_ref, dctx_ref, dinner_ref, y1_ref,
            dvec_ref, db_in_ref, act_all, dbranch_all, dattn_all, ctx_all if fused else None,
            w_out_ref, w_in_ref, w_down_ref, stage, sems,
        )

    if not fused:
        token_rows()
        return

    pl.when(step < parts)(token_rows)

    @pl.when(step == parts)
    def _():
        grad_out[...] = mm_tn(ctx_all[...], dattn_all[...]).astype(BF)

    @pl.when(step >= parts)
    def _():
        grad_down(where_ref, step - parts, dbranch_all, act_all, grad_out, send_ref, keep_ref)


def grad_down(where_ref, step, dbranch_ref, act_ref, grad_out, send_ref, keep_ref):
    y, x, core = where_ref[1], where_ref[2], where_ref[3]
    wide, down = D // 2, D // 4
    high, half = D // 8, D // 16
    first = core == 0

    def put(far_y, far_x, rows, cols, even, odd):
        keep_ref[far_y, far_x, 0, rows, cols] = jnp.where(first, even, odd)
        send_ref[far_y, far_x, 0, rows, cols] = jnp.where(first, odd, even)

    cols = pl.ds(pl.multiple_of(step * D, D), D)
    grad = mm_tn(dbranch_ref[...], act_ref[:, cols]).astype(BF)
    for j in range(2):
        top = pl.multiple_of((2 * step + j) * high, high)
        upper, lower = grad_out[pl.ds(top, half), :], grad_out[pl.ds(top + half, half), :]
        for i in range(2):
            pair = [slice((2 * i + k) * down, (2 * i + k + 1) * down) for k in range(2)]
            side = slice(j * wide, (j + 1) * wide)
            far = (y ^ j, x ^ i)
            put(*far, slice(0, down), slice(None), grad[pair[0], side], grad[pair[1], side])
            tail = slice(down, down + half)
            put(*far, tail, slice(0, down), upper[:, pair[0]], upper[:, pair[1]])
            put(*far, tail, slice(down, 2 * down), lower[:, pair[0]], lower[:, pair[1]])


def middle_rows(
    parts, table_ref, down_table_ref, x_ref, ctx_a_ref, ctx_b_ref, cot_ref, vec_ref,
    b_in_ref, in_refs, down_refs, out_ref, dh1_ref, dctx_ref, dinner_ref, y1_ref,
    dvec_ref, db_in_ref, act_all, dbranch_all, dattn_all, ctx_all,
    w_out_ref, w_in_ref, w_down_ref, stage, sems,
):
    step, rows = pl.program_id(0), x_ref.shape[0]
    here = pl.ds(pl.multiple_of(step * rows, rows), rows)
    wide = act_all.shape[1] // 4

    @pl.when(step == 0)
    def _():
        load_middle(
            table_ref, down_table_ref, in_refs, down_refs,
            w_out_ref, w_in_ref, w_down_ref, stage, sems,
        )
        for c in range(4):
            wait_whole(w_in_ref.at[:, pl.ds(c * wide, wide)], sems.at[1 + c])
            wait_whole(w_down_ref.at[:, pl.ds(c * wide, wide)], sems.at[5 + c])
        dvec_ref[...] = jnp.zeros_like(dvec_ref)
        db_in_ref[...] = jnp.zeros_like(db_in_ref)

    vec = lambda i: vec_ref[i : i + 1, :]
    total = lambda v: jnp.sum(v, 0, keepdims=True)

    ctx = jnp.where(step < parts // 2, ctx_a_ref[...], ctx_b_ref[...])
    if ctx_all is not None:
        ctx_all[here, :] = ctx
    h1 = x_ref[...].astype(F32) + (mm(ctx, w_out_ref[...]) + vec(2))
    normed1, inverse1 = norm(h1)
    y1 = normed1 * vec(3) + vec(4)
    y1_low = y1.astype(BF)
    y1_ref[...] = y1_low
    h2 = y1 + vec(5)
    part = lambda c: slice(c * wide, (c + 1) * wide)
    expand = lambda c: mm(y1_low, w_in_ref[:, part(c)]) + b_in_ref[:, part(c)]
    slopes, ahead = [], expand(0)
    for c in range(4):
        cols = part(c)
        inner = ahead
        if c < 3:
            ahead = expand(c + 1)
        act, slope = gelu_and_slope(inner)
        act = act.astype(BF)
        act_all[here, cols] = act
        slopes.append(slope)
        h2 = h2 + mm_nt(act, w_down_ref[:, cols])
    normed2, inverse2 = norm(h2)
    out_ref[...] = (normed2 * vec(6) + vec(7)).astype(BF)
    cot = cot_ref[...].astype(F32)
    dh2 = norm_back(cot * vec(6), normed2, inverse2)
    dbranch = dh2.astype(BF)
    dbranch_all[here, :] = dbranch
    dvec_ref[5:6, :] += total(dbranch.astype(F32))
    dvec_ref[6:7, :] += total(cot * normed2)
    dvec_ref[7:8, :] += total(cot)
    dy1, ahead = dh2, mm(dbranch, w_down_ref[:, part(0)])
    for c in range(4):
        cols = part(c)
        dact = ahead
        if c < 3:
            ahead = mm(dbranch, w_down_ref[:, part(c + 1)])
        dinner = (dact * slopes[c]).astype(BF)
        dinner_ref[:, cols] = dinner
        db_in_ref[:, cols] += total(dinner.astype(F32))
        dy1 = dy1 + mm_nt(dinner, w_in_ref[:, cols])
    dh1 = norm_back(dy1 * vec(3), normed1, inverse1)
    dh1_ref[...] = dh1
    dattn = dh1.astype(BF)
    dattn_all[here, :] = dattn
    dctx_ref[...] = mm_nt(dattn, w_out_ref[...]).astype(BF)
    dvec_ref[2:3, :] += total(dattn.astype(F32))
    dvec_ref[3:4, :] += total(dy1 * normed1)
    dvec_ref[4:5, :] += total(dy1)


def middle(table, down_table, x, ctx_a, ctx_b, cot, vectors, b_in, in_pieces, down_pieces, where=None):
    tokens = x.shape[0]
    ff = b_in.shape[1]
    step = 256
    parts = tokens // step
    half = parts // 2
    fused = where is not None
    late = lambda i: jnp.minimum(i, parts - 1)
    rows = lambda width: pl.BlockSpec((step, width), lambda i, *_: (late(i), 0))
    ctx_specs = [
        pl.BlockSpec((step, D), lambda i, *_: (jnp.minimum(i, half - 1), 0)),
        pl.BlockSpec((step, D), lambda i, *_: (jnp.clip(i - half, 0, half - 1), 0)),
    ]
    whole = lambda *shape: pl.BlockSpec(shape, lambda i, *_: (0, 0))
    sds = jax.ShapeDtypeStruct
    counts = (len(in_pieces), len(down_pieces))
    out_specs = [rows(D)] * 3 + [rows(ff), rows(D), whole(8, D), whole(1, ff)]
    out_shape = [
        sds((tokens, D), BF),
        sds((tokens, D), F32),
        sds((tokens, D), BF),
        sds((tokens, ff), BF),
        sds((tokens, D), BF),
        sds((8, D), F32),
        sds((1, ff), F32),
    ]
    scratch = []
    if fused:
        piece = (D // 4 + D // 16, ff // 8)
        spec = pl.BlockSpec(
            (2, 2, 1) + piece,
            lambda i, t, d, w: (0, 0, jnp.maximum(i - parts, 0) ^ w[0], 0, 0),
        )
        out_specs += [spec, spec]
        out_shape += [sds((2, 2, 4) + piece, BF)] * 2
        scratch = [pltpu.VMEM((tokens, ff), BF)] + [pltpu.VMEM((tokens, D), BF)] * 3
        scratch += [pltpu.VMEM((D, D), BF)]
    else:
        out_specs += [whole(tokens, ff), whole(tokens, D), whole(tokens, D)]
        out_shape += [sds((tokens, ff), BF), sds((tokens, D), BF), sds((tokens, D), BF)]
        where = jnp.zeros((4,), jnp.int32)
    return pl.pallas_call(
        functools.partial(middle_kernel, counts, fused),
        grid_spec=pltpu.PrefetchScalarGridSpec(
            num_scalar_prefetch=3,
            grid=(parts + 4 if fused else parts,),
            in_specs=[rows(D)]
            + ctx_specs
            + [rows(D), whole(8, D), whole(1, ff)]
            + [ANY] * sum(counts),
            out_specs=out_specs,
            scratch_shapes=scratch
            + [
                pltpu.VMEM((D, D), BF),
                pltpu.VMEM((D, ff), BF),
                pltpu.VMEM((D, ff), BF),
                pltpu.VMEM((4, 8, D // 16, ff // 8), BF),
                pltpu.SemaphoreType.DMA((9,)),
            ],
        ),
        out_shape=out_shape,
        compiler_params=pltpu.CompilerParams(vmem_limit_bytes=GRANT),
        cost_estimate=pl.CostEstimate(
            flops=tokens * (10 * D * ff + 6 * D * D),
            bytes_accessed=30 * MIB,
            transcendentals=2 * tokens * ff,
        ),
    )(table, down_table, where, x, ctx_a, ctx_b, cot, vectors, b_in, *in_pieces, *down_pieces)


def grad_in_kernel(where_ref, y1_ref, dinner_ref, *refs):
    send_ref, keep_ref = refs[-2:]
    z, y = where_ref[0], where_ref[1]
    step = pl.program_id(0)
    high = D // 8
    grad = mm_tn(y1_ref[...], dinner_ref[...]).astype(BF)

    def put(ref):
        for d in range(8):
            ref[0, y ^ (d & 1), (d >> 1) ^ z] = grad[d * high : (d + 1) * high]

    @pl.when(step < 2)
    def _():
        put(send_ref)

    @pl.when(step >= 2)
    def _():
        put(keep_ref)


def grad_in(where, y1, dinner, deps=()):
    tokens, ff = dinner.shape
    wide = ff // 4

    def columns(t, where):
        return (0, 2 * (where[2] ^ (t & 1)) + (where[3] ^ (1 - (t >> 1))))

    piece = (1, 2, 4, D // 8, wide)
    shape = jax.ShapeDtypeStruct((2, 2, 4, D // 8, wide), BF)
    return pl.pallas_call(
        grad_in_kernel,
        grid_spec=pltpu.PrefetchScalarGridSpec(
            num_scalar_prefetch=1,
            grid=(4,),
            in_specs=[
                pl.BlockSpec((tokens, D), lambda t, w: (0, 0)),
                pl.BlockSpec((tokens, wide), columns),
            ]
            + [ANY] * len(deps),
            out_specs=[
                pl.BlockSpec(piece, lambda t, w: (jnp.minimum(t, 1), 0, 0, 0, 0)),
                pl.BlockSpec(piece, lambda t, w: (jnp.maximum(t - 2, 0), 0, 0, 0, 0)),
            ],
        ),
        out_shape=[shape, shape],
        compiler_params=pltpu.CompilerParams(vmem_limit_bytes=GRANT),
        cost_estimate=pl.CostEstimate(
            flops=2 * tokens * D * ff, bytes_accessed=14 * MIB, transcendentals=0
        ),
    )(where, y1, dinner, *deps)


def grad_qkv_kernel(where_ref, x0_ref, *refs):
    x2_refs, refs = refs[:2], refs[2:]
    dq_refs, refs = refs[:2], refs[2:]
    own_refs, refs = refs[:4], refs[4:]
    far_refs, refs = refs[:4], refs[4:]
    dvec_ref, db_ref = refs[:2]
    *out_refs, grad, dvec = refs[-6:]
    z, y, x, core = (where_ref[i] for i in range(4))
    step = pl.program_id(0)
    wide, high = 3 * D // 4, D // 8
    cut = out_refs[0].shape[3]
    part = x2_refs[0].shape[0]
    x0 = lambda h: x0_ref[h * part : (h + 1) * part]

    @pl.when(step == 0)
    def _():
        total = mm_tn(x0(0), dq_refs[0][...]) + mm_tn(x0(1), dq_refs[1][...])
        grad[:, :D] = total.astype(BF)
        dvec[...] = dvec_ref[...]
        for ref in dq_refs:
            dvec[0:1, :] += jnp.sum(ref[...].astype(F32), 0, keepdims=True)

    def emit():
        first = core == 0
        for i in range(2):
            even = grad[:, 2 * i * wide : (2 * i + 1) * wide]
            odd = grad[:, (2 * i + 1) * wide : (2 * i + 2) * wide]
            kept = jnp.where(first, even, odd)
            sent = jnp.where(first, odd, even)
            for d in range(8):
                top, far_z = d * high, (d >> 1) ^ z
                upper = (y ^ (d & 1), x ^ i, far_z)
                lower = (x ^ i, y ^ (d & 1), far_z)
                extra = []
                for k in range(2):
                    s = 2 * i + k
                    own = dvec[2 * s : 2 * s + 2, d * high : (d + 1) * high]
                    at = (4 * d + s) * high
                    rest = jnp.zeros((PAD - 3, high), F32)
                    extra.append(jnp.concatenate([own, db_ref[0:1, at : at + high], rest], 0))
                tail = lower + (slice(high - cut, high - cut + PAD), slice(0, high))
                pairs = ((sent, extra[1], extra[0]), (kept, extra[0], extra[1]))
                for n, (part, one, other) in enumerate(pairs):
                    out_refs[n][upper] = part[top : top + cut]
                    out_refs[2 + n][lower + (slice(0, high - cut), slice(None))] = part[
                        top + cut : top + high
                    ]
                    out_refs[2 + n][tail] = jnp.where(first, one, other).astype(BF)

    for t in (1, 2):

        @pl.when(step == t)
        def _():
            total = None
            for h in range(2):
                own, far = (
                    low(add(refs[h][...], refs[2 + h][...])) for refs in (own_refs, far_refs)
                )
                if t == 2:
                    both = jnp.sum(own.astype(F32), 0, keepdims=True)
                    dvec[1:2, :] += both + jnp.sum(far.astype(F32), 0, keepdims=True)
                piece = mm_tn(x0(h), own) + mm_tn(x2_refs[h][...], far)
                total = piece if total is None else total + piece
            grad[:, t * D : (t + 1) * D] = total.astype(BF)
            if t == 2:
                emit()


def grad_qkv(where, x0, x2, dq, own, far, dvec, db_in, deps=()):
    tokens = x0.shape[0]
    fixed = lambda *shape: pl.BlockSpec(shape, lambda t, w: (0, 0))
    half = fixed(tokens // 2, D)
    part = pl.BlockSpec((tokens // 2, D), lambda t, w: (0, jnp.maximum(t - 1, 0)))
    cut = D // 12
    dims = [(2, 2, 4, rows, 3 * D // 4) for rows in (cut, D // 8 - cut + PAD) for _ in range(2)]
    return pl.pallas_call(
        grad_qkv_kernel,
        grid_spec=pltpu.PrefetchScalarGridSpec(
            num_scalar_prefetch=1,
            grid=(3,),
            in_specs=[fixed(tokens, D)]
            + [half] * 4
            + [part] * 8
            + [fixed(8, D)]
            + [fixed(*db_in.shape)]
            + [ANY] * len(deps),
            out_specs=[pl.BlockSpec(d, lambda t, w: (0, 0, 0, 0, 0)) for d in dims],
            scratch_shapes=[pltpu.VMEM((D, 3 * D), BF), pltpu.VMEM((8, D), F32)],
        ),
        out_shape=[jax.ShapeDtypeStruct(d, BF) for d in dims],
        compiler_params=pltpu.CompilerParams(vmem_limit_bytes=GRANT),
        cost_estimate=pl.CostEstimate(
            flops=2 * tokens * D * 5 * D, bytes_accessed=16 * MIB, transcendentals=0
        ),
    )(where, x0, *x2, *dq, *own, *far, dvec, db_in, *deps)


def grad_far_kernel(dkv_ref, got_ref, w_ref, *refs):
    total = low(add(dkv_ref[...], got_ref[...]))
    refs[-1][...] = mm_nt(total, w_ref[:, D:]).astype(BF)


def grad_far(dkv, got, w_qkv, deps=()):
    tokens = dkv.shape[0]
    step = 256
    rows = lambda width: pl.BlockSpec((step, width), lambda i: (i, 0))
    return pl.pallas_call(
        grad_far_kernel,
        grid=(tokens // step,),
        in_specs=[
            rows(2 * D),
            rows(2 * D),
            pl.BlockSpec((D, 3 * D), lambda i: (0, 0), pipeline_mode=pl.Buffered(1)),
        ]
        + [ANY] * len(deps),
        out_specs=rows(D),
        out_shape=jax.ShapeDtypeStruct((tokens, D), BF),
        compiler_params=pltpu.CompilerParams(vmem_limit_bytes=GRANT),
        cost_estimate=pl.CostEstimate(
            flops=2 * tokens * D * 2 * D, bytes_accessed=10 * MIB, transcendentals=0
        ),
    )(dkv, got, w_qkv, *deps)


def grad_own_kernel(*refs):
    dkv_refs, refs = refs[:2], refs[2:]
    got_refs, refs = refs[:2], refs[2:]
    dq_refs, refs = refs[:2], refs[2:]
    dh1_ref, w_ref = refs[:2]
    dx_ref = refs[-1]
    early = pl.program_id(0) < pl.num_programs(0) // 2
    pick = lambda pair: jnp.where(early, pair[0][...], pair[1][...])
    total = (pick(dkv_refs).astype(F32) + pick(got_refs).astype(F32)).astype(BF)
    dx = mm_nt(total, w_ref[:, D:]) + mm_nt(pick(dq_refs), w_ref[:, :D])
    dx_ref[...] = dx + dh1_ref[...]


def grad_own(dkv, got, dq, dh1, w_qkv, deps=()):
    tokens = dh1.shape[0]
    step = 256
    half = tokens // step // 2

    def pair(width):
        return [
            pl.BlockSpec((step, width), lambda i: (jnp.minimum(i, half - 1), 0)),
            pl.BlockSpec((step, width), lambda i: (jnp.maximum(i - half, 0), 0)),
        ]

    rows = pl.BlockSpec((step, D), lambda i: (i, 0))
    return pl.pallas_call(
        grad_own_kernel,
        grid=(tokens // step,),
        in_specs=pair(2 * D)
        + pair(2 * D)
        + pair(D)
        + [rows, pl.BlockSpec((D, 3 * D), lambda i: (0, 0), pipeline_mode=pl.Buffered(1))]
        + [ANY] * len(deps),
        out_specs=rows,
        out_shape=jax.ShapeDtypeStruct((tokens, D), F32),
        compiler_params=pltpu.CompilerParams(vmem_limit_bytes=GRANT),
        cost_estimate=pl.CostEstimate(
            flops=2 * tokens * D * 3 * D, bytes_accessed=20 * MIB, transcendentals=0
        ),
    )(*dkv, *got, *dq, dh1, w_qkv, *deps)


def gather_small(b_in, vectors):
    dp, seq = lax.axis_size("dp"), lax.axis_size("seq")
    small = jnp.concatenate([vectors.reshape(-1), b_in])
    whole = lax.all_gather(small, BOTH, axis=0, tiled=False)
    nv = vectors.size
    vec = whole[:, :nv].reshape((dp, seq) + vectors.shape).transpose(1, 2, 0, 3)
    return whole[:, nv:].reshape(1, -1), vec.reshape(8, D)


def reduce_small(g_b, g_vec):
    dp, seq = lax.axis_size("dp"), lax.axis_size("seq")
    vec = g_vec.reshape(seq, 8 // seq, dp, D // dp).transpose(2, 0, 1, 3)
    small = jnp.concatenate([vec.reshape(dp * seq, -1), g_b.reshape(dp * seq, -1)], 1)
    mine = lax.psum_scatter(small, BOTH, scatter_dimension=0, tiled=True)[0]
    nv = 8 * D // (dp * seq)
    return mine[nv:], mine[:nv].reshape(8 // seq, D // dp)


def gather_plain(w_qkv, w_out, w_in, w_down_t):
    both = lambda a, first, second: lax.all_gather(
        lax.all_gather(a, first, axis=0, tiled=True), second, axis=1, tiled=True
    )
    return (
        [both(w_qkv, "dp", "seq")],
        [both(w_in, "dp", "seq")],
        [both(w_down_t, "seq", "dp"), both(w_out, "dp", "seq")],
    )


def reduce_plain(a, first, second):
    part = lax.psum_scatter(a.astype(BF), first, scatter_dimension=0, tiled=True)
    return lax.psum_scatter(part, second, scatter_dimension=1, tiled=True).astype(F32)


def together(*parts):
    return lax.optimization_barrier(parts)


def forward_apart(order, lengths, table, x0, prev_logits, weights):
    w_qkv, w_out, w_in, w_down, b_in, vectors = weights
    seqs = x0.shape[0]
    half = seqs // 2
    cut = w_out.shape[0] // 2
    turned = jnp.concatenate([w_out[:cut], w_out[cut:]], 1)
    down = jnp.concatenate([w_down.T, turned], 0)
    down_x = swap_x(down)
    few = half // 2
    x2_a = swap_x(x0[:few])
    small = jnp.concatenate([vectors, b_in.reshape(1, -1)], 0)
    small = jnp.pad(small, ((0, PAD - small.shape[0]), (0, w_qkv.shape[1] - small.shape[1])))
    qkv = stack_z_direct(jnp.concatenate([w_qkv, small], 0))
    qkv, w_in, x_late, x_b, x_all, down, down_x, x2_a = together(
        qkv, w_in, x0[few:half], x0[half:], x0, down, down_x, x2_a
    )

    qkv_x, qkv_y = swap_x(qkv), swap_y(qkv)
    down = jnp.stack([down, down_x])
    down_y = swap_y(down)
    x2_late = swap_x(x_late)
    in_pair = jnp.stack([w_in, swap_z(w_in, 1)])
    in_got = swap_z(in_pair, 2)
    qkv, qkv_x, qkv_y, x2_late, x_all, in_pair, in_got, x_b, down, down_y = together(
        qkv, qkv_x, qkv_y, x2_late, x_all, in_pair, in_got, x_b, down, down_y
    )
    x2_a = jnp.concatenate([x2_a, x2_late], 0)

    qkv_xy, x2_b = swap_y(qkv_x), swap_x(x_b)
    x1, x3_a, qkv_far = swap_core(x_all), swap_core(x2_a), swap_core(qkv)
    down = [jnp.concatenate([down, down_y], 0)]
    down.append(turn_z(down[0]))
    qkv_xy, x2_b, x1, x3_a, qkv_far, *down = together(qkv_xy, x2_b, x1, x3_a, qkv_far, *down)
    in_own = jnp.concatenate([in_pair, in_got], 0)
    qkv_near = [qkv, qkv_x, qkv_y, qkv_xy]
    qkv_pieces = qkv_near + [qkv_far] + [swap_core(a) for a in qkv_near[1:]]

    in_x, in_y, x3_b = swap_x(in_own), swap_y(in_own), swap_core(x2_b)
    down.append(turn_z(down[1]))
    q_a, kv_a, ctx_a, probs_a, f_qkv, f_vec, f_b = lead(
        table, order, lengths, (x0, x1, x2_a, x3_a), (0, 0, 0, 0), half, 0,
        qkv_pieces, prev_logits,
    )
    in_own, in_x, in_y, x3_b, f_qkv, ctx_a, f_b, *down = together(
        in_own, in_x, in_y, x3_b, f_qkv, ctx_a, f_b, *down
    )

    in_xy = swap_y(in_x)
    in_far = [swap_core(a) for a in (in_own, in_x, in_y)]
    down_far = [swap_core(a) for a in down]
    down.append(turn_z(down[2]))
    q_b, kv_b, ctx_b, probs_b = lead(
        table, order, lengths, (x0, x1, x2_b, x3_b), (half, half, 0, 0), half, half,
        [f_qkv], prev_logits, f_vec,
    )
    in_xy, ctx_b, *both = together(in_xy, ctx_b, *in_far, *down_far, *down)
    in_far, down_far, down = both[:3], both[3:6], both[6:]

    in_pieces = [in_own, in_x, in_y, in_xy] + in_far + [swap_core(in_xy)]
    down_pieces = down + down_far + [swap_core(down[3])]
    first, second = (q_a, kv_a, ctx_a, probs_a), (q_b, kv_b, ctx_b, probs_b)
    return first, second, f_qkv, f_vec, f_b, in_pieces, down_pieces, [x2_a, x2_b]


def shards_apart(
    hidden_states, prev_logits, lengths, w_qkv, w_out, w_in, w_down, b_in, vectors, cotangent
):
    seqs, rows, _ = hidden_states.shape
    tokens = seqs * rows
    half = seqs // 2
    order = jnp.arange(4, dtype=jnp.int32) ^ lax.axis_index("seq")
    table, down_table = piece_table(), turned_table()
    where = jnp.stack(place()).astype(jnp.int32)
    x0 = hidden_states.reshape(tokens, D)
    first, second, f_qkv, f_vec, f_b, in_pieces, down_pieces, x2 = forward_apart(
        order, lengths, table, hidden_states, prev_logits,
        (w_qkv, w_out, w_in, w_down, b_in, vectors),
    )
    rows_of = lambda a: a.reshape(-1, D)
    ctx, x2 = [rows_of(first[2]), rows_of(second[2])], [rows_of(a) for a in x2]
    out, dh1, dctx, dinner, y1, dvec, db_in, d_send, d_keep = middle(
        table, down_table, x0, *ctx, cotangent.reshape(tokens, D), f_vec, f_b,
        in_pieces, down_pieces, where,
    )
    dctx = dctx.reshape(seqs, rows, D)

    d_core = swap_core(d_send)
    i_send, i_keep = grad_in(where, y1, dinner, [d_keep])
    i_core = swap_core(i_send)
    d_core = after(d_core, i_keep)
    d_sent = low(add(d_keep[1], d_core[1]))
    d_one = swap_y(d_sent)
    i_core = after(i_core, d_sent)
    i_sent = low(add(i_keep[1], i_core[1]))
    i_one = swap_x(i_sent)
    dlogits, dq_a, dkv_a = attend_back(
        order, first[0], first[1], first[3], dctx, None, 0, seqs, [d_sent, i_sent]
    )
    far_a, own_a = swap_core(dkv_a[3]), swap_core(dkv_a[1])
    dlogits, dq_b, dkv_b = attend_back(
        order, second[0], second[1], second[3], dctx, dlogits, half, seqs, [dq_a]
    )
    far_b, own_b = swap_core(dkv_b[3]), swap_core(dkv_b[1])
    far_a, own_a = after(far_a, dq_b), after(own_a, dq_b)
    d_one, i_one = after(d_one, dq_b), after(i_one, dq_b)
    d_sent = low(add(d_keep[0, 1], d_core[0, 1], d_one[1]))
    d_two = swap_x(d_sent)
    i_sent = low(add(i_keep[0, 1], i_core[0, 1], i_one[1]))
    i_two = swap_y(i_sent)
    dq, own, far = [dq_a, dq_b], [dkv_a[0], dkv_b[0], own_a, own_b], [dkv_a[2], dkv_b[2], far_a, far_b]
    a_send, a_keep, b_send, b_keep = grad_qkv(where, x0, x2, dq, own, far, dvec, db_in, [d_sent, i_sent])
    d_two, i_two, a_send, b_send = together(d_two, i_two, a_send, b_send)
    a_core, b_core = swap_core(a_send), swap_core(b_send)
    d_part = lambda k: add(d_keep[0, 0, k], d_core[0, 0, k], d_one[0, k], d_two[k])
    i_part = lambda k: add(i_keep[0, 0, k], i_core[0, 0, k], i_one[0, k], i_two[k])
    upper, lower = slice(2, 4), slice(0, 2)
    d_sent, i_sent = low(d_part(upper)), low(i_part(upper))
    i_far, d_far = swap_z(i_sent, 2), swap_z(d_sent, 2)
    a_core, b_core = after(a_core, d_sent, i_sent), after(b_core, d_sent, i_sent)
    a_sent, b_sent = low(add(a_keep[1], a_core[1])), low(add(b_keep[1], b_core[1]))
    a_one, b_one = swap_y(a_sent), swap_x(b_sent)
    dx2_a = grad_far(far[0], far[2], f_qkv, [a_sent, b_sent])
    got_a = swap_x(dx2_a)
    dx2_b = grad_far(far[1], far[3], f_qkv, [dx2_a])
    dx = grad_own(own[:2], own[2:], dq, dh1, f_qkv, [dx2_b])
    a_one, b_one, dx, dx2_b = together(a_one, b_one, dx, dx2_b)
    a_sent = low(add(a_keep[0, 1], a_core[0, 1], a_one[1]))
    b_sent = low(add(b_keep[0, 1], b_core[0, 1], b_one[1]))
    a_two, b_two = swap_x(a_sent), swap_y(b_sent)
    got_b = swap_x(after(dx2_b, a_sent))
    i_far, d_far = after(i_far, a_sent, b_sent), after(d_far, a_sent, b_sent)
    i_last = i_part(lower) + i_far.astype(F32)
    i_end = swap_z(low(i_last[1]), 1)
    d_last = d_part(lower) + d_far.astype(F32)
    d_end = swap_z(low(d_last[1]), 1)
    a_two, b_two, i_last, d_last, got_a = together(a_two, b_two, i_last, d_last, got_a)
    a_part = lambda k: add(a_keep[0, 0, k], a_core[0, 0, k], a_one[0, k], a_two[k])
    b_part = lambda k: add(b_keep[0, 0, k], b_core[0, 0, k], b_one[0, k], b_two[k])
    q_part = lambda k: jnp.concatenate([a_part(k), b_part(k)], 0)
    q_sent = [low(q_part(k)) for k in range(1, 4)]
    q_far = [swap_z(q, k) for q, k in zip(q_sent, range(1, 4))]
    i_end, d_end, dx = after((i_end, d_end, dx), *q_sent)
    o_in = i_last[0] + i_end.astype(F32)
    o_low = d_last[0] + d_end.astype(F32)
    o_top = q_part(0) + add(*q_far)
    got_b = after(got_b, o_top)
    grad_hidden = low(dx + jnp.concatenate([got_a, got_b], 0).astype(F32))
    down, cut, (extra, high) = w_down.shape[1], w_qkv.shape[0], vectors.shape
    shape = hidden_states.shape
    return (
        out.reshape(shape),
        grad_hidden.reshape(shape),
        dlogits,
        o_top[:cut],
        jnp.concatenate([o_low[down:, :down], o_low[down:, down:]], 0),
        o_in,
        o_low[:down].T,
        o_top[cut + extra, : b_in.shape[0]],
        o_top[cut : cut + extra, :high],
    )


def shards_plain(
    hidden_states, prev_logits, lengths, w_qkv, w_out, w_in, w_down, b_in, vectors, cotangent
):
    seqs, rows, _ = hidden_states.shape
    tokens = seqs * rows
    order = jnp.arange(4, dtype=jnp.int32) ^ lax.axis_index("seq")
    half = seqs // 2
    x0 = hidden_states.reshape(tokens, D)
    x1, x2 = swap_core(hidden_states), swap_x(hidden_states)
    x_blocks = (hidden_states, x1, x2, swap_core(x2))
    table = down_table = jnp.zeros((2,), jnp.int32)
    qkv, in_pieces, down_pieces = gather_plain(w_qkv, w_out, w_in, w_down.T)
    f_qkv = qkv[0]
    f_b, f_vec = gather_small(b_in, vectors)
    f_b, f_vec = f_b.astype(F32), f_vec.astype(F32)
    made = [
        lead(
            table, order, lengths, x_blocks, (h * half,) * 4, half, h * half, qkv,
            prev_logits, f_vec,
        )
        for h in range(2)
    ]
    ctx = [m[2].reshape(-1, D) for m in made]
    out, dh1, dctx, dinner, y1, dvec, db_in, act, dbranch, dattn = middle(
        table, down_table, x0, *ctx, cotangent.reshape(tokens, D), f_vec, f_b, in_pieces, down_pieces
    )
    dctx = dctx.reshape(seqs, rows, D)
    dlogits, dq, dkv = None, [], []
    for h in range(2):
        dlogits, dq_h, dkv_h = attend_back(
            order, made[h][0], made[h][1], made[h][3], dctx, dlogits, h * half, seqs
        )
        dq.append(dq_h)
        dkv.append(dkv_h)
    got_far = [swap_core(dkv[h][3]) for h in range(2)]
    far = [grad_far(dkv[h][2], got_far[h], f_qkv) for h in range(2)]
    got_rows = [swap_x(f) for f in far]
    got_kv = [swap_core(dkv[h][1]) for h in range(2)]
    dkv0 = [dkv[h][0] for h in range(2)]
    dx = grad_own(dkv0, got_kv, dq, dh1, f_qkv)
    whole = lambda pair: jnp.concatenate(pair, 0)
    grad_hidden = low(dx + whole(got_rows).astype(F32))
    sum0 = whole([low(add(a, b)) for a, b in zip(dkv0, got_kv)])
    sum2 = whole([low(add(dkv[h][2], got_far[h])) for h in range(2)])
    dq = whole(dq)
    g_kv = mm_tn(x0, sum0) + mm_tn(x2.reshape(tokens, D), sum2)
    g_qkv = jnp.concatenate([mm_tn(x0, dq), g_kv], 1)
    dvec = dvec.at[0].add(jnp.sum(dq, 0, dtype=F32))
    dvec = dvec.at[1].add(jnp.sum(add(sum0[:, D:], sum2[:, D:]), 0))
    o_b, o_vec = reduce_small(db_in, dvec)
    shape = hidden_states.shape
    return (
        out.reshape(shape),
        grad_hidden.reshape(shape),
        dlogits,
        reduce_plain(g_qkv, "dp", "seq"),
        reduce_plain(mm_tn(whole(ctx), dattn), "dp", "seq"),
        reduce_plain(mm_tn(y1, dinner), "dp", "seq"),
        reduce_plain(mm_tn(act, dbranch), "dp", "seq"),
        o_b,
        o_vec,
    )


def shards(*args):
    return (shards_apart if by_pieces() else shards_plain)(*args)


def solution(mesh):
    return jax.shard_map(
        shards,
        mesh=mesh,
        in_specs=(
            P("dp", "seq", None),
            P("dp", None, "seq", None),
            P("dp"),
            P("dp", "seq"),
            P("dp", "seq"),
            P("dp", "seq"),
            P("dp", "seq"),
            P(("dp", "seq")),
            P("seq", "dp"),
            P("dp", "seq", None),
        ),
        out_specs=(
            P("dp", "seq", None),
            P("dp", "seq", None),
            P("dp", None, "seq", None),
            P("dp", "seq"),
            P("dp", "seq"),
            P("dp", "seq"),
            P("dp", "seq"),
            P(("dp", "seq")),
            P("seq", "dp"),
        ),
        check_vma=False,
    )
```

```python
import functools

import jax
import jax.numpy as jnp
from jax import lax
from jax.experimental import pallas as pl
from jax.experimental.pallas import tpu as pltpu
from jax.sharding import PartitionSpec as P

D = 768
HEADS = 12
HEAD_DIM = 64
PAIRS = HEADS // 2
PAIR = 2 * HEAD_DIM
SCALE = HEAD_DIM ** (-0.5)
BF = jnp.bfloat16
F32 = jnp.float32
BOTH = ("dp", "seq")
MIB = 1 << 20
PAD = 64
ANY = pl.BlockSpec(memory_space=pl.ANY)
GRANT = 60 * MIB


def mm(a, b):
    return lax.dot_general(a, b, (((1,), (0,)), ((), ())), preferred_element_type=F32)


def mm_nt(a, b):
    return lax.dot_general(a, b, (((1,), (1,)), ((), ())), preferred_element_type=F32)


def mm_tn(a, b):
    return lax.dot_general(a, b, (((0,), (0,)), ((), ())), preferred_element_type=F32)


def stack_heads(pair):
    lane = lax.broadcasted_iota(jnp.int32, pair.shape, 1)
    zero = jnp.zeros_like(pair)
    return jnp.concatenate(
        [jnp.where(lane < HEAD_DIM, pair, zero), jnp.where(lane < HEAD_DIM, zero, pair)], 0
    )


def pick_heads(stacked):
    rows = stacked.shape[0] // 2
    lane = lax.broadcasted_iota(jnp.int32, (rows, PAIR), 1)
    return jnp.where(lane < HEAD_DIM, stacked[:rows], stacked[rows:])


def swap(a, axis, bit):
    size = lax.axis_size(axis)
    return lax.ppermute(a, axis, [(i, i ^ bit) for i in range(size)])


def swap_core(a):
    return swap(a, "seq", 1)


def swap_x(a):
    return swap(a, "seq", 2)


def swap_y(a):
    return swap(a, "dp", 1)


def swap_z(a, places):
    return swap(a, "dp", 2 * places)


def turn_z(a):
    size = lax.axis_size("dp")
    return lax.ppermute(a, "dp", [(i, (i + 2) % size) for i in range(size)])


def by_pieces():
    return lax.axis_size("dp") == 8 and lax.axis_size("seq") == 4


def place():
    dp, seq = lax.axis_index("dp"), lax.axis_index("seq")
    return dp >> 1, dp & 1, seq >> 1, seq & 1


def stack_z_direct(a):
    return jnp.stack([a] + [swap_z(a, k) for k in range(1, 4)])


def piece_table():
    z, y, x, core = place()
    table = []
    for far in range(8):
        for k in range(4):
            table.append(2 * (z ^ k) + (y ^ (far >> 1 & 1)))
            table.append(2 * (x ^ (far & 1)) + (core ^ (far >> 2)))
    return jnp.stack(table).astype(jnp.int32)


def turned_table():
    z, y, x, core = place()
    table = []
    for far in range(8):
        for k in range(4):
            table.append(2 * ((z - (far & 3)) & 3) + (y ^ (k >> 1)))
            table.append(2 * (x ^ (k & 1)) + (core ^ (far >> 2)))
    return jnp.stack(table).astype(jnp.int32)


def pieces_of(refs, table_ref):
    for a, ref in enumerate(refs):
        depth = ref.shape[0]
        for k in range(depth):
            n = a * depth + k
            yield ref.at[k], table_ref[2 * n], table_ref[2 * n + 1]


def wait_whole(ref, sem):
    pltpu.make_async_copy(ref, ref, sem).wait()


def add(*parts):
    return sum(p.astype(F32) for p in parts)


def low(a):
    return a.astype(BF)


def after(a, *done):
    return lax.optimization_barrier((a,) + done)[0]


def load_qkv(table_ref, piece_refs, w_all, vec_ref, b_ref, stage, sems):
    high, wide = D // 8, 3 * D // 4
    for piece, dp, seq in pieces_of(piece_refs, table_ref):
        rows = pl.ds(pl.multiple_of(dp * high, high), high)
        pltpu.make_async_copy(piece, stage.at[seq, rows], sems.at[0]).start()
    wait_whole(stage, sems.at[0])
    for s in range(4):
        for d in range(8):
            top = d * high
            rows = slice(top, top + high)
            w_all[rows, s * wide : (s + 1) * wide] = stage[s, rows, :wide]
            extra = stage[s, top : top + 16, wide:].astype(F32)
            at = (4 * d + s) * high
            for n, (ref, row, left) in enumerate(
                ((vec_ref, 2 * s, top), (vec_ref, 2 * s + 1, top), (b_ref, 0, at))
            ):
                right = left + high - PAD
                ref[row : row + 1, left : left + PAD] = extra[2 * n : 2 * n + 1]
                ref[row : row + 1, right : right + PAD] = extra[2 * n + 1 : 2 * n + 2]


def small_rows(a):
    return jnp.stack([a[:, :PAD], a[:, -PAD:]], 1).reshape(-1, PAD)


def from_small_rows(a, width):
    return jnp.concatenate([a[0::2], a[1::2, 2 * PAD - width :]], 1)


def lead_kernel(count, assemble, first, table_ref, order_ref, len_ref, *refs):
    x_refs, refs = refs[:4], refs[4:]
    piece_refs, refs = refs[:count], refs[count:]
    if assemble:
        prev_ref, q_ref, kv_ref, ctx_ref, probs_ref, w_ref, vec_ref, b_ref = refs[:8]
    else:
        vec_ref, prev_ref, q_ref, kv_ref, ctx_ref, probs_ref = refs[:6]
    w_all, x_all, stage, sems = refs[-4:]
    rows, total = q_ref.shape[1], x_all.shape[0]

    @pl.when(pl.program_id(0) == 0)
    def _():
        if assemble:
            load_qkv(table_ref, piece_refs, w_all, vec_ref, b_ref, stage, sems)
            pltpu.make_async_copy(w_all, w_ref, sems.at[1]).start()
        else:
            pltpu.make_async_copy(piece_refs[0], w_all, sems.at[0]).start()
            wait_whole(w_all, sems.at[0])

    for j in range(4):
        start = pl.multiple_of(order_ref[j] * rows, rows)
        x_all[pl.ds(start, rows), :] = x_refs[j][0]
    valid = len_ref[first + pl.program_id(0)]
    key_pos = lax.broadcasted_iota(jnp.int32, (1, total), 1)
    padding = jnp.where(key_pos < valid, 0.0, -1e9)

    def project(g):
        width = 2 * PAIR
        cols = slice(g * width, (g + 1) * width)
        part = lambda n: slice(n * D + g * width, n * D + (g + 1) * width)
        query = (mm(x_refs[0][0], w_all[:, cols]) + vec_ref[0:1, cols]).astype(BF)
        q_ref[0, :, cols] = query * SCALE
        kv_ref[0, :, cols] = mm(x_all[...], w_all[:, part(1)]).astype(BF)
        value = mm(x_all[...], w_all[:, part(2)]) + vec_ref[1:2, cols]
        kv_ref[0, :, part(1)] = value.astype(BF)

    def score(i):
        cols = slice(i * PAIR, (i + 1) * PAIR)
        raw = mm_nt(stack_heads(q_ref[0, :, cols]), kv_ref[0, :, cols])
        prev = prev_ref[0, 2 * i : 2 * i + 2].reshape(2 * rows, total).astype(F32)
        return raw + (prev + padding)

    def mix(i, raw):
        cols = slice(i * PAIR, (i + 1) * PAIR)
        vcols = slice(D + i * PAIR, D + (i + 1) * PAIR)
        largest = jnp.max(raw, -1, keepdims=True)
        expo = jnp.exp(raw - largest)
        summed = jnp.sum(expo, -1, keepdims=True)
        probs = (expo * (1.0 / summed)).astype(BF)
        probs_ref[0, 2 * i : 2 * i + 2] = probs.reshape(2, rows, total)
        ctx_ref[0, :, cols] = pick_heads(mm(probs, kv_ref[0, :, vcols])).astype(BF)

    project(0)
    raw = score(0)
    for i in range(PAIRS):
        if i % 2 == 0 and i + 2 < PAIRS:
            project(i // 2 + 1)
        later = score(i + 1) if i + 1 < PAIRS else None
        mix(i, raw)
        raw = later

    if assemble:

        @pl.when(pl.program_id(0) == pl.num_programs(0) - 1)
        def _():
            pltpu.make_async_copy(w_all, w_ref, sems.at[1]).wait()


def lead(table, order, lengths, x_blocks, starts, seqs, first, pieces, prev_logits, vec=None):
    assemble = vec is None
    rows = x_blocks[0].shape[1]
    total = prev_logits.shape[-1]
    ff = 4 * D

    def x_spec(j):
        return pl.BlockSpec((1, rows, D), lambda b, *_: (starts[j] + b, 0, 0))

    fixed = lambda *shape: pl.BlockSpec(shape, lambda b, *_: (0, 0))
    row_spec = pl.BlockSpec((1, rows, D), lambda b, *_: (b, 0, 0))
    sds = jax.ShapeDtypeStruct
    out_specs = [
        row_spec,
        pl.BlockSpec((1, total, 2 * D), lambda b, *_: (b, 0, 0)),
        row_spec,
        pl.BlockSpec((1, HEADS, rows, total), lambda b, *_: (b, 0, 0, 0)),
    ]
    out_shape = [
        sds((seqs, rows, D), BF),
        sds((seqs, total, 2 * D), BF),
        sds((seqs, rows, D), BF),
        sds((seqs, HEADS, rows, total), BF),
    ]
    if assemble:
        out_specs += [ANY, fixed(8, D), fixed(1, ff)]
        out_shape += [sds((D, 3 * D), BF), sds((8, D), F32), sds((1, ff), F32)]
    stage = (4, D, 3 * D // 4 + PAD) if assemble else (1, 16, 128)
    return pl.pallas_call(
        functools.partial(lead_kernel, len(pieces), assemble, first),
        grid_spec=pltpu.PrefetchScalarGridSpec(
            num_scalar_prefetch=3,
            grid=(seqs,),
            in_specs=[x_spec(j) for j in range(4)]
            + [ANY] * len(pieces)
            + ([] if assemble else [fixed(8, D)])
            + [
                pl.BlockSpec(
                    (1, HEADS, rows, total), lambda b, *_: (first + b, 0, 0, 0)
                )
            ],
            out_specs=out_specs,
            scratch_shapes=[
                pltpu.VMEM((D, 3 * D), BF),
                pltpu.VMEM((total, D), BF),
                pltpu.VMEM(stage, BF),
                pltpu.SemaphoreType.DMA((2,)),
            ],
        ),
        out_shape=out_shape,
        compiler_params=pltpu.CompilerParams(vmem_limit_bytes=GRANT),
        cost_estimate=pl.CostEstimate(
            flops=seqs * rows * D * (18 * D + 4 * total),
            bytes_accessed=seqs * 8 * MIB,
            transcendentals=seqs * HEADS * rows * total,
        ),
    )(table, order, lengths, *x_blocks, *pieces, *([] if assemble else [vec]), prev_logits)


def attend_back_kernel(order_ref, q_ref, kv_ref, probs_ref, dctx_ref, *refs):
    dlogits_ref, dq_ref, *dkv_refs, dkv_all = refs[-7:]
    rows = q_ref.shape[1]
    total = dkv_all.shape[0]

    def ahead(i):
        cols = slice(i * PAIR, (i + 1) * PAIR)
        vcols = slice(D + i * PAIR, D + (i + 1) * PAIR)
        dctx = stack_heads(dctx_ref[0, :, cols])
        return dctx, mm_nt(dctx, kv_ref[0, :, vcols])

    dctx, dprobs = ahead(0)
    for i in range(PAIRS):
        later = ahead(i + 1) if i + 1 < PAIRS else (None, None)
        cols = slice(i * PAIR, (i + 1) * PAIR)
        vcols = slice(D + i * PAIR, D + (i + 1) * PAIR)
        probs = probs_ref[0, 2 * i : 2 * i + 2].reshape(2 * rows, total)
        dkv_all[:, vcols] = mm_tn(probs, dctx).astype(BF)
        wide = probs.astype(F32)
        prod = wide * dprobs
        weighted = jnp.sum(prod, -1, keepdims=True)
        dlogits = (prod - wide * weighted).astype(BF)
        dlogits_ref[0, 2 * i : 2 * i + 2] = dlogits.reshape(2, rows, total)
        dq_ref[0, :, cols] = (pick_heads(mm(dlogits, kv_ref[0, :, cols])) * SCALE).astype(BF)
        dkv_all[:, cols] = mm_tn(dlogits, stack_heads(q_ref[0, :, cols])).astype(BF)
        dctx, dprobs = later
    for j in range(4):
        start = pl.multiple_of(order_ref[j] * rows, rows)
        dkv_refs[j][0] = dkv_all[pl.ds(start, rows), :]


def attend_back(order, queries, keys_values, probs, dctx, dlogits, first, seqs_all, deps=()):
    seqs, rows, _ = queries.shape
    blocks = 4
    total = probs.shape[-1]
    row_spec = lambda width: pl.BlockSpec((1, rows, width), lambda b, *_: (b, 0, 0))
    late_spec = lambda width: pl.BlockSpec((1, rows, width), lambda b, *_: (first + b, 0, 0))
    head_spec = pl.BlockSpec((1, HEADS, rows, total), lambda b, *_: (b, 0, 0, 0))
    late_head = pl.BlockSpec((1, HEADS, rows, total), lambda b, *_: (first + b, 0, 0, 0))
    more = ([] if dlogits is None else [dlogits]) + list(deps)
    outs = pl.pallas_call(
        attend_back_kernel,
        grid_spec=pltpu.PrefetchScalarGridSpec(
            num_scalar_prefetch=1,
            grid=(seqs,),
            in_specs=[
                row_spec(D),
                pl.BlockSpec((1, total, 2 * D), lambda b, *_: (b, 0, 0)),
                head_spec,
                late_spec(D),
            ]
            + [ANY] * len(more),
            out_specs=[late_head, row_spec(D)] + [row_spec(2 * D)] * blocks,
            scratch_shapes=[pltpu.VMEM((total, 2 * D), BF)],
        ),
        out_shape=[
            jax.ShapeDtypeStruct((seqs_all, HEADS, rows, total), BF),
            jax.ShapeDtypeStruct(queries.shape, BF),
        ]
        + [jax.ShapeDtypeStruct((seqs, rows, 2 * D), BF)] * blocks,
        input_output_aliases={} if dlogits is None else {5: 0},
        compiler_params=pltpu.CompilerParams(vmem_limit_bytes=GRANT),
        cost_estimate=pl.CostEstimate(
            flops=8 * seqs * HEADS * rows * total * PAIR,
            bytes_accessed=4 * seqs * HEADS * rows * total,
            transcendentals=0,
        ),
    )(order, queries, keys_values, probs, dctx, *more)
    dkv = [b.reshape(seqs * rows, 2 * D) for b in outs[2:]]
    return outs[0], outs[1].reshape(seqs * rows, D), dkv


def gelu_and_slope(values):
    cdf = 0.5 * lax.erf(values * 0.7071067811865476) + 0.5
    bell = jnp.exp(values * values * -0.5)
    return values * cdf, cdf + values * bell * 0.3989422804014327


def norm(values):
    average = jnp.mean(values, -1, keepdims=True)
    centred = values - average
    inverse = lax.rsqrt(jnp.mean(centred * centred, -1, keepdims=True) + 1e-06)
    return centred * inverse, inverse


def norm_back(grad, normed, inverse):
    first = jnp.mean(grad, -1, keepdims=True)
    second = jnp.mean(grad * normed, -1, keepdims=True)
    return inverse * (grad - first - normed * second)


def load_middle(table_ref, down_table_ref, in_refs, down_refs, w_out_ref, w_in_ref, w_down_ref, stage, sems):
    if len(in_refs) == 1:
        ff = w_in_ref.shape[1]
        pltpu.make_async_copy(down_refs[1], w_out_ref, sems.at[0]).start()
        for c in range(4):
            cols = pl.ds(c * (ff // 4), ff // 4)
            pltpu.make_async_copy(
                in_refs[0].at[:, cols], w_in_ref.at[:, cols], sems.at[1 + c]
            ).start()
            pltpu.make_async_copy(
                down_refs[0].at[:, cols], w_down_ref.at[:, cols], sems.at[5 + c]
            ).start()
        wait_whole(w_out_ref, sems.at[0])
    else:
        down = w_down_ref.shape[0] // 4
        wide = w_down_ref.shape[1] // 8
        high, half = D // 8, D // 16
        for piece, dp, seq in pieces_of(down_refs, down_table_ref):
            pltpu.make_async_copy(
                piece.at[pl.ds(down, half)], stage.at[seq, dp], sems.at[0]
            ).start()
        for piece, dp, seq in pieces_of(in_refs, table_ref):
            rows = pl.ds(pl.multiple_of(dp * high, high), high)
            cols = pl.ds(pl.multiple_of(seq * D, D), D)
            pltpu.make_async_copy(piece, w_in_ref.at[rows, cols], sems.at[1 + seq]).start()
        for piece, dp, seq in pieces_of(down_refs, down_table_ref):
            rows = pl.ds(pl.multiple_of(seq * down, down), down)
            cols = pl.ds(pl.multiple_of(dp * wide, wide), wide)
            pltpu.make_async_copy(
                piece.at[pl.ds(0, down)], w_down_ref.at[rows, cols], sems.at[5 + (dp >> 1)]
            ).start()
        wait_whole(stage, sems.at[0])
        for s in range(4):
            for d in range(8):
                cols = slice(s * down, (s + 1) * down)
                w_out_ref[d * high : d * high + half, cols] = stage[s, d][:, :down]
                w_out_ref[d * high + half : (d + 1) * high, cols] = stage[s, d][:, down:]


def middle_kernel(
    counts, fused, table_ref, down_table_ref, where_ref, x_ref, ctx_a_ref, ctx_b_ref, cot_ref,
    vec_ref, b_in_ref, *refs
):
    in_refs, refs = refs[: counts[0]], refs[counts[0] :]
    down_refs, refs = refs[: counts[1]], refs[counts[1] :]
    out_ref, dh1_ref, dctx_ref, dinner_ref, y1_ref, dvec_ref, db_in_ref = refs[:7]
    if fused:
        send_ref, keep_ref, act_all, dbranch_all, dattn_all, ctx_all, grad_out = refs[7:14]
    else:
        act_all, dbranch_all, dattn_all = refs[7:10]
    w_out_ref, w_in_ref, w_down_ref, stage, sems = refs[-5:]
    step = pl.program_id(0)
    rows = x_ref.shape[0]
    parts = pl.num_programs(0) - (4 if fused else 0)

    def token_rows():
        middle_rows(
            parts, table_ref, down_table_ref, x_ref, ctx_a_ref, ctx_b_ref, cot_ref, vec_ref,
            b_in_ref, in_refs, down_refs, out_ref, dh1_ref, dctx_ref, dinner_ref, y1_ref,
            dvec_ref, db_in_ref, act_all, dbranch_all, dattn_all, ctx_all if fused else None,
            w_out_ref, w_in_ref, w_down_ref, stage, sems,
        )

    if not fused:
        token_rows()
        return

    pl.when(step < parts)(token_rows)

    @pl.when(step == parts)
    def _():
        grad_out[...] = mm_tn(ctx_all[...], dattn_all[...]).astype(BF)

    @pl.when(step >= parts)
    def _():
        grad_down(where_ref, step - parts, dbranch_all, act_all, grad_out, send_ref, keep_ref)


def grad_down(where_ref, step, dbranch_ref, act_ref, grad_out, send_ref, keep_ref):
    y, x, core = where_ref[1], where_ref[2], where_ref[3]
    wide, down = D // 2, D // 4
    high, half = D // 8, D // 16
    first = core == 0

    def put(far_y, far_x, rows, cols, even, odd):
        keep_ref[far_y, far_x, 0, rows, cols] = jnp.where(first, even, odd)
        send_ref[far_y, far_x, 0, rows, cols] = jnp.where(first, odd, even)

    cols = pl.ds(pl.multiple_of(step * D, D), D)
    grad = mm_tn(dbranch_ref[...], act_ref[:, cols]).astype(BF)
    for j in range(2):
        top = pl.multiple_of((2 * step + j) * high, high)
        upper, lower = grad_out[pl.ds(top, half), :], grad_out[pl.ds(top + half, half), :]
        for i in range(2):
            pair = [slice((2 * i + k) * down, (2 * i + k + 1) * down) for k in range(2)]
            side = slice(j * wide, (j + 1) * wide)
            far = (y ^ j, x ^ i)
            put(*far, slice(0, down), slice(None), grad[pair[0], side], grad[pair[1], side])
            tail = slice(down, down + half)
            put(*far, tail, slice(0, down), upper[:, pair[0]], upper[:, pair[1]])
            put(*far, tail, slice(down, 2 * down), lower[:, pair[0]], lower[:, pair[1]])


def middle_rows(
    parts, table_ref, down_table_ref, x_ref, ctx_a_ref, ctx_b_ref, cot_ref, vec_ref,
    b_in_ref, in_refs, down_refs, out_ref, dh1_ref, dctx_ref, dinner_ref, y1_ref,
    dvec_ref, db_in_ref, act_all, dbranch_all, dattn_all, ctx_all,
    w_out_ref, w_in_ref, w_down_ref, stage, sems,
):
    step, rows = pl.program_id(0), x_ref.shape[0]
    here = pl.ds(pl.multiple_of(step * rows, rows), rows)
    wide = act_all.shape[1] // 4

    @pl.when(step == 0)
    def _():
        load_middle(
            table_ref, down_table_ref, in_refs, down_refs,
            w_out_ref, w_in_ref, w_down_ref, stage, sems,
        )
        for c in range(4):
            wait_whole(w_in_ref.at[:, pl.ds(c * wide, wide)], sems.at[1 + c])
            wait_whole(w_down_ref.at[:, pl.ds(c * wide, wide)], sems.at[5 + c])
        dvec_ref[...] = jnp.zeros_like(dvec_ref)
        db_in_ref[...] = jnp.zeros_like(db_in_ref)

    vec = lambda i: vec_ref[i : i + 1, :]
    total = lambda v: jnp.sum(v, 0, keepdims=True)

    ctx = jnp.where(step < parts // 2, ctx_a_ref[...], ctx_b_ref[...])
    if ctx_all is not None:
        ctx_all[here, :] = ctx
    h1 = x_ref[...].astype(F32) + (mm(ctx, w_out_ref[...]) + vec(2))
    normed1, inverse1 = norm(h1)
    y1 = normed1 * vec(3) + vec(4)
    y1_low = y1.astype(BF)
    y1_ref[...] = y1_low
    h2 = y1 + vec(5)
    part = lambda c: slice(c * wide, (c + 1) * wide)
    expand = lambda c: mm(y1_low, w_in_ref[:, part(c)]) + b_in_ref[:, part(c)]
    slopes, ahead = [], expand(0)
    for c in range(4):
        cols = part(c)
        inner = ahead
        if c < 3:
            ahead = expand(c + 1)
        act, slope = gelu_and_slope(inner)
        act = act.astype(BF)
        act_all[here, cols] = act
        slopes.append(slope)
        h2 = h2 + mm_nt(act, w_down_ref[:, cols])
    normed2, inverse2 = norm(h2)
    out_ref[...] = (normed2 * vec(6) + vec(7)).astype(BF)
    cot = cot_ref[...].astype(F32)
    dh2 = norm_back(cot * vec(6), normed2, inverse2)
    dbranch = dh2.astype(BF)
    dbranch_all[here, :] = dbranch
    dvec_ref[5:6, :] += total(dbranch.astype(F32))
    dvec_ref[6:7, :] += total(cot * normed2)
    dvec_ref[7:8, :] += total(cot)
    dy1, ahead = dh2, mm(dbranch, w_down_ref[:, part(0)])
    for c in range(4):
        cols = part(c)
        dact = ahead
        if c < 3:
            ahead = mm(dbranch, w_down_ref[:, part(c + 1)])
        dinner = (dact * slopes[c]).astype(BF)
        dinner_ref[:, cols] = dinner
        db_in_ref[:, cols] += total(dinner.astype(F32))
        dy1 = dy1 + mm_nt(dinner, w_in_ref[:, cols])
    dh1 = norm_back(dy1 * vec(3), normed1, inverse1)
    dh1_ref[...] = dh1
    dattn = dh1.astype(BF)
    dattn_all[here, :] = dattn
    dctx_ref[...] = mm_nt(dattn, w_out_ref[...]).astype(BF)
    dvec_ref[2:3, :] += total(dattn.astype(F32))
    dvec_ref[3:4, :] += total(dy1 * normed1)
    dvec_ref[4:5, :] += total(dy1)


def middle(table, down_table, x, ctx_a, ctx_b, cot, vectors, b_in, in_pieces, down_pieces, where=None):
    tokens = x.shape[0]
    ff = b_in.shape[1]
    step = 256
    parts = tokens // step
    half = parts // 2
    fused = where is not None
    late = lambda i: jnp.minimum(i, parts - 1)
    rows = lambda width: pl.BlockSpec((step, width), lambda i, *_: (late(i), 0))
    ctx_specs = [
        pl.BlockSpec((step, D), lambda i, *_: (jnp.minimum(i, half - 1), 0)),
        pl.BlockSpec((step, D), lambda i, *_: (jnp.clip(i - half, 0, half - 1), 0)),
    ]
    whole = lambda *shape: pl.BlockSpec(shape, lambda i, *_: (0, 0))
    sds = jax.ShapeDtypeStruct
    counts = (len(in_pieces), len(down_pieces))
    out_specs = [rows(D)] * 3 + [rows(ff), rows(D), whole(8, D), whole(1, ff)]
    out_shape = [
        sds((tokens, D), BF),
        sds((tokens, D), F32),
        sds((tokens, D), BF),
        sds((tokens, ff), BF),
        sds((tokens, D), BF),
        sds((8, D), F32),
        sds((1, ff), F32),
    ]
    scratch = []
    if fused:
        piece = (D // 4 + D // 16, ff // 8)
        spec = pl.BlockSpec(
            (2, 2, 1) + piece,
            lambda i, t, d, w: (0, 0, jnp.maximum(i - parts, 0) ^ w[0], 0, 0),
        )
        out_specs += [spec, spec]
        out_shape += [sds((2, 2, 4) + piece, BF)] * 2
        scratch = [pltpu.VMEM((tokens, ff), BF)] + [pltpu.VMEM((tokens, D), BF)] * 3
        scratch += [pltpu.VMEM((D, D), BF)]
    else:
        out_specs += [whole(tokens, ff), whole(tokens, D), whole(tokens, D)]
        out_shape += [sds((tokens, ff), BF), sds((tokens, D), BF), sds((tokens, D), BF)]
        where = jnp.zeros((4,), jnp.int32)
    return pl.pallas_call(
        functools.partial(middle_kernel, counts, fused),
        grid_spec=pltpu.PrefetchScalarGridSpec(
            num_scalar_prefetch=3,
            grid=(parts + 4 if fused else parts,),
            in_specs=[rows(D)]
            + ctx_specs
            + [rows(D), whole(8, D), whole(1, ff)]
            + [ANY] * sum(counts),
            out_specs=out_specs,
            scratch_shapes=scratch
            + [
                pltpu.VMEM((D, D), BF),
                pltpu.VMEM((D, ff), BF),
                pltpu.VMEM((D, ff), BF),
                pltpu.VMEM((4, 8, D // 16, ff // 8), BF),
                pltpu.SemaphoreType.DMA((9,)),
            ],
        ),
        out_shape=out_shape,
        compiler_params=pltpu.CompilerParams(vmem_limit_bytes=GRANT),
        cost_estimate=pl.CostEstimate(
            flops=tokens * (10 * D * ff + 6 * D * D),
            bytes_accessed=30 * MIB,
            transcendentals=2 * tokens * ff,
        ),
    )(table, down_table, where, x, ctx_a, ctx_b, cot, vectors, b_in, *in_pieces, *down_pieces)


def grad_in_kernel(where_ref, y1_ref, dinner_ref, *refs):
    send_ref, keep_ref = refs[-2:]
    z, y = where_ref[0], where_ref[1]
    step = pl.program_id(0)
    high = D // 8
    grad = mm_tn(y1_ref[...], dinner_ref[...]).astype(BF)

    def put(ref):
        for d in range(8):
            ref[0, y ^ (d & 1), (d >> 1) ^ z] = grad[d * high : (d + 1) * high]

    @pl.when(step < 2)
    def _():
        put(send_ref)

    @pl.when(step >= 2)
    def _():
        put(keep_ref)


def grad_in(where, y1, dinner, deps=()):
    tokens, ff = dinner.shape
    wide = ff // 4

    def columns(t, where):
        return (0, 2 * (where[2] ^ (t & 1)) + (where[3] ^ (1 - (t >> 1))))

    piece = (1, 2, 4, D // 8, wide)
    shape = jax.ShapeDtypeStruct((2, 2, 4, D // 8, wide), BF)
    return pl.pallas_call(
        grad_in_kernel,
        grid_spec=pltpu.PrefetchScalarGridSpec(
            num_scalar_prefetch=1,
            grid=(4,),
            in_specs=[
                pl.BlockSpec((tokens, D), lambda t, w: (0, 0)),
                pl.BlockSpec((tokens, wide), columns),
            ]
            + [ANY] * len(deps),
            out_specs=[
                pl.BlockSpec(piece, lambda t, w: (jnp.minimum(t, 1), 0, 0, 0, 0)),
                pl.BlockSpec(piece, lambda t, w: (jnp.maximum(t - 2, 0), 0, 0, 0, 0)),
            ],
        ),
        out_shape=[shape, shape],
        compiler_params=pltpu.CompilerParams(vmem_limit_bytes=GRANT),
        cost_estimate=pl.CostEstimate(
            flops=2 * tokens * D * ff, bytes_accessed=14 * MIB, transcendentals=0
        ),
    )(where, y1, dinner, *deps)


def grad_qkv_kernel(where_ref, x0_ref, *refs):
    x2_refs, refs = refs[:2], refs[2:]
    dq_refs, refs = refs[:2], refs[2:]
    own_refs, refs = refs[:4], refs[4:]
    far_refs, refs = refs[:4], refs[4:]
    dvec_ref, db_ref = refs[:2]
    *out_refs, grad, dvec = refs[-6:]
    z, y, x, core = (where_ref[i] for i in range(4))
    step = pl.program_id(0)
    wide, high = 3 * D // 4, D // 8
    cut = out_refs[0].shape[3]
    part = x2_refs[0].shape[0]
    x0 = lambda h: x0_ref[h * part : (h + 1) * part]

    @pl.when(step == 0)
    def _():
        total = mm_tn(x0(0), dq_refs[0][...]) + mm_tn(x0(1), dq_refs[1][...])
        grad[:, :D] = total.astype(BF)
        dvec[...] = dvec_ref[...]
        for ref in dq_refs:
            dvec[0:1, :] += jnp.sum(ref[...].astype(F32), 0, keepdims=True)

    def emit():
        first = core == 0
        for i in range(2):
            even = grad[:, 2 * i * wide : (2 * i + 1) * wide]
            odd = grad[:, (2 * i + 1) * wide : (2 * i + 2) * wide]
            kept = jnp.where(first, even, odd)
            sent = jnp.where(first, odd, even)
            for d in range(8):
                top, far_z = d * high, (d >> 1) ^ z
                upper = (y ^ (d & 1), x ^ i, far_z)
                lower = (x ^ i, y ^ (d & 1), far_z)
                extra = []
                for k in range(2):
                    s = 2 * i + k
                    at = (4 * d + s) * high
                    rows = []
                    for ref, row, left in (
                        (dvec, 2 * s, top), (dvec, 2 * s + 1, top), (db_ref, 0, at)
                    ):
                        right = left + high - PAD
                        rows.append(ref[row : row + 1, left : left + PAD])
                        rows.append(ref[row : row + 1, right : right + PAD])
                    rows.append(jnp.zeros((cut - len(rows), PAD), F32))
                    extra.append(jnp.concatenate(rows, 0))
                main, side = slice(0, wide), slice(wide, wide + PAD)
                every = slice(None)
                pairs = ((sent, extra[1], extra[0]), (kept, extra[0], extra[1]))
                for n, (part, one, other) in enumerate(pairs):
                    out_refs[n][upper + (every, main)] = part[top : top + cut]
                    out_refs[n][upper + (every, side)] = jnp.where(first, one, other).astype(BF)
                    out_refs[2 + n][lower + (every, main)] = part[top + cut : top + high]
                    out_refs[2 + n][lower + (every, side)] = jnp.zeros((high - cut, PAD), BF)

    for t in (1, 2):

        @pl.when(step == t)
        def _():
            total = None
            for h in range(2):
                own, far = (
                    low(add(refs[h][...], refs[2 + h][...])) for refs in (own_refs, far_refs)
                )
                if t == 2:
                    both = jnp.sum(own.astype(F32), 0, keepdims=True)
                    dvec[1:2, :] += both + jnp.sum(far.astype(F32), 0, keepdims=True)
                piece = mm_tn(x0(h), own) + mm_tn(x2_refs[h][...], far)
                total = piece if total is None else total + piece
            grad[:, t * D : (t + 1) * D] = total.astype(BF)
            if t == 2:
                emit()


def grad_qkv(where, x0, x2, dq, own, far, dvec, db_in, deps=()):
    tokens = x0.shape[0]
    fixed = lambda *shape: pl.BlockSpec(shape, lambda t, w: (0, 0))
    half = fixed(tokens // 2, D)
    part = pl.BlockSpec((tokens // 2, D), lambda t, w: (0, jnp.maximum(t - 1, 0)))
    cut = D // 12
    dims = [(2, 2, 4, n, 3 * D // 4 + PAD) for n in (cut, D // 8 - cut) for _ in range(2)]
    return pl.pallas_call(
        grad_qkv_kernel,
        grid_spec=pltpu.PrefetchScalarGridSpec(
            num_scalar_prefetch=1,
            grid=(3,),
            in_specs=[fixed(tokens, D)]
            + [half] * 4
            + [part] * 8
            + [fixed(8, D)]
            + [fixed(*db_in.shape)]
            + [ANY] * len(deps),
            out_specs=[pl.BlockSpec(d, lambda t, w: (0, 0, 0, 0, 0)) for d in dims],
            scratch_shapes=[pltpu.VMEM((D, 3 * D), BF), pltpu.VMEM((8, D), F32)],
        ),
        out_shape=[jax.ShapeDtypeStruct(d, BF) for d in dims],
        compiler_params=pltpu.CompilerParams(vmem_limit_bytes=GRANT),
        cost_estimate=pl.CostEstimate(
            flops=2 * tokens * D * 5 * D, bytes_accessed=16 * MIB, transcendentals=0
        ),
    )(where, x0, *x2, *dq, *own, *far, dvec, db_in, *deps)


def grad_far_kernel(dkv_ref, got_ref, w_ref, *refs):
    total = low(add(dkv_ref[...], got_ref[...]))
    refs[-1][...] = mm_nt(total, w_ref[:, D:]).astype(BF)


def grad_far(dkv, got, w_qkv, deps=()):
    tokens = dkv.shape[0]
    step = 256
    rows = lambda width: pl.BlockSpec((step, width), lambda i: (i, 0))
    return pl.pallas_call(
        grad_far_kernel,
        grid=(tokens // step,),
        in_specs=[
            rows(2 * D),
            rows(2 * D),
            pl.BlockSpec((D, 3 * D), lambda i: (0, 0), pipeline_mode=pl.Buffered(1)),
        ]
        + [ANY] * len(deps),
        out_specs=rows(D),
        out_shape=jax.ShapeDtypeStruct((tokens, D), BF),
        compiler_params=pltpu.CompilerParams(vmem_limit_bytes=GRANT),
        cost_estimate=pl.CostEstimate(
            flops=2 * tokens * D * 2 * D, bytes_accessed=10 * MIB, transcendentals=0
        ),
    )(dkv, got, w_qkv, *deps)


def grad_own_kernel(*refs):
    dkv_refs, refs = refs[:2], refs[2:]
    got_refs, refs = refs[:2], refs[2:]
    dq_refs, refs = refs[:2], refs[2:]
    dh1_ref, w_ref = refs[:2]
    dx_ref = refs[-1]
    early = pl.program_id(0) < pl.num_programs(0) // 2
    pick = lambda pair: jnp.where(early, pair[0][...], pair[1][...])
    total = (pick(dkv_refs).astype(F32) + pick(got_refs).astype(F32)).astype(BF)
    dx = mm_nt(total, w_ref[:, D:]) + mm_nt(pick(dq_refs), w_ref[:, :D])
    dx_ref[...] = dx + dh1_ref[...]


def grad_own(dkv, got, dq, dh1, w_qkv, deps=()):
    tokens = dh1.shape[0]
    step = 256
    half = tokens // step // 2

    def pair(width):
        return [
            pl.BlockSpec((step, width), lambda i: (jnp.minimum(i, half - 1), 0)),
            pl.BlockSpec((step, width), lambda i: (jnp.maximum(i - half, 0), 0)),
        ]

    rows = pl.BlockSpec((step, D), lambda i: (i, 0))
    return pl.pallas_call(
        grad_own_kernel,
        grid=(tokens // step,),
        in_specs=pair(2 * D)
        + pair(2 * D)
        + pair(D)
        + [rows, pl.BlockSpec((D, 3 * D), lambda i: (0, 0), pipeline_mode=pl.Buffered(1))]
        + [ANY] * len(deps),
        out_specs=rows,
        out_shape=jax.ShapeDtypeStruct((tokens, D), F32),
        compiler_params=pltpu.CompilerParams(vmem_limit_bytes=GRANT),
        cost_estimate=pl.CostEstimate(
            flops=2 * tokens * D * 3 * D, bytes_accessed=20 * MIB, transcendentals=0
        ),
    )(*dkv, *got, *dq, dh1, w_qkv, *deps)


def gather_small(b_in, vectors):
    dp, seq = lax.axis_size("dp"), lax.axis_size("seq")
    small = jnp.concatenate([vectors.reshape(-1), b_in])
    whole = lax.all_gather(small, BOTH, axis=0, tiled=False)
    nv = vectors.size
    vec = whole[:, :nv].reshape((dp, seq) + vectors.shape).transpose(1, 2, 0, 3)
    return whole[:, nv:].reshape(1, -1), vec.reshape(8, D)


def reduce_small(g_b, g_vec):
    dp, seq = lax.axis_size("dp"), lax.axis_size("seq")
    vec = g_vec.reshape(seq, 8 // seq, dp, D // dp).transpose(2, 0, 1, 3)
    small = jnp.concatenate([vec.reshape(dp * seq, -1), g_b.reshape(dp * seq, -1)], 1)
    mine = lax.psum_scatter(small, BOTH, scatter_dimension=0, tiled=True)[0]
    nv = 8 * D // (dp * seq)
    return mine[nv:], mine[:nv].reshape(8 // seq, D // dp)


def gather_plain(w_qkv, w_out, w_in, w_down_t):
    both = lambda a, first, second: lax.all_gather(
        lax.all_gather(a, first, axis=0, tiled=True), second, axis=1, tiled=True
    )
    return (
        [both(w_qkv, "dp", "seq")],
        [both(w_in, "dp", "seq")],
        [both(w_down_t, "seq", "dp"), both(w_out, "dp", "seq")],
    )


def reduce_plain(a, first, second):
    part = lax.psum_scatter(a.astype(BF), first, scatter_dimension=0, tiled=True)
    return lax.psum_scatter(part, second, scatter_dimension=1, tiled=True).astype(F32)


def together(*parts):
    return lax.optimization_barrier(parts)


def forward_apart(order, lengths, table, x0, prev_logits, weights):
    w_qkv, w_out, w_in, w_down, b_in, vectors = weights
    seqs = x0.shape[0]
    half = seqs // 2
    cut = w_out.shape[0] // 2
    turned = jnp.concatenate([w_out[:cut], w_out[cut:]], 1)
    down = jnp.concatenate([w_down.T, turned], 0)
    down_x = swap_x(down)
    few = half // 2
    x2_a = swap_x(x0[:few])
    small = small_rows(jnp.concatenate([vectors, b_in.reshape(1, -1)], 0))
    small = jnp.pad(small, ((0, w_qkv.shape[0] - small.shape[0]), (0, 0)))
    qkv = stack_z_direct(jnp.concatenate([w_qkv, small], 1))
    qkv, w_in, x_late, x_b, x_all, down, down_x, x2_a = together(
        qkv, w_in, x0[few:half], x0[half:], x0, down, down_x, x2_a
    )

    qkv_x, qkv_y = swap_x(qkv), swap_y(qkv)
    down = jnp.stack([down, down_x])
    down_y = swap_y(down)
    x2_late = swap_x(x_late)
    in_pair = jnp.stack([w_in, swap_z(w_in, 1)])
    in_got = swap_z(in_pair, 2)
    qkv, qkv_x, qkv_y, x2_late, x_all, in_pair, in_got, x_b, down, down_y = together(
        qkv, qkv_x, qkv_y, x2_late, x_all, in_pair, in_got, x_b, down, down_y
    )
    x2_a = jnp.concatenate([x2_a, x2_late], 0)

    qkv_xy, x2_b = swap_y(qkv_x), swap_x(x_b)
    x1, x3_a, qkv_far = swap_core(x_all), swap_core(x2_a), swap_core(qkv)
    down = [jnp.concatenate([down, down_y], 0)]
    down.append(turn_z(down[0]))
    qkv_xy, x2_b, x1, x3_a, qkv_far, *down = together(qkv_xy, x2_b, x1, x3_a, qkv_far, *down)
    in_own = jnp.concatenate([in_pair, in_got], 0)
    qkv_near = [qkv, qkv_x, qkv_y, qkv_xy]
    qkv_pieces = qkv_near + [qkv_far] + [swap_core(a) for a in qkv_near[1:]]

    in_x, in_y, x3_b = swap_x(in_own), swap_y(in_own), swap_core(x2_b)
    down.append(turn_z(down[1]))
    q_a, kv_a, ctx_a, probs_a, f_qkv, f_vec, f_b = lead(
        table, order, lengths, (x0, x1, x2_a, x3_a), (0, 0, 0, 0), half, 0,
        qkv_pieces, prev_logits,
    )
    in_own, in_x, in_y, x3_b, f_qkv, ctx_a, f_b, *down = together(
        in_own, in_x, in_y, x3_b, f_qkv, ctx_a, f_b, *down
    )

    in_xy = swap_y(in_x)
    in_far = [swap_core(a) for a in (in_own, in_x, in_y)]
    down_far = [swap_core(a) for a in down]
    down.append(turn_z(down[2]))
    q_b, kv_b, ctx_b, probs_b = lead(
        table, order, lengths, (x0, x1, x2_b, x3_b), (half, half, 0, 0), half, half,
        [f_qkv], prev_logits, f_vec,
    )
    in_xy, ctx_b, *both = together(in_xy, ctx_b, *in_far, *down_far, *down)
    in_far, down_far, down = both[:3], both[3:6], both[6:]

    in_pieces = [in_own, in_x, in_y, in_xy] + in_far + [swap_core(in_xy)]
    down_pieces = down + down_far + [swap_core(down[3])]
    first, second = (q_a, kv_a, ctx_a, probs_a), (q_b, kv_b, ctx_b, probs_b)
    return first, second, f_qkv, f_vec, f_b, in_pieces, down_pieces, [x2_a, x2_b]


def shards_apart(
    hidden_states, prev_logits, lengths, w_qkv, w_out, w_in, w_down, b_in, vectors, cotangent
):
    seqs, rows, _ = hidden_states.shape
    tokens = seqs * rows
    half = seqs // 2
    order = jnp.arange(4, dtype=jnp.int32) ^ lax.axis_index("seq")
    table, down_table = piece_table(), turned_table()
    where = jnp.stack(place()).astype(jnp.int32)
    x0 = hidden_states.reshape(tokens, D)
    first, second, f_qkv, f_vec, f_b, in_pieces, down_pieces, x2 = forward_apart(
        order, lengths, table, hidden_states, prev_logits,
        (w_qkv, w_out, w_in, w_down, b_in, vectors),
    )
    rows_of = lambda a: a.reshape(-1, D)
    ctx, x2 = [rows_of(first[2]), rows_of(second[2])], [rows_of(a) for a in x2]
    out, dh1, dctx, dinner, y1, dvec, db_in, d_send, d_keep = middle(
        table, down_table, x0, *ctx, cotangent.reshape(tokens, D), f_vec, f_b,
        in_pieces, down_pieces, where,
    )
    dctx = dctx.reshape(seqs, rows, D)

    d_core = swap_core(d_send)
    i_send, i_keep = grad_in(where, y1, dinner, [d_keep])
    i_core = swap_core(i_send)
    d_core = after(d_core, i_keep)
    d_sent = low(add(d_keep[1], d_core[1]))
    d_one = swap_y(d_sent)
    i_core = after(i_core, d_sent)
    i_sent = low(add(i_keep[1], i_core[1]))
    i_one = swap_x(i_sent)
    dlogits, dq_a, dkv_a = attend_back(
        order, first[0], first[1], first[3], dctx, None, 0, seqs, [d_sent, i_sent]
    )
    far_a, own_a = swap_core(dkv_a[3]), swap_core(dkv_a[1])
    dlogits, dq_b, dkv_b = attend_back(
        order, second[0], second[1], second[3], dctx, dlogits, half, seqs, [dq_a]
    )
    far_b, own_b = swap_core(dkv_b[3]), swap_core(dkv_b[1])
    far_a, own_a = after(far_a, dq_b), after(own_a, dq_b)
    d_one, i_one = after(d_one, dq_b), after(i_one, dq_b)
    d_sent = low(add(d_keep[0, 1], d_core[0, 1], d_one[1]))
    d_two = swap_x(d_sent)
    i_sent = low(add(i_keep[0, 1], i_core[0, 1], i_one[1]))
    i_two = swap_y(i_sent)
    dq, own, far = [dq_a, dq_b], [dkv_a[0], dkv_b[0], own_a, own_b], [dkv_a[2], dkv_b[2], far_a, far_b]
    a_send, a_keep, b_send, b_keep = grad_qkv(where, x0, x2, dq, own, far, dvec, db_in, [d_sent, i_sent])
    d_two, i_two, a_send, b_send = together(d_two, i_two, a_send, b_send)
    a_core, b_core = swap_core(a_send), swap_core(b_send)
    d_part = lambda k: add(d_keep[0, 0, k], d_core[0, 0, k], d_one[0, k], d_two[k])
    i_part = lambda k: add(i_keep[0, 0, k], i_core[0, 0, k], i_one[0, k], i_two[k])
    upper, lower = slice(2, 4), slice(0, 2)
    d_sent, i_sent = low(d_part(upper)), low(i_part(upper))
    i_far, d_far = swap_z(i_sent, 2), swap_z(d_sent, 2)
    a_core, b_core = after(a_core, d_sent, i_sent), after(b_core, d_sent, i_sent)
    a_sent, b_sent = low(add(a_keep[1], a_core[1])), low(add(b_keep[1], b_core[1]))
    a_one, b_one = swap_y(a_sent), swap_x(b_sent)
    dx2_a = grad_far(far[0], far[2], f_qkv, [a_sent, b_sent])
    got_a = swap_x(dx2_a)
    dx2_b = grad_far(far[1], far[3], f_qkv, [dx2_a])
    dx = grad_own(own[:2], own[2:], dq, dh1, f_qkv, [dx2_b])
    a_one, b_one, dx, dx2_b = together(a_one, b_one, dx, dx2_b)
    a_sent = low(add(a_keep[0, 1], a_core[0, 1], a_one[1]))
    b_sent = low(add(b_keep[0, 1], b_core[0, 1], b_one[1]))
    a_two, b_two = swap_x(a_sent), swap_y(b_sent)
    got_b = swap_x(after(dx2_b, a_sent))
    i_far, d_far = after(i_far, a_sent, b_sent), after(d_far, a_sent, b_sent)
    i_last = i_part(lower) + i_far.astype(F32)
    i_end = swap_z(low(i_last[1]), 1)
    d_last = d_part(lower) + d_far.astype(F32)
    d_end = swap_z(low(d_last[1]), 1)
    a_two, b_two, i_last, d_last, got_a = together(a_two, b_two, i_last, d_last, got_a)
    a_part = lambda k: add(a_keep[0, 0, k], a_core[0, 0, k], a_one[0, k], a_two[k])
    b_part = lambda k: add(b_keep[0, 0, k], b_core[0, 0, k], b_one[0, k], b_two[k])
    q_part = lambda k: jnp.concatenate([a_part(k), b_part(k)], 0)
    q_sent = [low(q_part(k)) for k in range(1, 4)]
    q_far = [swap_z(q, k) for q, k in zip(q_sent, range(1, 4))]
    i_end, d_end, dx = after((i_end, d_end, dx), *q_sent)
    o_in = i_last[0] + i_end.astype(F32)
    o_low = d_last[0] + d_end.astype(F32)
    o_top = q_part(0) + add(*q_far)
    got_b = after(got_b, o_top)
    grad_hidden = low(dx + jnp.concatenate([got_a, got_b], 0).astype(F32))
    down, wide, (extra, high) = w_down.shape[1], w_qkv.shape[1], vectors.shape
    o_small = from_small_rows(o_top[: 2 * (extra + 1), wide:], high)
    shape = hidden_states.shape
    return (
        out.reshape(shape),
        grad_hidden.reshape(shape),
        dlogits,
        o_top[:, :wide],
        jnp.concatenate([o_low[down:, :down], o_low[down:, down:]], 0),
        o_in,
        o_low[:down].T,
        o_small[extra],
        o_small[:extra],
    )


def shards_plain(
    hidden_states, prev_logits, lengths, w_qkv, w_out, w_in, w_down, b_in, vectors, cotangent
):
    seqs, rows, _ = hidden_states.shape
    tokens = seqs * rows
    order = jnp.arange(4, dtype=jnp.int32) ^ lax.axis_index("seq")
    half = seqs // 2
    x0 = hidden_states.reshape(tokens, D)
    x1, x2 = swap_core(hidden_states), swap_x(hidden_states)
    x_blocks = (hidden_states, x1, x2, swap_core(x2))
    table = down_table = jnp.zeros((2,), jnp.int32)
    qkv, in_pieces, down_pieces = gather_plain(w_qkv, w_out, w_in, w_down.T)
    f_qkv = qkv[0]
    f_b, f_vec = gather_small(b_in, vectors)
    f_b, f_vec = f_b.astype(F32), f_vec.astype(F32)
    made = [
        lead(
            table, order, lengths, x_blocks, (h * half,) * 4, half, h * half, qkv,
            prev_logits, f_vec,
        )
        for h in range(2)
    ]
    ctx = [m[2].reshape(-1, D) for m in made]
    out, dh1, dctx, dinner, y1, dvec, db_in, act, dbranch, dattn = middle(
        table, down_table, x0, *ctx, cotangent.reshape(tokens, D), f_vec, f_b, in_pieces, down_pieces
    )
    dctx = dctx.reshape(seqs, rows, D)
    dlogits, dq, dkv = None, [], []
    for h in range(2):
        dlogits, dq_h, dkv_h = attend_back(
            order, made[h][0], made[h][1], made[h][3], dctx, dlogits, h * half, seqs
        )
        dq.append(dq_h)
        dkv.append(dkv_h)
    got_far = [swap_core(dkv[h][3]) for h in range(2)]
    far = [grad_far(dkv[h][2], got_far[h], f_qkv) for h in range(2)]
    got_rows = [swap_x(f) for f in far]
    got_kv = [swap_core(dkv[h][1]) for h in range(2)]
    dkv0 = [dkv[h][0] for h in range(2)]
    dx = grad_own(dkv0, got_kv, dq, dh1, f_qkv)
    whole = lambda pair: jnp.concatenate(pair, 0)
    grad_hidden = low(dx + whole(got_rows).astype(F32))
    sum0 = whole([low(add(a, b)) for a, b in zip(dkv0, got_kv)])
    sum2 = whole([low(add(dkv[h][2], got_far[h])) for h in range(2)])
    dq = whole(dq)
    g_kv = mm_tn(x0, sum0) + mm_tn(x2.reshape(tokens, D), sum2)
    g_qkv = jnp.concatenate([mm_tn(x0, dq), g_kv], 1)
    dvec = dvec.at[0].add(jnp.sum(dq, 0, dtype=F32))
    dvec = dvec.at[1].add(jnp.sum(add(sum0[:, D:], sum2[:, D:]), 0))
    o_b, o_vec = reduce_small(db_in, dvec)
    shape = hidden_states.shape
    return (
        out.reshape(shape),
        grad_hidden.reshape(shape),
        dlogits,
        reduce_plain(g_qkv, "dp", "seq"),
        reduce_plain(mm_tn(whole(ctx), dattn), "dp", "seq"),
        reduce_plain(mm_tn(y1, dinner), "dp", "seq"),
        reduce_plain(mm_tn(act, dbranch), "dp", "seq"),
        o_b,
        o_vec,
    )


def shards(*args):
    return (shards_apart if by_pieces() else shards_plain)(*args)


def solution(mesh):
    return jax.shard_map(
        shards,
        mesh=mesh,
        in_specs=(
            P("dp", "seq", None),
            P("dp", None, "seq", None),
            P("dp"),
            P("dp", "seq"),
            P("dp", "seq"),
            P("dp", "seq"),
            P("dp", "seq"),
            P(("dp", "seq")),
            P("seq", "dp"),
            P("dp", "seq", None),
        ),
        out_specs=(
            P("dp", "seq", None),
            P("dp", "seq", None),
            P("dp", None, "seq", None),
            P("dp", "seq"),
            P("dp", "seq"),
            P("dp", "seq"),
            P("dp", "seq"),
            P(("dp", "seq")),
            P("seq", "dp"),
        ),
        check_vma=False,
    )
```
